128 devices in a mesh: patch: 16 (over x, y), band: 8 (over z, core).
Axes of the slice: x: 4, y: 4, z: 4, core: 2. Of those that a mesh axis runs over, the one named last changes fastest.
Arguments:
- exposure_image: bfloat16 [128, 768, 768], P(('patch', 'band')), may hold values from -6 to 6
- exposure_mask: int32 [128, 768, 768], P(('patch', 'band')), may hold values from 0 to 15
- exposure_weight: float32 [128], P(('patch', 'band')), may hold values from 0.25 to 4
- warp_anchor: int32 [128, 32, 2], P(('patch', 'band')), may hold values from 0 to 584
- warp_frac: float32 [128, 32, 2], P(('patch', 'band')), may hold values from 0 to 1
- warp_scale: float32 [128, 32, 2], P(('patch', 'band')), may hold values from -0.01 to 0.01
- psf_kernels: bfloat16 [128, 32, 41, 41], P(('patch', 'band')), may hold values from -0.15625 to 0.15625
- tile_dest: int32 [128, 32], P(('patch', 'band')), may hold values from 0 to 8, as said below
- tile_offset: int32 [128, 32], P(('patch', 'band')), may hold values from 0 to 15, as said below
Outputs:
- wavelets: float32 [4, 4096, 8192], P(None, 'band', 'patch')
- smooth: float32 [4096, 8192], P('band', 'patch')
The draws below stay inside these ranges and needn't reach their ends.
Inputs may be any that keep to these rules, and one draw needn't show every extreme that they name: `tile_dest`: every tile's block lies inside the tract. Among the 32 tiles of one exposure at most 16 share a value, and exactly 16 have the value 4 (the exposure's own block). Tiles of one exposure with the same tile_dest have different tile_offset.
All inputs are finite; a program needn't handle non-finite values.
Results may differ from the reference program's by a relative error of at most 0.0068.
Values may be sent and summed in bfloat16 or wider, within the bound.
A program may use at most 192 MiB of HBM per device.

```python
import math
import jax
import jax.numpy as jnp
from jax import lax

TILE = 128
KS = 41
SCALES = 4
TR = 4
TC = 4
EXP_PIX = 768
TILES_EXP = 32
MARGIN = 20
WARP_N = 168
SRC_N = 184
EXPOSURES = 128
NY = 4096
NX = 8192
N_PATCH = 16
N_BAND = 8


def neighbour_plan(key):
    cells = TR * TC
    slots = 9 * cells
    owner = jnp.arange(EXPOSURES)
    band_home = owner % N_BAND
    patch_home = owner // N_BAND
    codes = jnp.arange(9)
    band_to = band_home[:, None] + codes[None, :] // 3 - 1
    patch_to = patch_home[:, None] + codes[None, :] % 3 - 1
    valid = (band_to >= 0) & (band_to < N_BAND) & (patch_to >= 0) & (patch_to < N_PATCH)
    bias_offset = jax.random.randint(jax.random.fold_in(key, 11), (EXPOSURES, 9), 0, 8)
    random_perturbation = jax.random.randint(jax.random.fold_in(key, 12), (EXPOSURES, slots), 0, 64)
    position_label = jnp.arange(slots) // cells
    extra_reward = jnp.where(position_label == 4, 4096, jnp.where(position_label == 8, 2048, jnp.where(position_label == 0, 1024, 0)))
    ranking_preference = bias_offset[:, position_label] * 64 + random_perturbation + extra_reward[None, :]
    score = jnp.where(valid[:, position_label], ranking_preference * slots + jnp.arange(slots)[None, :], -1 - jnp.arange(slots)[None, :])
    chosen = lax.top_k(score, TILES_EXP)[1]
    shuffle_keys = jax.random.randint(jax.random.fold_in(key, 13), (EXPOSURES, TILES_EXP), 0, 1024) * TILES_EXP + jnp.arange(TILES_EXP)[None, :]
    order = jnp.argsort(shuffle_keys, axis=1)
    chosen = jnp.take_along_axis(chosen, order, axis=1)
    cell_key_values = jax.random.randint(jax.random.fold_in(key, 14), (EXPOSURES, 9, cells), 0, 1024) * cells + jnp.arange(cells)[None, None, :]
    cell_perm = jnp.argsort(cell_key_values, axis=2).reshape(EXPOSURES, slots)
    places = jnp.take_along_axis(cell_perm, chosen, axis=1)
    return ((chosen // cells).astype(jnp.int32), places.astype(jnp.int32))


def draw_tile_dest(key, part):
    return neighbour_plan(key)[0]


def draw_tile_offset(key, part):
    return neighbour_plan(key)[1]


def plant(entries, rng, smallest, top_value):
    longest = entries.shape.index(max(entries.shape))
    spots = []
    for shift in (0, 1):
        where = [jax.random.randint(jax.random.fold_in(rng, axis), (), 0, length) for axis, length in enumerate(entries.shape)]
        where[longest] = (where[longest] + shift) % entries.shape[longest]
        spots.append(tuple(where))
    return entries.at[spots[0]].set(smallest).at[spots[1]].set(top_value)


def block_scale(own_key, extent, shards, smallest, high):
    def one(dim, blocks):
        draws = jax.random.uniform(jax.random.fold_in(jax.random.fold_in(own_key, 6), dim), (blocks,), jnp.float32, smallest / len(shards), high / len(shards))
        return jnp.repeat(jnp.exp(draws), extent[dim] // blocks).reshape((-1,) + (1,) * (len(extent) - dim - 1))

    gain = one(*shards[0])
    for cut in shards[1:]:
        gain = gain * one(*cut)
    return gain


def noise(key, dims, scale, reach, split=(), kind=jnp.bfloat16):
    result = jax.random.normal(key, dims, jnp.float32) * scale
    if len(split) > 0:
        result = block_scale(key, dims, split, -0.22, 0.18) * result
    return jnp.clip(result, min=-reach, max=reach).astype(kind)


def setup_inputs(seed: int = 0) -> dict:
    arg_keys = jax.random.split(jax.random.key(seed), 10)
    exposure_image = noise(arg_keys[0], (EXPOSURES, EXP_PIX, EXP_PIX), 1.0, 6.0, ((0, 128),))
    exposure_mask = plant(jax.random.randint(arg_keys[1], (EXPOSURES, EXP_PIX, EXP_PIX), 0, 16), jax.random.fold_in(arg_keys[1], 1), 0, 15).astype(jnp.int32)
    exposure_weight = jnp.clip(jnp.exp(math.log(4.0) - 2.7725887 * jax.random.uniform(arg_keys[2], (EXPOSURES,), jnp.float32) ** block_scale(arg_keys[2], (EXPOSURES,), ((0, 128),), -0.2, 0.2)), 0.25, 4.0)
    warp_anchor = plant(jax.random.randint(arg_keys[3], (EXPOSURES, TILES_EXP, 2), 0, EXP_PIX - SRC_N + 1), jax.random.fold_in(arg_keys[3], 1), 0, EXP_PIX - SRC_N).astype(jnp.int32)
    warp_frac = jnp.clip(1.0 * jax.random.uniform(arg_keys[4], (EXPOSURES, TILES_EXP, 2), jnp.float32) ** block_scale(arg_keys[4], (EXPOSURES, TILES_EXP, 2), ((0, 128),), -0.2, 0.2), 0.0, 1.0)
    warp_scale = jnp.clip(jax.random.uniform(arg_keys[5], (EXPOSURES, TILES_EXP, 2), jnp.float32, -0.01, 0.01) * block_scale(arg_keys[5], (EXPOSURES, TILES_EXP, 2), ((0, 128),), -0.4, 0.0), -0.01, 0.01)
    psf_kernels = noise(arg_keys[6], (EXPOSURES, TILES_EXP, KS, KS), (KS * KS) ** -0.5, 0.15625, ((0, 128),))
    tile_dest = draw_tile_dest(jax.random.fold_in(arg_keys[9], 71), 0)
    tile_offset = draw_tile_offset(jax.random.fold_in(arg_keys[9], 71), 0)
    return dict(exposure_image=exposure_image, exposure_mask=exposure_mask, exposure_weight=exposure_weight, warp_anchor=warp_anchor, warp_frac=warp_frac, warp_scale=warp_scale, psf_kernels=psf_kernels, tile_dest=tile_dest, tile_offset=tile_offset)


def lanczos_rows(fraction, stretch, length, width):
    position = 5.0 + fraction + jnp.arange(length, dtype=jnp.float32) * (1.0 + stretch)
    distance = jnp.arange(width, dtype=jnp.float32)[None, :] - position[:, None]
    kernel = jnp.where(jnp.abs(distance) < 5.0, jnp.sinc(distance) * jnp.sinc(distance / 5.0), 0.0)
    return kernel.astype(jnp.bfloat16)


def b3_axis(padded, spacing, direction, length):
    terms = [lax.slice_in_dim(padded, spacing * factor, spacing * factor + length, axis=direction) for factor in range(5)]
    return (terms[0] + 4.0 * terms[1] + 6.0 * terms[2] + 4.0 * terms[3] + terms[4]) / 16.0


def exposure_tiles(picture, bitmask, weight, corners, fraction, stretch, kernels):
    usable = (jnp.bitwise_and(bitmask, 7) != 7).astype(jnp.bfloat16)
    masked = picture * usable

    def window(corner):
        first = lax.dynamic_slice(masked, (corner[0], corner[1]), (SRC_N, SRC_N))
        second = lax.dynamic_slice(usable, (corner[0], corner[1]), (SRC_N, SRC_N))
        return jnp.stack([first, second])

    windows = jax.vmap(window)(corners)
    row_kernels = jax.vmap(lambda offset_value, stretch_value: lanczos_rows(offset_value, stretch_value, WARP_N, SRC_N))(fraction[:, 0], stretch[:, 0])
    col_kernels = jax.vmap(lambda offset_value, stretch_value: lanczos_rows(offset_value, stretch_value, WARP_N, SRC_N))(fraction[:, 1], stretch[:, 1])
    half_warp = jnp.einsum("tij,tcjk->tcik", row_kernels.astype(jnp.float32), windows.astype(jnp.float32), precision=lax.Precision.HIGHEST).astype(jnp.bfloat16)
    warped = jnp.einsum("tcik,tlk->tcil", half_warp.astype(jnp.float32), col_kernels.astype(jnp.float32), precision=lax.Precision.HIGHEST)
    resampled = warped[:, 0].astype(jnp.bfloat16)
    coverage = warped[:, 1]
    matched = lax.conv_general_dilated(resampled.astype(jnp.float32)[None], kernels.astype(jnp.float32)[:, None], (1, 1), "VALID", dimension_numbers=("NCHW", "OIHW", "NCHW"), feature_group_count=kernels.shape[0], precision=lax.Precision.HIGHEST)[0]
    numerator = (weight * matched).astype(jnp.bfloat16)
    inner = coverage[:, MARGIN:MARGIN + TILE, MARGIN:MARGIN + TILE]
    denominator = (weight * inner).astype(jnp.bfloat16)
    return numerator, denominator


def reference(exposure_image, exposure_mask, exposure_weight, warp_anchor, warp_frac, warp_scale, psf_kernels, tile_dest, tile_offset):
    block_rows = TR * TILE
    block_cols = TC * TILE

    def absorb(carry, item):
        owner, picture, bitmask, weight, corners, fraction, stretch, kernels, targets, places = item
        numerator, denominator = exposure_tiles(picture, bitmask, weight, corners, fraction, stretch, kernels)
        band_home = owner % N_BAND
        patch_home = owner // N_BAND

        def place(position, images):
            sum_image, weight_image = images
            code = targets[position]
            cell_index = places[position]
            row_start = ((band_home + code // 3 - 1) * block_rows + (cell_index // TC) * TILE).astype(jnp.int32)
            col_start = ((patch_home + code % 3 - 1) * block_cols + (cell_index % TC) * TILE).astype(jnp.int32)
            old_sum = lax.dynamic_slice(sum_image, (row_start, col_start), (TILE, TILE))
            sum_image = lax.dynamic_update_slice(sum_image, old_sum + numerator[position].astype(jnp.float32), (row_start, col_start))
            previous_weight = lax.dynamic_slice(weight_image, (row_start, col_start), (TILE, TILE))
            weight_image = lax.dynamic_update_slice(weight_image, previous_weight + denominator[position].astype(jnp.float32), (row_start, col_start))
            return sum_image, weight_image

        return lax.fori_loop(0, TILES_EXP, place, carry), None

    empty = jnp.zeros((NY, NX), jnp.float32)
    owners = jnp.arange(EXPOSURES, dtype=jnp.int32)
    (sum_image, weight_image), unused = lax.scan(absorb, (empty, empty), (owners, exposure_image, exposure_mask, exposure_weight, warp_anchor, warp_frac, warp_scale, psf_kernels, tile_dest, tile_offset))
    level = sum_image / (jnp.maximum(weight_image, 0.0) + 1.0)
    details = []
    for scale_index in range(SCALES):
        spacing = 2 ** scale_index
        extended = jnp.pad(level, 2 * spacing)
        smoother = b3_axis(b3_axis(extended, spacing, 0, NY), spacing, 1, NX)
        details.append(level - smoother)
        level = smoother
    return jnp.stack(details), level
```

```python
import functools
import math

import numpy as np
import ml_dtypes
import jax
import jax.numpy as jnp
from jax import lax
from jax.experimental import pallas as pl
from jax.experimental.pallas import tpu as pltpu
from jax.sharding import PartitionSpec as P

TILE, KS, SCALES, TR, TC, MARGIN, WARP_N, SRC_N = 128, 41, 4, 4, 4, 20, 168, 184
ROWS = 176
HALF = 88
WIN = 256
F32, BF16 = jnp.float32, jnp.bfloat16


def split_bf16(values):
    high = values.astype(ml_dtypes.bfloat16)
    low = (values - high.astype(np.float64)).astype(ml_dtypes.bfloat16)
    return high, low


def spectra():
    bins = np.arange(WARP_N // 2 + 1)

    def forward(points, sign):
        angle = 2.0 * np.pi / WARP_N * np.outer(bins, points)
        return np.cos(angle), sign * np.sin(angle)

    order = (np.arange(WARP_N) + MARGIN) % WARP_N
    real, imag = forward(order, -1.0)
    rows = np.zeros((ROWS, WIN))
    rows[: len(bins), :WARP_N] = real
    rows[HALF : HALF + len(bins), :WARP_N] = imag
    cols = np.zeros((WIN, WIN))
    cols[:WARP_N, : len(bins)] = real.T
    cols[:WARP_N, 128 : 128 + len(bins)] = imag.T
    real, imag = forward(np.arange(KS), 1.0)
    kcols = np.zeros((64, WIN))
    kcols[:KS, : len(bins)] = real.T
    kcols[:KS, 128 : 128 + len(bins)] = imag.T
    krows = np.zeros((ROWS, 48))
    krows[: len(bins), :KS] = real
    krows[HALF : HALF + len(bins), :KS] = imag
    count = np.full(len(bins), 2.0)
    count[0] = count[-1] = 1.0
    angle = 2.0 * np.pi / WARP_N * np.outer(np.arange(TILE), bins)
    back_real = np.cos(angle) * count / WARP_N
    back_imag = -np.sin(angle) * count / WARP_N
    icols = np.zeros((WIN, TILE))
    icols[: len(bins)] = back_real.T
    icols[128 : 128 + len(bins)] = back_imag.T
    irows = np.zeros((TILE, ROWS))
    irows[:, : len(bins)] = 0.5 * back_real
    irows[:, HALF : HALF + len(bins)] = 0.5 * back_imag
    kcols_high, kcols_low = split_bf16(kcols)
    krows_high, krows_low = split_bf16(krows)
    icols_high, icols_low = split_bf16(icols)
    irows_high, irows_low = split_bf16(irows)
    rows_pad = rows[:, :ROWS]
    return (
        cols.astype(ml_dtypes.bfloat16),
        rows_pad.astype(ml_dtypes.bfloat16),
        np.concatenate([kcols_high, kcols_low]),
        np.concatenate([krows_high, krows_high, krows_low], axis=1),
        np.concatenate([icols_high, icols_low], axis=1),
        np.concatenate([irows_high, irows_low]),
    )


def phase_constants():
    j = np.arange(WIN)
    sign = 1.0 - 2.0 * (j % 2)
    cosine = (sign * np.cos(np.pi * j / 5.0)).astype(np.float32)
    sine = (sign * np.sin(np.pi * j / 5.0)).astype(np.float32)
    along = np.zeros((8, WIN), np.float32)
    along[0], along[1] = cosine, sine
    down = np.stack([np.repeat(cosine[:, None], 128, 1), np.repeat(sine[:, None], 128, 1)])
    return along, down


def poly(coefficients, x):
    total = jnp.full_like(x, coefficients[-1])
    for value in coefficients[-2::-1]:
        total = total * x + value
    return total


SIN_PI = (3.14159265, -5.16771276, 2.55016332, -0.5992522, 0.0820504, -0.00702839)
SIN_TURN = (6.28318531, -41.34170222, 81.60524742, -76.70580022, 42.05775402, -15.08656526, 3.78131888, -0.62077872)
COS_TURN = (1.0, -19.73920874, 64.93938908, -85.45665831, 60.24213134, -26.40466819, 7.80013144, -1.45311232)


def warp_quantities(fraction, stretch, offset):
    lanes = np.arange(WIN)
    index = jnp.asarray((lanes + MARGIN) % WARP_N, F32)
    position = 5.0 + fraction[:, None] + index * (1.0 + stretch[:, None])
    nearest = jnp.floor(position + 0.5)
    odd = nearest - 2.0 * jnp.floor(nearest * 0.5)
    part = position - nearest
    sine = (1.0 - 2.0 * odd) * part * poly(SIN_PI, part * part)
    odd_offset = (offset % 2).astype(F32)[:, None]
    amplitude = (-5.0 / math.pi**2) * (1.0 - 2.0 * odd_offset) * sine
    turn = position - 10.0 * jnp.floor(position * 0.1) + (offset % 10).astype(F32)[:, None]
    turn = turn * 0.1
    turn = turn - jnp.floor(turn + 0.5)
    square = turn * turn
    cosine, sine = poly(COS_TURN, square), turn * poly(SIN_TURN, square)
    position = jnp.where(jnp.asarray(lanes < WARP_N), position, 1e4)
    return jnp.stack([position, amplitude * cosine, amplitude * sine] + [position] * 5, axis=1)


def lanczos(d, cos_row, sin_row, cos_col, sin_col):
    d2 = d * d
    u = cos_row * sin_col - sin_row * cos_col
    g = u / d2
    g = jnp.where(d2 < 1e-5, 1.0, g)
    return jnp.where(d2 < 25.0, g, 0.0).astype(BF16)


def dot(a, b):
    return lax.dot_general(a, b, (((1,), (0,)), ((), ())), preferred_element_type=F32)


def tile_kernel(group, order_ref, place_ref, weight_ref, planes_ref, q0_ref, q1_ref, kern_ref,
                along_ref, down_ref, cols_ref, rows_ref, kcols_ref, krows_ref, icols_ref, irows_ref, out_ref):
    step = pl.program_id(0)
    weight = weight_ref[0]
    lane = lax.broadcasted_iota(jnp.int32, (ROWS, WIN), 1)
    sub = lax.broadcasted_iota(jnp.int32, (WIN, WIN), 0)
    tiles = [order_ref[step * group + g] for g in range(group)]
    each = range(group)
    half_img, half_cov, lt = [], [], []
    for g in each:
        t = tiles[g]
        row = pl.multiple_of(place_ref[0, t] * 16, 16)
        par = place_ref[1, t]
        col = pl.multiple_of(place_ref[2, t] * 128, 128)
        off_r = place_ref[3, t]
        off_c = place_ref[4, t]
        s_img = planes_ref[par, 0, pl.ds(row, WIN), pl.ds(col, WIN)]
        s_cov = planes_ref[par, 1, pl.ds(row, WIN), pl.ds(col, WIN)]
        q0 = jnp.transpose(q0_ref[t])[:ROWS]
        d0 = (lane - off_r).astype(F32) - q0[:, 0:1]
        l0 = lanczos(d0, q0[:, 1:2], q0[:, 2:3], along_ref[0:1, :], along_ref[1:2, :])
        q1 = q1_ref[t]
        d1 = (sub - off_c).astype(F32) - q1[0:1, :]
        cosd = down_ref[0]
        sind = down_ref[1]
        cosd = jnp.concatenate([cosd, cosd], axis=1)
        sind = jnp.concatenate([sind, sind], axis=1)
        l1t = lanczos(d1, q1[1:2, :], q1[2:3, :], cosd, sind)
        lt.append(l1t)
        half_img.append(dot(l0, s_img).astype(BF16))
        half_cov.append(dot(l0[:TILE], s_cov).astype(BF16))
    warped = [dot(half_img[g], lt[g]).astype(BF16) for g in each]
    for g in each:
        coverage = dot(half_cov[g], lt[g][:, :TILE])
        out_ref[g, 1] = (weight * coverage).astype(BF16)
    x1 = dot(jnp.concatenate(warped, axis=0), cols_ref[...]).astype(BF16)
    x2 = [dot(rows_ref[...], x1[g * ROWS : (g + 1) * ROWS]) for g in each]
    k1 = dot(jnp.concatenate([kern_ref[tiles[g]] for g in each], axis=0), kcols_ref[...])
    k1h = k1.astype(BF16)
    k1l = (k1 - k1h.astype(F32)).astype(BF16)
    z = []
    for g in each:
        h, l = k1h[g * 48 : g * 48 + 48], k1l[g * 48 : g * 48 + 48]
        k2 = dot(krows_ref[...], jnp.concatenate([h, l, h], axis=0))
        x = x2[g]
        xrr, xri, xir, xii = x[:HALF, :128], x[:HALF, 128:], x[HALF:, :128], x[HALF:, 128:]
        krr, kri, kir, kii = k2[:HALF, :128], k2[:HALF, 128:], k2[HALF:, :128], k2[HALF:, 128:]
        xpr, xpi, xmr, xmi = xrr - xii, xir + xri, xrr + xii, xir - xri
        kpr, kpi, kmr, kmi = krr - kii, kir + kri, krr + kii, kir - kri
        ppr, ppi = xpr * kpr - xpi * kpi, xpr * kpi + xpi * kpr
        pmr, pmi = xmr * kmr - xmi * kmi, xmr * kmi + xmi * kmr
        top = jnp.concatenate([ppr + pmr, ppi - pmi], axis=1)
        bottom = jnp.concatenate([ppi + pmi, pmr - ppr], axis=1)
        z.append(jnp.concatenate([top, bottom], axis=0).astype(BF16))
    y = dot(jnp.concatenate(z, axis=0), icols_ref[...])
    y = y[:, :TILE] + y[:, TILE:]
    yh = y.astype(BF16)
    yl = (y - yh.astype(F32)).astype(BF16)
    ycat = jnp.concatenate([yh, yl], axis=1)
    for g in each:
        o = dot(irows_ref[...], ycat[g * ROWS : (g + 1) * ROWS])
        matched = o[:TILE, :TILE] + (o[:TILE, TILE:] + o[TILE:, :TILE])
        out_ref[g, 0] = (weight * matched).astype(BF16)


def tile_call(order, places, weight, planes, q0, q1, kern, consts, group):
    count = order.shape[0]
    whole = lambda a: pl.BlockSpec(a.shape, lambda i, *_: (0,) * a.ndim, pipeline_mode=pl.Buffered(1))
    vm = [planes, q0, q1, kern] + list(consts)
    return pl.pallas_call(
        functools.partial(tile_kernel, group),
        grid_spec=pltpu.PrefetchScalarGridSpec(
            num_scalar_prefetch=3,
            grid=(count // group,),
            in_specs=[whole(a) for a in vm],
            out_specs=pl.BlockSpec((group, 2, TILE, TILE), lambda i, *_: (i, 0, 0, 0)),
        ),
        out_shape=jax.ShapeDtypeStruct((count, 2, TILE, TILE), BF16),
        compiler_params=pltpu.CompilerParams(vmem_limit_bytes=56 * 2**20),
    )(order, places, weight, *vm)


def constants():
    along, down = phase_constants()
    return [jnp.asarray(a) for a in (along, down) + spectra()]


def prepare(image, mask, anchor, frac, scale, kernels):
    usable = (jnp.bitwise_and(mask, 7) != 7).astype(BF16)
    masked = image * usable
    base = jnp.stack([masked, usable])
    moved = jnp.pad(base[:, :, 64:], ((0, 0), (0, 0), (0, 64)))
    planes = jnp.stack([base, moved])
    r16 = jnp.minimum(anchor[:, 0] // 16, 32)
    c64 = jnp.minimum(anchor[:, 1] // 64, 8)
    off_r = anchor[:, 0] - 16 * r16
    off_c = anchor[:, 1] - 64 * c64
    places = jnp.stack([r16, c64 % 2, c64 // 2, off_r, off_c])
    q = warp_quantities(frac.T.reshape(-1), scale.T.reshape(-1), jnp.concatenate([off_r, off_c]))
    q0, q1 = q[:32], q[32:]
    kp = jnp.pad(kernels, ((0, 0), (0, 7), (0, 23)))
    kern = jnp.concatenate([kp, kp], axis=-1)
    return places, planes, q0, q1, kern


CELLS = TR * TC
SPAN = TR * TILE
PAD = 32
WIDE = SPAN + 128
TOP = 8 + PAD
TALL = SPAN + 2 * TOP


def whole(a):
    return pl.BlockSpec(a.shape, lambda *_: (0,) * a.ndim)


def combine_kernel(table_ref, own_ref, left_ref, right_ref, out_ref):
    sources = (own_ref, left_ref, right_ref)

    def place(position, carry):
        total = None
        for s in range(3):
            slot = table_ref[s, position]
            present = jnp.where(slot >= 0, 1.0, 0.0)
            term = sources[s][jnp.maximum(slot, 0)].astype(F32) * present
            total = term if total is None else total + term
        out_ref[position] = total.astype(out_ref.dtype)
        return carry

    lax.fori_loop(0, out_ref.shape[0], place, 0)


def combine_call(table, own, left, right, dtype):
    vm = (own, left, right)
    return pl.pallas_call(
        combine_kernel,
        in_specs=[pl.BlockSpec(memory_space=pltpu.SMEM)] + [whole(a) for a in vm],
        out_specs=pl.BlockSpec((table.shape[1], 2, TILE, TILE), lambda: (0, 0, 0, 0)),
        out_shape=jax.ShapeDtypeStruct((table.shape[1], 2, TILE, TILE), dtype),
        compiler_params=pltpu.CompilerParams(vmem_limit_bytes=48 * 2**20),
    )(table, *vm)


def finish_kernel(home_ref, side_ref, above_ref, below_ref, out_ref):
    for cell in range(CELLS):
        total = home_ref[cell].astype(F32) + side_ref[cell]
        total = total + (above_ref[cell].astype(F32) + below_ref[cell].astype(F32))
        row, col = cell // TC * TILE, cell % TC * TILE
        out_ref[row : row + TILE, col : col + TILE] = total[0] / (jnp.maximum(total[1], 0.0) + 1.0)


def finish_call(home, side, above, below):
    vm = (home, side, above, below)
    return pl.pallas_call(
        finish_kernel,
        in_specs=[whole(a) for a in vm],
        out_specs=pl.BlockSpec((SPAN, SPAN), lambda: (0, 0)),
        out_shape=jax.ShapeDtypeStruct((SPAN, SPAN), F32),
        compiler_params=pltpu.CompilerParams(vmem_limit_bytes=48 * 2**20),
    )(*vm)


LEVEL_ROWS = ((8, 584), (16, 576), (24, 568), (40, 552))
BLOCK = 8


def starlet_kernel(edge_ref, first_ref, details_ref, smooth_ref, ping, pong):
    top, bottom, left, right = (edge_ref[i] for i in range(4))
    lane = lax.broadcasted_iota(jnp.int32, (BLOCK, 128), 1)
    side_mask = jnp.where(lane < 64, right, left)
    zero = jnp.zeros((8, WIDE), F32)
    for ref in (ping, pong):
        ref[0:8, :] = zero
        ref[TALL - 8 : TALL, :] = zero
    source = first_ref
    for k in range(SCALES):
        s = 2**k
        target = (ping, pong)[k % 2]
        begin, end = LEVEL_ROWS[k]

        def one(block, carry, source=source, target=target, s=s, k=k, begin=begin):
            row = pl.multiple_of(begin + block * BLOCK, 8)

            def shifted_rows(by):
                if by % 8 == 0:
                    return source[pl.ds(pl.multiple_of(row + by, 8), BLOCK), :]
                base = pl.multiple_of(row - 8, 8)
                return source[pl.ds(base, BLOCK + 16), :][8 + by : 8 + by + BLOCK]

            center = shifted_rows(0)
            rows = (shifted_rows(-2 * s) + shifted_rows(2 * s)) + 4.0 * (shifted_rows(-s) + shifted_rows(s)) + 6.0 * center
            rows = rows * (1.0 / 16.0)
            outer = pltpu.roll(rows, 2 * s, 1) + pltpu.roll(rows, WIDE - 2 * s, 1)
            inner = pltpu.roll(rows, s, 1) + pltpu.roll(rows, WIDE - s, 1)
            smoother = (outer + 4.0 * inner + 6.0 * rows) * (1.0 / 16.0)
            outside = jnp.where(row < TOP, top, jnp.where(row >= TOP + SPAN, bottom, 1.0))
            if k < SCALES - 1:
                target[pl.ds(row, BLOCK), :SPAN] = smoother[:, :SPAN] * outside
                target[pl.ds(row, BLOCK), SPAN:] = smoother[:, SPAN:] * (side_mask * outside)

            @pl.when((row >= TOP) & (row < TOP + SPAN))
            def _():
                here = pl.multiple_of(row - TOP, 8)
                details_ref[k, pl.ds(here, BLOCK), :] = center[:, :SPAN] - smoother[:, :SPAN]
                if k == SCALES - 1:
                    smooth_ref[pl.ds(here, BLOCK), :] = smoother[:, :SPAN]

            return carry

        lax.fori_loop(0, (end - begin) // BLOCK, one, 0)
        source = target


def starlet_call(edges, first):
    return pl.pallas_call(
        starlet_kernel,
        in_specs=[pl.BlockSpec(memory_space=pltpu.SMEM), whole(first)],
        out_specs=[
            pl.BlockSpec((SCALES, SPAN, SPAN), lambda: (0, 0, 0)),
            pl.BlockSpec((SPAN, SPAN), lambda: (0, 0)),
        ],
        out_shape=[
            jax.ShapeDtypeStruct((SCALES, SPAN, SPAN), F32),
            jax.ShapeDtypeStruct((SPAN, SPAN), F32),
        ],
        scratch_shapes=[pltpu.VMEM((TALL, WIDE), F32)] * 2,
        compiler_params=pltpu.CompilerParams(vmem_limit_bytes=48 * 2**20),
    )(edges, first)


def shift(value, axis, by):
    count = lax.axis_size(axis)
    return lax.ppermute(value, axis, [(i, i + by) for i in range(count) if 0 <= i + by < count])


def shards(image, mask, weight, anchor, frac, scale, kernels, dest, offset):
    dest, offset = dest[0], offset[0]
    away = dest != 4
    tile = jnp.arange(32, dtype=jnp.int32)
    rank = jnp.sum((away[None, :] & (tile[None, :] < tile[:, None])).astype(jnp.int32), axis=1)
    slots = jnp.arange(CELLS, dtype=jnp.int32)
    pick = (away[None, :] & (rank[None, :] == slots[:, None])).astype(jnp.int32)
    order_away = jnp.sum(pick * tile[None, :], axis=1)
    label = jnp.sum(pick * (dest * CELLS + offset + 1)[None, :], axis=1)
    pick_home = (~away[None, :] & (offset[None, :] == slots[:, None])).astype(jnp.int32)
    order_home = jnp.sum(pick_home * tile[None, :], axis=1)
    label_left = shift(label, "patch", 1)
    label_right = shift(label, "patch", -1)

    places, planes, q0, q1, kern = prepare(image[0], mask[0], anchor[0], frac[0], scale[0], kernels[0])
    consts = constants()
    tiles = functools.partial(
        tile_call, places=places, weight=weight, planes=planes, q0=q0, q1=q1, kern=kern, consts=consts, group=4
    )
    own = tiles(order_away)
    left = shift(own, "patch", 1)
    right = shift(own, "patch", -1)
    home = tiles(order_home)

    positions = jnp.arange(3 * CELLS, dtype=jnp.int32)
    labels = jnp.stack([label, label_left, label_right])
    columns = jnp.asarray([1, 2, 0], jnp.int32)
    wanted = (3 * (positions // CELLS)[None, :] + columns[:, None]) * CELLS + (positions % CELLS)[None, :] + 1
    found = labels[:, None, :] == wanted[:, :, None]
    table = jnp.sum(jnp.where(found, slots[None, None, :] + 1, 0), axis=2) - 1
    moving = combine_call(
        jnp.concatenate([table[:, :CELLS], table[:, 2 * CELLS :]], axis=1), own, left, right, BF16
    )
    above = shift(moving[CELLS:], "band", 1)
    below = shift(moving[:CELLS], "band", -1)
    side = combine_call(table[:, CELLS : 2 * CELLS], own, left, right, F32)
    first = finish_call(home, side, above, below)

    from_left = shift(first[:, SPAN - PAD :], "patch", 1)
    from_right = shift(first[:, :PAD], "patch", -1)
    gap = jnp.zeros((SPAN, 128 - 2 * PAD), F32)
    first = jnp.concatenate([first, from_right, gap, from_left], axis=1)
    from_above = shift(first[SPAN - PAD :], "band", 1)
    from_below = shift(first[:PAD], "band", -1)
    rim = jnp.zeros((8, WIDE), F32)
    first = jnp.concatenate([rim, from_above, first, from_below, rim], axis=0)
    band, patch = lax.axis_index("band"), lax.axis_index("patch")
    edges = jnp.stack(
        [band > 0, band < lax.axis_size("band") - 1, patch > 0, patch < lax.axis_size("patch") - 1]
    ).astype(F32)
    return tuple(starlet_call(edges, first))


def solution(mesh):
    owner = ("patch", "band")
    in_specs = (
        P(owner, None, None),
        P(owner, None, None),
        P(owner),
        P(owner, None, None),
        P(owner, None, None),
        P(owner, None, None),
        P(owner, None, None, None),
        P(owner, None),
        P(owner, None),
    )
    out_specs = (P(None, "band", "patch"), P("band", "patch"))
    return jax.shard_map(shards, mesh=mesh, in_specs=in_specs, out_specs=out_specs, check_vma=False)
```

```python
import math
import numpy as np
import ml_dtypes
import jax
import jax.numpy as jnp
from jax import lax
from jax.experimental import pallas as pl
from jax.experimental.pallas import tpu as pltpu
from jax.sharding import PartitionSpec as P

TILE, KS, SCALES, TR, TC, MARGIN, WARP_N, SRC_N = 128, 41, 4, 4, 4, 20, 168, 184
ROWS = 176
HALF = 88
WIN = 256
F32, BF16 = jnp.float32, jnp.bfloat16


def split_bf16(values):
    high = values.astype(ml_dtypes.bfloat16)
    low = (values - high.astype(np.float64)).astype(ml_dtypes.bfloat16)
    return high, low


def spectra():
    bins = np.arange(WARP_N // 2 + 1)

    def forward(points, sign):
        angle = 2.0 * np.pi / WARP_N * np.outer(bins, points)
        return np.cos(angle), sign * np.sin(angle)

    order = (np.arange(WARP_N) + MARGIN) % WARP_N
    real, imag = forward(order, -1.0)
    rows = np.zeros((ROWS, WIN))
    rows[: len(bins), :WARP_N] = real
    rows[HALF : HALF + len(bins), :WARP_N] = imag
    cols = np.zeros((WIN, WIN))
    cols[:WARP_N, : len(bins)] = real.T
    cols[:WARP_N, 128 : 128 + len(bins)] = imag.T
    real, imag = forward(np.arange(KS), 1.0)
    kcols = np.zeros((64, WIN))
    kcols[:KS, : len(bins)] = real.T
    kcols[:KS, 128 : 128 + len(bins)] = imag.T
    krows = np.zeros((ROWS, 48))
    krows[: len(bins), :KS] = real
    krows[HALF : HALF + len(bins), :KS] = imag
    count = np.full(len(bins), 2.0)
    count[0] = count[-1] = 1.0
    angle = 2.0 * np.pi / WARP_N * np.outer(np.arange(TILE), bins)
    back_real = np.cos(angle) * count / WARP_N
    back_imag = -np.sin(angle) * count / WARP_N
    icols = np.zeros((WIN, TILE))
    icols[: len(bins)] = back_real.T
    icols[128 : 128 + len(bins)] = back_imag.T
    irows = np.zeros((TILE, ROWS))
    irows[:, : len(bins)] = 0.5 * back_real
    irows[:, HALF : HALF + len(bins)] = 0.5 * back_imag
    kcols_high, kcols_low = split_bf16(kcols)
    krows_high, krows_low = split_bf16(krows)
    icols_high, icols_low = split_bf16(icols)
    irows_high, irows_low = split_bf16(irows)
    rows_pad = rows[:, :ROWS]
    return (
        cols.astype(ml_dtypes.bfloat16),
        rows_pad.astype(ml_dtypes.bfloat16),
        np.concatenate([kcols_high, kcols_low]),
        np.concatenate([krows_high, krows_high, krows_low], axis=1),
        np.concatenate([icols_high, icols_low], axis=1),
        np.concatenate([irows_high, irows_low]),
    )


def phase_constants():
    j = np.arange(WIN)
    sign = 1.0 - 2.0 * (j % 2)
    cosine = (sign * np.cos(np.pi * j / 5.0)).astype(np.float32)
    sine = (sign * np.sin(np.pi * j / 5.0)).astype(np.float32)
    along = np.zeros((8, WIN), np.float32)
    along[0], along[1] = cosine, sine
    down = np.stack([np.repeat(cosine[:, None], 128, 1), np.repeat(sine[:, None], 128, 1)])
    return along, down


def poly(coefficients, x):
    total = jnp.full_like(x, coefficients[-1])
    for value in coefficients[-2::-1]:
        total = total * x + value
    return total


SIN_PI = (3.14159265, -5.16771276, 2.55016332, -0.5992522, 0.0820504, -0.00702839)
SIN_TURN = (6.28318531, -41.34170222, 81.60524742, -76.70580022, 42.05775402, -15.08656526, 3.78131888, -0.62077872)
COS_TURN = (1.0, -19.73920874, 64.93938908, -85.45665831, 60.24213134, -26.40466819, 7.80013144, -1.45311232)


def lanczos(d, cos_row, sin_row, cos_col, sin_col):
    d2 = d * d
    u = cos_row * sin_col - sin_row * cos_col
    g = u / d2
    g = jnp.where(d2 < 1e-5, 1.0, g)
    return jnp.where(d2 < 25.0, g, 0.0).astype(BF16)


def dot(a, b):
    return lax.dot_general(a, b, (((1,), (0,)), ((), ())), preferred_element_type=F32)


def constants():
    along, down = phase_constants()
    return [jnp.asarray(a) for a in (along, down) + spectra()]


CELLS = TR * TC
GROUP = 4
SPAN = TR * TILE
PAD = 32
WIDE = SPAN + 128
TOP = 8 + PAD
TALL = SPAN + 2 * TOP
MESH = pl.DeviceIdType.MESH


def within(value, top):
    return jnp.minimum(jnp.maximum(value, 0), top)


def whole(a):
    return pl.BlockSpec(a.shape, lambda *_: (0,) * a.ndim)


def order_kernel(dest_ref, offset_ref, order_ref, label_ref):
    filled = jnp.int32(0)
    for i in range(2 * CELLS):
        code, cell = dest_ref[0, i], offset_ref[0, i]
        away = code != 4
        slot = jnp.where(away, filled, CELLS + cell)
        order_ref[slot] = jnp.int32(i)
        label_ref[pl.ds(slot, 1), :] = jnp.full((1, 128), code * CELLS + cell + 1, jnp.int32)
        filled = filled + away.astype(jnp.int32)


def order_call(dest, offset):
    smem = pl.BlockSpec(memory_space=pltpu.SMEM)
    return pl.pallas_call(
        order_kernel,
        in_specs=[smem, smem],
        out_specs=[smem, pl.BlockSpec((2 * CELLS + 8, 128), lambda: (0, 0))],
        out_shape=[
            jax.ShapeDtypeStruct((2 * CELLS,), jnp.int32),
            jax.ShapeDtypeStruct((2 * CELLS + 8, 128), jnp.int32),
        ],
    )(dest, offset)


def wanted_labels():
    lanes = np.arange(128)
    rows = np.zeros((8, 128), np.int32)
    for source, column in enumerate((1, 2, 0)):
        rows[source] = np.where(lanes < 3 * CELLS, (3 * (lanes // CELLS) + column) * CELLS + lanes % CELLS + 1, -1)
    return rows


def coaddition_kernel(
    order_ref, anchor_ref, frac_ref, scale_ref, weight_ref,
    image_ref, mask_ref, kern_ref, label_ref, wanted_ref,
    along_ref, down_ref, cols_ref, rows_ref, kcols_ref, krows_ref, icols_ref, irows_ref,
    out_ref,
    planes, tiles, beside, label_in, table, table_smem, send, recv, total, edge_send, edge_recv, rim_recv,
    side_send_sem, side_recv_sem, label_send_sem, label_recv_sem, row_send_sem, row_recv_sem,
    edge_send_sem, edge_recv_sem, rim_send_sem, rim_recv_sem, local_sem,
):
    patch, band = lax.axis_index("patch"), lax.axis_index("band")
    n_patch, n_band = lax.axis_size("patch"), lax.axis_size("band")
    left = {"patch": lax.rem(patch + n_patch - 1, n_patch)}
    right = {"patch": lax.rem(patch + 1, n_patch)}
    above = {"band": lax.rem(band + n_band - 1, n_band)}
    below = {"band": lax.rem(band + 1, n_band)}
    has_left = jnp.where(patch > 0, 1.0, 0.0)
    has_right = jnp.where(patch < n_patch - 1, 1.0, 0.0)
    has_above = jnp.where(band > 0, 1.0, 0.0)
    has_below = jnp.where(band < n_band - 1, 1.0, 0.0)

    barrier = pltpu.get_barrier_semaphore()
    for device in (left, right, above, below):
        pl.semaphore_signal(barrier, inc=1, device_id=device, device_id_type=MESH)

    def remote(src, dst, send_sem, recv_sem, device):
        return pltpu.make_async_remote_copy(
            src_ref=src, dst_ref=dst, send_sem=send_sem, recv_sem=recv_sem, device_id=device, device_id_type=MESH
        )

    sideways = (right, left)

    def label_copy(way):
        return remote(
            label_ref.at[pl.ds(0, CELLS)], label_in.at[way], label_send_sem.at[way], label_recv_sem.at[way], sideways[way]
        )

    def side_copy(way, part):
        piece = pl.ds(part * GROUP, GROUP)
        return remote(
            tiles.at[piece], beside.at[way, piece], side_send_sem.at[way, part], side_recv_sem.at[way, part], sideways[way]
        )

    upward = (above, below)

    def row_copy(way, part):
        piece = pl.ds(part * TC, TC)
        return remote(
            send.at[way, piece], recv.at[way, piece], row_send_sem.at[way, part], row_recv_sem.at[way, part], upward[way]
        )

    def edge_copy(way):
        return remote(
            edge_send.at[way], edge_recv.at[way], edge_send_sem.at[way], edge_recv_sem.at[way], sideways[way]
        )

    def rim_copy(way):
        rows = out_ref.at[pl.ds(TOP if way == 0 else TOP + SPAN - PAD, PAD)]
        return remote(rows, rim_recv.at[way], rim_send_sem.at[way], rim_recv_sem.at[way], upward[way])

    def prepare(block, carry):
        rows = pl.ds(pl.multiple_of(block * 32, 32), 32)
        usable = jnp.where((mask_ref[0, rows, :] & 7) != 7, 1.0, 0.0)
        masked = image_ref[0, rows, :].astype(F32) * usable
        for plane, value in enumerate((masked, usable)):
            moved = pltpu.roll(value, 768 - 64, 1)
            for way, data in enumerate((value.astype(BF16), moved.astype(BF16))):
                for j in range(6):
                    for i in range(2):
                        planes[way, plane, j, block * 2 + i] = data[16 * i : 16 * i + 16, 128 * j : 128 * j + 128]
        return carry

    lax.fori_loop(0, 768 // 32, prepare, 0)

    lane = lax.broadcasted_iota(jnp.int32, (ROWS, WIN), 1)
    sub = lax.broadcasted_iota(jnp.int32, (WIN, WIN), 0)
    short = lax.broadcasted_iota(jnp.int32, (8, WIN), 1)
    quantity = lax.broadcasted_iota(jnp.int32, (8, WIN), 0)
    index = (short + jnp.where(short < WARP_N - MARGIN, MARGIN, MARGIN - WARP_N)).astype(F32)

    def warp_rows(fraction, stretch, shift):
        position = (5.0 + fraction) + index * (1.0 + stretch)
        nearest = jnp.floor(position + 0.5)
        odd = nearest - 2.0 * jnp.floor(nearest * 0.5)
        part = position - nearest
        sine = (1.0 - 2.0 * odd) * part * poly(SIN_PI, part * part)
        sign = (1 - 2 * (shift & 1)).astype(F32)
        amplitude = ((-5.0 / math.pi**2) * sign) * sine
        turn = position - 10.0 * jnp.floor(position * 0.1) + lax.rem(shift, 10).astype(F32)
        turn = turn * 0.1
        turn = turn - jnp.floor(turn + 0.5)
        square = turn * turn
        cosine, sine = poly(COS_TURN, square), turn * poly(SIN_TURN, square)
        position = jnp.where(short < WARP_N, position, 1e4)
        return jnp.where(quantity == 0, position, jnp.where(quantity == 1, amplitude * cosine, amplitude * sine))

    weight = weight_ref[0]
    each = range(GROUP)

    def work(step, carry):
        chosen = [within(order_ref[step * GROUP + g], 2 * CELLS - 1) for g in each]
        half_img, half_cov, lt = [], [], []
        for g in each:
            t = chosen[g]
            first_row, first_col = anchor_ref[0, t, 0], anchor_ref[0, t, 1]
            row16 = within(first_row // 16, (768 - WIN) // 16)
            col64 = within(first_col // 64, (768 - WIN) // 64)
            off_r = first_row - row16 * 16
            off_c = first_col - col64 * 64
            par = within(col64 % 2, 1)
            pair = within(col64 // 2, 4)
            s_img, s_cov = (
                jnp.concatenate(
                    [
                        jnp.concatenate([planes[par, plane, pair + j, row16 + i] for i in range(16)], axis=0)
                        for j in range(2)
                    ],
                    axis=1,
                )
                for plane in range(2)
            )
            q0 = jnp.transpose(warp_rows(frac_ref[0, t, 0], scale_ref[0, t, 0], off_r))[:ROWS]
            d0 = (lane - off_r).astype(F32) - q0[:, 0:1]
            l0 = lanczos(d0, q0[:, 1:2], q0[:, 2:3], along_ref[0:1, :], along_ref[1:2, :])
            q1 = warp_rows(frac_ref[0, t, 1], scale_ref[0, t, 1], off_c)
            d1 = (sub - off_c).astype(F32) - q1[0:1, :]
            cosd = jnp.concatenate([down_ref[0], down_ref[0]], axis=1)
            sind = jnp.concatenate([down_ref[1], down_ref[1]], axis=1)
            lt.append(lanczos(d1, q1[1:2, :], q1[2:3, :], cosd, sind))
            half_img.append(dot(l0, s_img).astype(BF16))
            half_cov.append(dot(l0[:TILE], s_cov).astype(BF16))
        warped = [dot(half_img[g], lt[g]).astype(BF16) for g in each]
        for g in each:
            coverage = dot(half_cov[g], lt[g][:, :TILE])
            tiles[step * GROUP + g, 1] = (weight * coverage).astype(BF16)
        x1 = dot(jnp.concatenate(warped, axis=0), cols_ref[...]).astype(BF16)
        x2 = [dot(rows_ref[...], x1[g * ROWS : (g + 1) * ROWS]) for g in each]
        k1 = dot(jnp.concatenate([kern_ref[chosen[g]] for g in each], axis=0), kcols_ref[...])
        k1h = k1.astype(BF16)
        k1l = (k1 - k1h.astype(F32)).astype(BF16)
        z = []
        for g in each:
            h, l = k1h[g * 48 : g * 48 + 48], k1l[g * 48 : g * 48 + 48]
            k2 = dot(krows_ref[...], jnp.concatenate([h, l, h], axis=0))
            x = x2[g]
            xrr, xri, xir, xii = x[:HALF, :128], x[:HALF, 128:], x[HALF:, :128], x[HALF:, 128:]
            krr, kri, kir, kii = k2[:HALF, :128], k2[:HALF, 128:], k2[HALF:, :128], k2[HALF:, 128:]
            xpr, xpi, xmr, xmi = xrr - xii, xir + xri, xrr + xii, xir - xri
            kpr, kpi, kmr, kmi = krr - kii, kir + kri, krr + kii, kir - kri
            ppr, ppi = xpr * kpr - xpi * kpi, xpr * kpi + xpi * kpr
            pmr, pmi = xmr * kmr - xmi * kmi, xmr * kmi + xmi * kmr
            top = jnp.concatenate([ppr + pmr, ppi - pmi], axis=1)
            bottom = jnp.concatenate([ppi + pmi, pmr - ppr], axis=1)
            z.append(jnp.concatenate([top, bottom], axis=0).astype(BF16))
        y = dot(jnp.concatenate(z, axis=0), icols_ref[...])
        y = y[:, :TILE] + y[:, TILE:]
        yh = y.astype(BF16)
        yl = (y - yh.astype(F32)).astype(BF16)
        ycat = jnp.concatenate([yh, yl], axis=1)
        for g in each:
            o = dot(irows_ref[...], ycat[g * ROWS : (g + 1) * ROWS])
            matched = o[:TILE, :TILE] + (o[:TILE, TILE:] + o[TILE:, :TILE])
            tiles[step * GROUP + g, 0] = (weight * matched).astype(BF16)

        @pl.when(step == 0)
        def _():
            pl.semaphore_wait(barrier, 4)
            for way in range(2):
                label_copy(way).start()

        @pl.when(step < CELLS // GROUP)
        def _():
            for way in range(2):
                side_copy(way, step).start()

        return carry

    lax.fori_loop(0, 2 * CELLS // GROUP, work, 0)

    for way in range(2):
        label_copy(way).wait()
    lookup = [label_ref[:CELLS, :], label_in[0], label_in[1]]
    for source in range(3):
        found = jnp.zeros((1, 128), jnp.int32)
        for slot in range(CELLS):
            same = lookup[source][slot : slot + 1] == wanted_ref[source : source + 1, :]
            found = found + jnp.where(same, slot + 1, 0)
        table[source : source + 1, :] = found - 1
    to_smem = pltpu.make_async_copy(table, table_smem, local_sem)
    to_smem.start()
    to_smem.wait()

    def side_wait(part, carry):
        for way in range(2):
            side_copy(way, part).wait()
        return carry

    lax.fori_loop(0, CELLS // GROUP, side_wait, 0)

    def gather(position):
        value = None
        for source in range(3):
            slot = table_smem[source, position]
            present = jnp.where(slot >= 0, 1.0, 0.0)
            at = within(slot, CELLS - 1)
            data = tiles[at] if source == 0 else beside[source - 1, at]
            term = data.astype(F32) * present
            value = term if value is None else value + term
        return value

    def outgoing(part, carry):
        for way in range(2):
            for c in range(TC):
                cell = part * TC + c
                send[way, cell] = gather(2 * CELLS * way + cell).astype(BF16)
            row_copy(way, part).start()
        return carry

    lax.fori_loop(0, TR, outgoing, 0)

    def staying(cell, carry):
        total[cell] = gather(CELLS + cell) + tiles[CELLS + cell].astype(F32)
        return carry

    lax.fori_loop(0, CELLS, staying, 0)

    def finish(part, carry):
        for way in range(2):
            row_copy(way, part).wait()
        rows = pl.ds(pl.multiple_of(TOP + part * TILE, 8), TILE)
        for c in range(TC):
            cell = part * TC + c
            value = total[cell] + (recv[0, cell].astype(F32) + recv[1, cell].astype(F32))
            out_ref[rows, c * TILE : (c + 1) * TILE] = value[0] / (jnp.maximum(value[1], 0.0) + 1.0)
        return carry

    lax.fori_loop(0, TR, finish, 0)

    lane = lax.broadcasted_iota(jnp.int32, (TILE, TILE), 1)
    packed = [jnp.zeros((TILE, TILE), F32)] * 2
    for q in range(4):
        rows = pl.ds(TOP + q * TILE, TILE)
        mine = (lane >= PAD * q) & (lane < PAD * (q + 1))
        ends = (out_ref[rows, SPAN - TILE : SPAN], out_ref[rows, :TILE])
        for way, turn in enumerate((PAD * q + PAD, PAD * q)):
            moved = ends[way] if turn % TILE == 0 else pltpu.roll(ends[way], turn % TILE, 1)
            packed[way] = jnp.where(mine, moved, packed[way])
    for way in range(2):
        edge_send[way] = packed[way]
        edge_copy(way).start()
    for way in range(2):
        edge_copy(way).wait()
    from_left, from_right = edge_recv[0] * has_left, edge_recv[1] * has_right
    for q in range(4):
        turn = (TILE - PAD * q) % TILE
        near = from_right if turn == 0 else pltpu.roll(from_right, turn, 1)
        turn = (TILE - PAD - PAD * q) % TILE
        far = from_left if turn == 0 else pltpu.roll(from_left, turn, 1)
        out_ref[TOP + q * TILE : TOP + (q + 1) * TILE, SPAN:] = jnp.where(
            lane < PAD, near, jnp.where(lane >= TILE - PAD, far, 0.0)
        )
    for way in range(2):
        rim_copy(way).start()
    blank = jnp.zeros((8, WIDE), F32)
    out_ref[0:8, :] = blank
    out_ref[TALL - 8 : TALL, :] = blank
    for way in range(2):
        rim_copy(way).wait()
    out_ref[8:TOP, :] = rim_recv[1] * has_above
    out_ref[TOP + SPAN : TALL - 8, :] = rim_recv[0] * has_below


def coaddition_call(order, anchor, frac, scale, weight, image, mask, kern, label, consts):
    scalars = (order, anchor, frac, scale, weight)
    arrays = (image, mask, kern, label, jnp.asarray(wanted_labels())) + tuple(consts)
    dma = pltpu.SemaphoreType.DMA
    tile = (2, TILE, TILE)
    parts = CELLS // GROUP
    return pl.pallas_call(
        coaddition_kernel,
        in_specs=[pl.BlockSpec(memory_space=pltpu.SMEM)] * len(scalars) + [whole(a) for a in arrays],
        out_specs=pl.BlockSpec((TALL, WIDE), lambda: (0, 0)),
        out_shape=jax.ShapeDtypeStruct((TALL, WIDE), F32),
        scratch_shapes=[
            pltpu.VMEM((2, 2, 6, 48, 16, 128), BF16),
            pltpu.VMEM((2 * CELLS,) + tile, BF16),
            pltpu.VMEM((2, CELLS) + tile, BF16),
            pltpu.VMEM((2, CELLS, 128), jnp.int32),
            pltpu.VMEM((8, 128), jnp.int32),
            pltpu.SMEM((8, 128), jnp.int32),
            pltpu.VMEM((2, CELLS) + tile, BF16),
            pltpu.VMEM((2, CELLS) + tile, BF16),
            pltpu.VMEM((CELLS,) + tile, F32),
            pltpu.VMEM((2, TILE, TILE), F32),
            pltpu.VMEM((2, TILE, TILE), F32),
            pltpu.VMEM((2, PAD, WIDE), F32),
            dma((2, parts)), dma((2, parts)), dma((2,)), dma((2,)), dma((2, TR)), dma((2, TR)),
            dma((2,)), dma((2,)), dma((2,)), dma((2,)), dma(()),
        ],
        compiler_params=pltpu.CompilerParams(
            vmem_limit_bytes=56 * 2**20, collective_id=0, has_side_effects=True
        ),
    )(*scalars, *arrays)


LEVEL_ROWS = ((8, 584), (16, 576), (24, 568), (40, 552))
BLOCK = 128


def starlet_kernel(edge_ref, first_ref, details_ref, smooth_ref, ping, pong):
    top, bottom, left, right = (edge_ref[i] for i in range(4))
    tiles = WIDE // 128
    zero = jnp.zeros((8, WIDE), F32)
    for ref in (ping, pong):
        ref[0:8, :] = zero
        ref[TALL - 8 : TALL, :] = zero
    source = first_ref
    for k in range(SCALES):
        s = 2**k
        target = (ping, pong)[k % 2]
        begin, end = LEVEL_ROWS[k]

        def smoothed(view, count, s=s):
            def near(by):
                return view[16 + by : 16 + by + count, :]

            center = near(0)
            rows = (near(-2 * s) + near(2 * s)) + 4.0 * (near(-s) + near(s)) + 6.0 * center
            parts = [rows[:, 128 * j : 128 * (j + 1)] for j in range(tiles)]
            lane = lax.broadcasted_iota(jnp.int32, (count, 128), 1)

            def after(by):
                turned = [pltpu.roll(part, by, 1) for part in parts]
                return [jnp.where(lane < by, turned[j - 1], turned[j]) for j in range(tiles)]

            def before(by):
                turned = [pltpu.roll(part, 128 - by, 1) for part in parts]
                return [jnp.where(lane >= 128 - by, turned[(j + 1) % tiles], turned[j]) for j in range(tiles)]

            a, b, c, d = after(2 * s), before(2 * s), after(s), before(s)
            full = [((a[j] + b[j]) + 4.0 * (c[j] + d[j]) + 6.0 * parts[j]) * (1.0 / 256.0) for j in range(tiles)]
            return center, full

        def store(row, count, full, factor, target=target):
            lane = lax.broadcasted_iota(jnp.int32, (count, 128), 1)
            side = jnp.where(lane < 64, right, left)
            for j in range(tiles):
                value = full[j] * side if j == tiles - 1 else full[j]
                value = value if factor is None else value * factor
                target[pl.ds(row, count), 128 * j : 128 * (j + 1)] = value

        if k < SCALES - 1:
            for row, last, factor in ((begin, TOP, top), (TOP + SPAN, end, bottom)):
                low, high = max(row - 16, 0), min(last + 16, TALL)
                count = last - row
                rows = source[low:high, :]
                if low > row - 16:
                    rows = jnp.concatenate([jnp.zeros((low - row + 16, WIDE), F32), rows], axis=0)
                if high < last + 16:
                    rows = jnp.concatenate([rows, jnp.zeros((last + 16 - high, WIDE), F32)], axis=0)
                store(row, count, smoothed(rows, count)[1], factor)

        def one(block, carry, k=k, source=source, smoothed=smoothed, store=store):
            row = pl.multiple_of(TOP + block * BLOCK, 8)
            here = pl.multiple_of(block * BLOCK, 8)
            center, full = smoothed(source.at[pl.ds(pl.multiple_of(row - 16, 8), BLOCK + 32), :], BLOCK)
            if k < SCALES - 1:
                store(row, BLOCK, full, None)
            for j in range(SPAN // 128):
                cols = slice(128 * j, 128 * (j + 1))
                details_ref[k, pl.ds(here, BLOCK), cols] = center[:, cols] - full[j]
                if k == SCALES - 1:
                    smooth_ref[pl.ds(here, BLOCK), cols] = full[j]
            return carry

        lax.fori_loop(0, SPAN // BLOCK, one, 0)
        source = target


def starlet_call(edges, first):
    return pl.pallas_call(
        starlet_kernel,
        in_specs=[pl.BlockSpec(memory_space=pltpu.SMEM), whole(first)],
        out_specs=[
            pl.BlockSpec((SCALES, SPAN, SPAN), lambda: (0, 0, 0)),
            pl.BlockSpec((SPAN, SPAN), lambda: (0, 0)),
        ],
        out_shape=[
            jax.ShapeDtypeStruct((SCALES, SPAN, SPAN), F32),
            jax.ShapeDtypeStruct((SPAN, SPAN), F32),
        ],
        scratch_shapes=[pltpu.VMEM((TALL, WIDE), F32)] * 2,
        compiler_params=pltpu.CompilerParams(vmem_limit_bytes=48 * 2**20),
    )(edges, first)


def shards(image, mask, weight, anchor, frac, scale, kernels, dest, offset):
    order, label = order_call(dest, offset)
    padded = jnp.pad(kernels[0], ((0, 0), (0, 7), (0, 23)))
    kern = jnp.concatenate([padded, padded], axis=-1)
    first = coaddition_call(order, anchor, frac, scale, weight, image, mask, kern, label, constants())
    band, patch = lax.axis_index("band"), lax.axis_index("patch")
    edges = jnp.stack(
        [band > 0, band < lax.axis_size("band") - 1, patch > 0, patch < lax.axis_size("patch") - 1]
    ).astype(F32)
    return tuple(starlet_call(edges, first))


def solution(mesh):
    owner = ("patch", "band")
    in_specs = (
        P(owner, None, None),
        P(owner, None, None),
        P(owner),
        P(owner, None, None),
        P(owner, None, None),
        P(owner, None, None),
        P(owner, None, None, None),
        P(owner, None),
        P(owner, None),
    )
    out_specs = (P(None, "band", "patch"), P("band", "patch"))
    return jax.shard_map(shards, mesh=mesh, in_specs=in_specs, out_specs=out_specs, check_vma=False)
```

```python
import math
import numpy as np
import ml_dtypes
import jax
import jax.numpy as jnp
from jax import lax
from jax.experimental import pallas as pl
from jax.experimental.pallas import tpu as pltpu
from jax.sharding import PartitionSpec as P

TILE, KS, SCALES, TR, TC, MARGIN, WARP_N, SRC_N = 128, 41, 4, 4, 4, 20, 168, 184
ROWS = 176
HALF = 88
WIN = 256
F32, BF16 = jnp.float32, jnp.bfloat16


def split_bf16(values):
    high = values.astype(ml_dtypes.bfloat16)
    low = (values - high.astype(np.float64)).astype(ml_dtypes.bfloat16)
    return high, low


def spectra():
    bins = np.arange(WARP_N // 2 + 1)

    def forward(points, sign):
        angle = 2.0 * np.pi / WARP_N * np.outer(bins, points)
        return np.cos(angle), sign * np.sin(angle)

    order = (np.arange(WARP_N) + MARGIN) % WARP_N
    real, imag = forward(order, -1.0)
    rows = np.zeros((ROWS, WIN))
    rows[: len(bins), :WARP_N] = real
    rows[HALF : HALF + len(bins), :WARP_N] = imag
    cols = np.zeros((WIN, WIN))
    cols[:WARP_N, : len(bins)] = real.T
    cols[:WARP_N, 128 : 128 + len(bins)] = imag.T
    real, imag = forward(np.arange(KS), 1.0)
    kcols = np.zeros((64, WIN))
    kcols[:KS, : len(bins)] = real.T
    kcols[:KS, 128 : 128 + len(bins)] = imag.T
    krows = np.zeros((ROWS, 48))
    krows[: len(bins), :KS] = real
    krows[HALF : HALF + len(bins), :KS] = imag
    count = np.full(len(bins), 2.0)
    count[0] = count[-1] = 1.0
    angle = 2.0 * np.pi / WARP_N * np.outer(np.arange(TILE), bins)
    back_real = np.cos(angle) * count / WARP_N
    back_imag = -np.sin(angle) * count / WARP_N
    icols = np.zeros((WIN, TILE))
    icols[: len(bins)] = back_real.T
    icols[128 : 128 + len(bins)] = back_imag.T
    irows = np.zeros((TILE, ROWS))
    irows[:, : len(bins)] = 0.5 * back_real
    irows[:, HALF : HALF + len(bins)] = 0.5 * back_imag
    kcols_high, kcols_low = split_bf16(kcols)
    krows_high, krows_low = split_bf16(krows)
    icols_high, icols_low = split_bf16(icols)
    irows_high, irows_low = split_bf16(irows)
    rows_pad = rows[:, :ROWS]
    return (
        cols.astype(ml_dtypes.bfloat16),
        rows_pad.astype(ml_dtypes.bfloat16),
        np.concatenate([kcols_high, kcols_low]),
        np.concatenate([krows_high, krows_high, krows_low], axis=1),
        np.concatenate([icols_high, icols_low], axis=1),
        np.concatenate([irows_high, irows_low]),
    )


def phase_constants():
    j = np.arange(WIN)
    sign = 1.0 - 2.0 * (j % 2)
    cosine = (sign * np.cos(np.pi * j / 5.0)).astype(np.float32)
    sine = (sign * np.sin(np.pi * j / 5.0)).astype(np.float32)
    along = np.zeros((8, WIN), np.float32)
    along[0], along[1] = cosine, sine
    down = np.stack([np.repeat(cosine[:, None], 128, 1), np.repeat(sine[:, None], 128, 1)])
    return along, down


def poly(coefficients, x):
    total = jnp.full_like(x, coefficients[-1])
    for value in coefficients[-2::-1]:
        total = total * x + value
    return total


SIN_PI = (3.14159265, -5.16771276, 2.55016332, -0.5992522, 0.0820504, -0.00702839)
SIN_TURN = (6.28318531, -41.34170222, 81.60524742, -76.70580022, 42.05775402, -15.08656526, 3.78131888, -0.62077872)
COS_TURN = (1.0, -19.73920874, 64.93938908, -85.45665831, 60.24213134, -26.40466819, 7.80013144, -1.45311232)


def lanczos(d, cos_row, sin_row, cos_col, sin_col):
    d2 = d * d
    u = cos_row * sin_col - sin_row * cos_col
    g = u / d2
    g = jnp.where(d2 < 1e-5, 1.0, g)
    return jnp.where(d2 < 25.0, g, 0.0).astype(BF16)


def dot(a, b):
    return lax.dot_general(a, b, (((1,), (0,)), ((), ())), preferred_element_type=F32)


def constants():
    along, down = phase_constants()
    return [jnp.asarray(a) for a in (along, down) + spectra()]


CELLS = TR * TC
GROUP = 4
SLAB = TILE // 2
SPAN = TR * TILE
PAD = 32
WIDE = SPAN + 128
TOP = 8 + PAD
TALL = SPAN + 2 * TOP
MESH = pl.DeviceIdType.MESH


def within(value, top):
    return jnp.minimum(jnp.maximum(value, 0), top)


def whole(a):
    return pl.BlockSpec(a.shape, lambda *_: (0,) * a.ndim)


def order_kernel(dest_ref, offset_ref, order_ref, label_ref):
    filled = jnp.int32(0)
    for i in range(2 * CELLS):
        code, cell = dest_ref[0, i], offset_ref[0, i]
        away = code != 4
        slot = jnp.where(away, filled, CELLS + cell)
        order_ref[slot] = jnp.int32(i)
        label_ref[pl.ds(slot, 1), :] = jnp.full((1, 128), code * CELLS + cell + 1, jnp.int32)
        filled = filled + away.astype(jnp.int32)


def order_call(dest, offset):
    smem = pl.BlockSpec(memory_space=pltpu.SMEM)
    return pl.pallas_call(
        order_kernel,
        in_specs=[smem, smem],
        out_specs=[smem, pl.BlockSpec((2 * CELLS + 8, 128), lambda: (0, 0))],
        out_shape=[
            jax.ShapeDtypeStruct((2 * CELLS,), jnp.int32),
            jax.ShapeDtypeStruct((2 * CELLS + 8, 128), jnp.int32),
        ],
    )(dest, offset)


def wanted_labels():
    lanes = np.arange(128)
    rows = np.full((8, 128), -1, np.int32)
    for source, step in enumerate((1, 2, 0)):
        rows[source] = (3 * (lanes // CELLS) + step) * CELLS + lanes % CELLS + 1
        rows[3 + source] = (3 * step + lanes // CELLS) * CELLS + lanes % CELLS + 1
    return np.where(lanes < 3 * CELLS, rows, -1).astype(np.int32)


def coaddition_kernel(
    order_ref, anchor_ref, frac_ref, scale_ref, weight_ref,
    image_ref, mask_ref, kern_ref, label_ref, wanted_ref,
    along_ref, down_ref, cols_ref, rows_ref, kcols_ref, krows_ref, icols_ref, irows_ref,
    out_ref,
    planes, tiles, upper_in, lower_in, label_in, table, table_smem, send, recv, total, edge_send, edge_recv, rim_recv, corner_recv,
    early_send_sem, early_recv_sem, label_send_sem, label_recv_sem, late_send_sem, late_recv_sem,
    halo_send_sem, halo_recv_sem, local_sem,
):
    patch, band = lax.axis_index("patch"), lax.axis_index("band")
    n_patch, n_band = lax.axis_size("patch"), lax.axis_size("band")
    left_patch, right_patch = lax.rem(patch + n_patch - 1, n_patch), lax.rem(patch + 1, n_patch)
    above_band, below_band = lax.rem(band + n_band - 1, n_band), lax.rem(band + 1, n_band)
    left, right = {"patch": left_patch, "band": band}, {"patch": right_patch, "band": band}
    above, below = {"patch": patch, "band": above_band}, {"patch": patch, "band": below_band}
    corners = [{"patch": p, "band": b} for b in (above_band, below_band) for p in (left_patch, right_patch)]
    has_left = jnp.where(patch > 0, 1.0, 0.0)
    has_right = jnp.where(patch < n_patch - 1, 1.0, 0.0)
    has_above = jnp.where(band > 0, 1.0, 0.0)
    has_below = jnp.where(band < n_band - 1, 1.0, 0.0)

    barrier = pltpu.get_barrier_semaphore()
    around = [left, right, above, below] + corners
    for device in around:
        pl.semaphore_signal(barrier, inc=1, device_id=device, device_id_type=MESH)

    def remote(src, dst, send_sem, recv_sem, device):
        return pltpu.make_async_remote_copy(
            src_ref=src, dst_ref=dst, send_sem=send_sem, recv_sem=recv_sem, device_id=device, device_id_type=MESH
        )

    beside = (upper_in, lower_in)

    early_to = ((right, left), (below, above))
    late_to = ((above, below), (left, right))

    def label_copy(half, way):
        return remote(
            label_ref.at[pl.ds(0, CELLS)],
            label_in.at[half, way],
            label_send_sem.at[half, way],
            label_recv_sem.at[half, way],
            early_to[half][way],
        )

    def early_copy(half, way, part):
        piece = pl.ds(part * GROUP, GROUP)
        return remote(
            tiles.at[half, piece],
            beside[half].at[way, piece],
            early_send_sem.at[half, way, part],
            early_recv_sem.at[half, way, part],
            early_to[half][way],
        )

    def late_copy(half, way, part):
        piece = pl.ds(part * TC, TC)
        return remote(
            send.at[half, way, piece],
            recv.at[half, way, piece],
            late_send_sem.at[half, way, part],
            late_recv_sem.at[half, way, part],
            late_to[half][way],
        )

    first_rows, last_rows = pl.ds(TOP, PAD), pl.ds(TOP + SPAN - PAD, PAD)

    def halo_copies():
        pairs = [(edge_send.at[0], edge_recv.at[0], right), (edge_send.at[1], edge_recv.at[1], left)]
        pairs += [
            (out_ref.at[first_rows, pl.ds(0, SPAN)], rim_recv.at[0], above),
            (out_ref.at[last_rows, pl.ds(0, SPAN)], rim_recv.at[1], below),
        ]
        for number, device in enumerate(corners):
            cols = pl.ds(0, TILE) if number % 2 == 0 else pl.ds(SPAN - TILE, TILE)
            rows = first_rows if number < 2 else last_rows
            pairs.append((out_ref.at[rows, cols], corner_recv.at[number], device))
        return [
            remote(src, dst, halo_send_sem.at[number], halo_recv_sem.at[number], device)
            for number, (src, dst, device) in enumerate(pairs)
        ]

    def prepare(block, carry):
        rows = pl.ds(pl.multiple_of(block * 32, 32), 32)
        usable = jnp.where((mask_ref[0, rows, :] & 7) != 7, 1.0, 0.0)
        masked = image_ref[0, rows, :].astype(F32) * usable
        for plane, value in enumerate((masked, usable)):
            moved = pltpu.roll(value, 768 - 64, 1)
            for way, data in enumerate((value.astype(BF16), moved.astype(BF16))):
                for j in range(6):
                    for i in range(2):
                        planes[way, plane, j, block * 2 + i] = data[16 * i : 16 * i + 16, 128 * j : 128 * j + 128]
        return carry

    lax.fori_loop(0, 768 // 32, prepare, 0)

    lane = lax.broadcasted_iota(jnp.int32, (ROWS, WIN), 1)
    sub = lax.broadcasted_iota(jnp.int32, (WIN, WIN), 0)
    short = lax.broadcasted_iota(jnp.int32, (8, WIN), 1)
    quantity = lax.broadcasted_iota(jnp.int32, (8, WIN), 0)
    index = (short + jnp.where(short < WARP_N - MARGIN, MARGIN, MARGIN - WARP_N)).astype(F32)

    def warp_rows(fraction, stretch, shift):
        position = (5.0 + fraction) + index * (1.0 + stretch)
        nearest = jnp.floor(position + 0.5)
        odd = nearest - 2.0 * jnp.floor(nearest * 0.5)
        part = position - nearest
        sine = (1.0 - 2.0 * odd) * part * poly(SIN_PI, part * part)
        sign = (1 - 2 * (shift & 1)).astype(F32)
        amplitude = ((-5.0 / math.pi**2) * sign) * sine
        turn = position - 10.0 * jnp.floor(position * 0.1) + lax.rem(shift, 10).astype(F32)
        turn = turn * 0.1
        turn = turn - jnp.floor(turn + 0.5)
        square = turn * turn
        cosine, sine = poly(COS_TURN, square), turn * poly(SIN_TURN, square)
        position = jnp.where(short < WARP_N, position, 1e4)
        return jnp.where(quantity == 0, position, jnp.where(quantity == 1, amplitude * cosine, amplitude * sine))

    weight = weight_ref[0]
    each = range(GROUP)

    def store_tile(slot, plane, value):
        for half in range(2):
            tiles[half, slot, plane] = value[half * SLAB : (half + 1) * SLAB].astype(BF16)

    def gather(half, position):
        value = None
        for source in range(3):
            slot = table_smem[3 * half + source, position]
            present = jnp.where(slot >= 0, 1.0, 0.0)
            at = within(slot, CELLS - 1)
            data = tiles[half, at] if source == 0 else beside[half][source - 1, at]
            term = data.astype(F32) * present
            value = term if value is None else value + term
        return value

    def find_slots():
        for half in range(2):
            for way in range(2):
                label_copy(half, way).wait()
            for source in range(3):
                lookup = label_ref[:CELLS, :] if source == 0 else label_in[half, source - 1]
                number = 3 * half + source
                found = jnp.zeros((1, 128), jnp.int32)
                for slot in range(CELLS):
                    same = lookup[slot : slot + 1] == wanted_ref[number : number + 1, :]
                    found = found + jnp.where(same, slot + 1, 0)
                table[number : number + 1, :] = found - 1
        to_smem = pltpu.make_async_copy(table, table_smem, local_sem)
        to_smem.start()
        to_smem.wait()

    def pass_on(half):
        for part in range(CELLS // GROUP):
            for way in range(2):
                early_copy(half, way, part).wait()

        def outgoing(part, carry):
            for way in range(2):
                for c in range(TC):
                    cell = part * TC + c
                    send[half, way, cell] = gather(half, 2 * CELLS * way + cell).astype(BF16)
                late_copy(half, way, part).start()
            return carry

        lax.fori_loop(0, TR, outgoing, 0)

    def work(step, carry):
        chosen = [within(order_ref[step * GROUP + g], 2 * CELLS - 1) for g in each]
        half_img, half_cov, lt = [], [], []
        for g in each:
            t = chosen[g]
            first_row, first_col = anchor_ref[0, t], anchor_ref[1, t]
            row16 = within(first_row // 16, (768 - WIN) // 16)
            col64 = within(first_col // 64, (768 - WIN) // 64)
            off_r = first_row - row16 * 16
            off_c = first_col - col64 * 64
            par = within(col64 % 2, 1)
            pair = within(col64 // 2, 4)
            s_img, s_cov = (
                jnp.concatenate(
                    [
                        jnp.concatenate([planes[par, plane, pair + j, row16 + i] for i in range(16)], axis=0)
                        for j in range(2)
                    ],
                    axis=1,
                )
                for plane in range(2)
            )
            q0 = jnp.transpose(warp_rows(frac_ref[0, t], scale_ref[0, t], off_r))[:ROWS]
            d0 = (lane - off_r).astype(F32) - q0[:, 0:1]
            l0 = lanczos(d0, q0[:, 1:2], q0[:, 2:3], along_ref[0:1, :], along_ref[1:2, :])
            q1 = warp_rows(frac_ref[1, t], scale_ref[1, t], off_c)
            d1 = (sub - off_c).astype(F32) - q1[0:1, :]
            cosd = jnp.concatenate([down_ref[0], down_ref[0]], axis=1)
            sind = jnp.concatenate([down_ref[1], down_ref[1]], axis=1)
            lt.append(lanczos(d1, q1[1:2, :], q1[2:3, :], cosd, sind))
            half_img.append(dot(l0, s_img).astype(BF16))
            half_cov.append(dot(l0[:TILE], s_cov).astype(BF16))
        warped = [dot(half_img[g], lt[g]).astype(BF16) for g in each]
        for g in each:
            coverage = dot(half_cov[g], lt[g][:, :TILE])
            store_tile(step * GROUP + g, 1, weight * coverage)
        x1 = dot(jnp.concatenate(warped, axis=0), cols_ref[...]).astype(BF16)
        x2 = [dot(rows_ref[...], x1[g * ROWS : (g + 1) * ROWS]) for g in each]
        k1 = dot(jnp.concatenate([kern_ref[chosen[g]] for g in each], axis=0), kcols_ref[...])
        k1h = k1.astype(BF16)
        k1l = (k1 - k1h.astype(F32)).astype(BF16)
        z = []
        for g in each:
            h, l = k1h[g * 48 : g * 48 + 48], k1l[g * 48 : g * 48 + 48]
            k2 = dot(krows_ref[...], jnp.concatenate([h, l, h], axis=0))
            x = x2[g]
            xrr, xri, xir, xii = x[:HALF, :128], x[:HALF, 128:], x[HALF:, :128], x[HALF:, 128:]
            krr, kri, kir, kii = k2[:HALF, :128], k2[:HALF, 128:], k2[HALF:, :128], k2[HALF:, 128:]
            xpr, xpi, xmr, xmi = xrr - xii, xir + xri, xrr + xii, xir - xri
            kpr, kpi, kmr, kmi = krr - kii, kir + kri, krr + kii, kir - kri
            ppr, ppi = xpr * kpr - xpi * kpi, xpr * kpi + xpi * kpr
            pmr, pmi = xmr * kmr - xmi * kmi, xmr * kmi + xmi * kmr
            top = jnp.concatenate([ppr + pmr, ppi - pmi], axis=1)
            bottom = jnp.concatenate([ppi + pmi, pmr - ppr], axis=1)
            z.append(jnp.concatenate([top, bottom], axis=0).astype(BF16))
        y = dot(jnp.concatenate(z, axis=0), icols_ref[...])
        y = y[:, :TILE] + y[:, TILE:]
        yh = y.astype(BF16)
        yl = (y - yh.astype(F32)).astype(BF16)
        ycat = jnp.concatenate([yh, yl], axis=1)
        for g in each:
            o = dot(irows_ref[...], ycat[g * ROWS : (g + 1) * ROWS])
            matched = o[:TILE, :TILE] + (o[:TILE, TILE:] + o[TILE:, :TILE])
            store_tile(step * GROUP + g, 0, weight * matched)

        @pl.when(step == 0)
        def _():
            pl.semaphore_wait(barrier, len(around))
            for half in range(2):
                for way in range(2):
                    label_copy(half, way).start()

        @pl.when(step < CELLS // GROUP)
        def _():
            for half in range(2):
                for way in range(2):
                    early_copy(half, way, step).start()

        @pl.when(step == 4)
        def _():
            find_slots()
            pass_on(1)

        @pl.when(step == 6)
        def _():
            pass_on(0)

        return carry

    lax.fori_loop(0, 2 * CELLS // GROUP, work, 0)

    def staying(cell, carry):
        for half in range(2):
            total[half, cell] = gather(half, CELLS + cell) + tiles[half, CELLS + cell].astype(F32)
        return carry

    lax.fori_loop(0, CELLS, staying, 0)

    def finish(part, carry):
        for half in range(2):
            for way in range(2):
                late_copy(half, way, part).wait()
            rows = pl.ds(pl.multiple_of(TOP + part * TILE + half * SLAB, 8), SLAB)
            for c in range(TC):
                cell = part * TC + c
                value = total[half, cell] + (recv[half, 0, cell].astype(F32) + recv[half, 1, cell].astype(F32))
                out_ref[rows, c * TILE : (c + 1) * TILE] = value[0] / (jnp.maximum(value[1], 0.0) + 1.0)
        return carry

    lax.fori_loop(0, TR, finish, 0)

    lane = lax.broadcasted_iota(jnp.int32, (TILE, TILE), 1)
    packed = [jnp.zeros((TILE, TILE), F32)] * 2
    for q in range(4):
        rows = pl.ds(TOP + q * TILE, TILE)
        mine = (lane >= PAD * q) & (lane < PAD * (q + 1))
        ends = (out_ref[rows, SPAN - TILE : SPAN], out_ref[rows, :TILE])
        for way, turn in enumerate((PAD * q + PAD, PAD * q)):
            moved = ends[way] if turn % TILE == 0 else pltpu.roll(ends[way], turn % TILE, 1)
            packed[way] = jnp.where(mine, moved, packed[way])
    for way in range(2):
        edge_send[way] = packed[way]
    copies = halo_copies()
    for copy in copies:
        copy.start()
    blank = jnp.zeros((8, WIDE), F32)
    out_ref[0:8, :] = blank
    out_ref[TALL - 8 : TALL, :] = blank
    for copy in copies:
        copy.wait()
    from_left, from_right = edge_recv[0] * has_left, edge_recv[1] * has_right
    for q in range(4):
        turn = (TILE - PAD * q) % TILE
        near = from_right if turn == 0 else pltpu.roll(from_right, turn, 1)
        turn = (TILE - PAD - PAD * q) % TILE
        far = from_left if turn == 0 else pltpu.roll(from_left, turn, 1)
        out_ref[TOP + q * TILE : TOP + (q + 1) * TILE, SPAN:] = jnp.where(
            lane < PAD, near, jnp.where(lane >= TILE - PAD, far, 0.0)
        )
    lane = lax.broadcasted_iota(jnp.int32, (PAD, TILE), 1)
    for rows, arrived, far, near, factor in (
        (slice(8, TOP), 1, 3, 2, has_above),
        (slice(TOP + SPAN, TALL - 8), 0, 1, 0, has_below),
    ):
        out_ref[rows, :SPAN] = rim_recv[arrived] * factor
        near, far = corner_recv[near] * (has_right * factor), corner_recv[far] * (has_left * factor)
        out_ref[rows, SPAN:] = jnp.where(lane < PAD, near, jnp.where(lane >= TILE - PAD, far, 0.0))


def coaddition_call(order, anchor, frac, scale, weight, image, mask, kern, label, consts):
    scalars = (order, anchor, frac, scale, weight)
    arrays = (image, mask, kern, label, jnp.asarray(wanted_labels())) + tuple(consts)
    dma = pltpu.SemaphoreType.DMA
    slab = (2, SLAB, TILE)
    parts = CELLS // GROUP
    return pl.pallas_call(
        coaddition_kernel,
        in_specs=[pl.BlockSpec(memory_space=pltpu.SMEM)] * len(scalars) + [whole(a) for a in arrays],
        out_specs=pl.BlockSpec((TALL, WIDE), lambda: (0, 0)),
        out_shape=jax.ShapeDtypeStruct((TALL, WIDE), F32),
        scratch_shapes=[
            pltpu.VMEM((2, 2, 6, 48, 16, 128), BF16),
            pltpu.VMEM((2, 2 * CELLS) + slab, BF16),
            pltpu.VMEM((2, CELLS) + slab, BF16),
            pltpu.VMEM((2, CELLS) + slab, BF16),
            pltpu.VMEM((2, 2, CELLS, 128), jnp.int32),
            pltpu.VMEM((8, 128), jnp.int32),
            pltpu.SMEM((8, 128), jnp.int32),
            pltpu.VMEM((2, 2, CELLS) + slab, BF16),
            pltpu.VMEM((2, 2, CELLS) + slab, BF16),
            pltpu.VMEM((2, CELLS) + slab, F32),
            pltpu.VMEM((2, TILE, TILE), F32),
            pltpu.VMEM((2, TILE, TILE), F32),
            pltpu.VMEM((2, PAD, SPAN), F32),
            pltpu.VMEM((4, PAD, TILE), F32),
            dma((2, 2, parts)), dma((2, 2, parts)), dma((2, 2)), dma((2, 2)), dma((2, 2, TR)), dma((2, 2, TR)),
            dma((8,)), dma((8,)), dma(()),
        ],
        compiler_params=pltpu.CompilerParams(
            vmem_limit_bytes=56 * 2**20, collective_id=0, has_side_effects=True
        ),
    )(*scalars, *arrays)


LEVEL_ROWS = ((8, 584), (16, 576), (24, 568), (40, 552))
BLOCK = 128


def starlet_kernel(edge_ref, first_ref, details_ref, smooth_ref, ping, pong):
    top, bottom, left, right = (edge_ref[i] for i in range(4))
    tiles = WIDE // 128
    zero = jnp.zeros((8, WIDE), F32)
    for ref in (ping, pong):
        ref[0:8, :] = zero
        ref[TALL - 8 : TALL, :] = zero
    source = first_ref
    for k in range(SCALES):
        s = 2**k
        target = (ping, pong)[k % 2]
        begin, end = LEVEL_ROWS[k]

        def smoothed(view, count, s=s):
            def near(by):
                return view[16 + by : 16 + by + count, :]

            center = near(0)
            rows = (near(-2 * s) + near(2 * s)) + 4.0 * (near(-s) + near(s)) + 6.0 * center
            parts = [rows[:, 128 * j : 128 * (j + 1)] for j in range(tiles)]
            lane = lax.broadcasted_iota(jnp.int32, (count, 128), 1)

            def after(by):
                turned = [pltpu.roll(part, by, 1) for part in parts]
                return [jnp.where(lane < by, turned[j - 1], turned[j]) for j in range(tiles)]

            def before(by):
                turned = [pltpu.roll(part, 128 - by, 1) for part in parts]
                return [jnp.where(lane >= 128 - by, turned[(j + 1) % tiles], turned[j]) for j in range(tiles)]

            a, b, c, d = after(2 * s), before(2 * s), after(s), before(s)
            full = [((a[j] + b[j]) + 4.0 * (c[j] + d[j]) + 6.0 * parts[j]) * (1.0 / 256.0) for j in range(tiles)]
            return center, full

        def store(row, count, full, factor, target=target):
            lane = lax.broadcasted_iota(jnp.int32, (count, 128), 1)
            side = jnp.where(lane < 64, right, left)
            for j in range(tiles):
                value = full[j] * side if j == tiles - 1 else full[j]
                value = value if factor is None else value * factor
                target[pl.ds(row, count), 128 * j : 128 * (j + 1)] = value

        if k < SCALES - 1:
            for row, last, factor in ((begin, TOP, top), (TOP + SPAN, end, bottom)):
                low, high = max(row - 16, 0), min(last + 16, TALL)
                count = last - row
                rows = source[low:high, :]
                if low > row - 16:
                    rows = jnp.concatenate([jnp.zeros((low - row + 16, WIDE), F32), rows], axis=0)
                if high < last + 16:
                    rows = jnp.concatenate([rows, jnp.zeros((last + 16 - high, WIDE), F32)], axis=0)
                store(row, count, smoothed(rows, count)[1], factor)

        def one(block, carry, k=k, source=source, smoothed=smoothed, store=store):
            row = pl.multiple_of(TOP + block * BLOCK, 8)
            here = pl.multiple_of(block * BLOCK, 8)
            center, full = smoothed(source.at[pl.ds(pl.multiple_of(row - 16, 8), BLOCK + 32), :], BLOCK)
            if k < SCALES - 1:
                store(row, BLOCK, full, None)
            for j in range(SPAN // 128):
                cols = slice(128 * j, 128 * (j + 1))
                details_ref[k, pl.ds(here, BLOCK), cols] = center[:, cols] - full[j]
                if k == SCALES - 1:
                    smooth_ref[pl.ds(here, BLOCK), cols] = full[j]
            return carry

        lax.fori_loop(0, SPAN // BLOCK, one, 0)
        source = target


def starlet_call(edges, first):
    return pl.pallas_call(
        starlet_kernel,
        in_specs=[pl.BlockSpec(memory_space=pltpu.SMEM), whole(first)],
        out_specs=[
            pl.BlockSpec((SCALES, SPAN, SPAN), lambda: (0, 0, 0)),
            pl.BlockSpec((SPAN, SPAN), lambda: (0, 0)),
        ],
        out_shape=[
            jax.ShapeDtypeStruct((SCALES, SPAN, SPAN), F32),
            jax.ShapeDtypeStruct((SPAN, SPAN), F32),
        ],
        scratch_shapes=[pltpu.VMEM((TALL, WIDE), F32)] * 2,
        compiler_params=pltpu.CompilerParams(vmem_limit_bytes=48 * 2**20),
    )(edges, first)


def shards(image, mask, weight, anchor, frac, scale, kernels, dest, offset):
    order, label = order_call(dest, offset)
    padded = jnp.pad(kernels[0], ((0, 0), (0, 7), (0, 23)))
    kern = jnp.concatenate([padded, padded], axis=-1)
    first = coaddition_call(
        order, anchor[0].T, frac[0].T, scale[0].T, weight, image, mask, kern, label, constants()
    )
    band, patch = lax.axis_index("band"), lax.axis_index("patch")
    edges = jnp.stack(
        [band > 0, band < lax.axis_size("band") - 1, patch > 0, patch < lax.axis_size("patch") - 1]
    ).astype(F32)
    return tuple(starlet_call(edges, first))


def solution(mesh):
    owner = ("patch", "band")
    in_specs = (
        P(owner, None, None),
        P(owner, None, None),
        P(owner),
        P(owner, None, None),
        P(owner, None, None),
        P(owner, None, None),
        P(owner, None, None, None),
        P(owner, None),
        P(owner, None),
    )
    out_specs = (P(None, "band", "patch"), P("band", "patch"))
    return jax.shard_map(shards, mesh=mesh, in_specs=in_specs, out_specs=out_specs, check_vma=False)
```

```python
import math
import numpy as np
import ml_dtypes
import jax
import jax.numpy as jnp
from jax import lax
from jax.experimental import pallas as pl
from jax.experimental.pallas import tpu as pltpu
from jax.sharding import PartitionSpec as P

TILE, KS, SCALES, TR, TC, MARGIN, WARP_N, SRC_N = 128, 41, 4, 4, 4, 20, 168, 184
ROWS = 176
HALF = 88
WIN = 256
F32, BF16 = jnp.float32, jnp.bfloat16


def split_bf16(values):
    high = values.astype(ml_dtypes.bfloat16)
    low = (values - high.astype(np.float64)).astype(ml_dtypes.bfloat16)
    return high, low


def spectra():
    bins = np.arange(WARP_N // 2 + 1)

    def forward(points, sign):
        angle = 2.0 * np.pi / WARP_N * np.outer(bins, points)
        return np.cos(angle), sign * np.sin(angle)

    order = (np.arange(WARP_N) + MARGIN) % WARP_N
    real, imag = forward(order, -1.0)
    rows = np.zeros((ROWS, WIN))
    rows[: len(bins), :WARP_N] = real
    rows[HALF : HALF + len(bins), :WARP_N] = imag
    cols = np.zeros((WIN, WIN))
    cols[:WARP_N, : len(bins)] = real.T
    cols[:WARP_N, 128 : 128 + len(bins)] = imag.T
    real, imag = forward(np.arange(KS), 1.0)
    kcols = np.zeros((64, WIN))
    kcols[:KS, : len(bins)] = real.T
    kcols[:KS, 128 : 128 + len(bins)] = imag.T
    krows = np.zeros((ROWS, 48))
    krows[: len(bins), :KS] = real
    krows[HALF : HALF + len(bins), :KS] = imag
    count = np.full(len(bins), 2.0)
    count[0] = count[-1] = 1.0
    angle = 2.0 * np.pi / WARP_N * np.outer(np.arange(TILE), bins)
    back_real = np.cos(angle) * count / WARP_N
    back_imag = -np.sin(angle) * count / WARP_N
    icols = np.zeros((WIN, TILE))
    icols[: len(bins)] = back_real.T
    icols[128 : 128 + len(bins)] = back_imag.T
    irows = np.zeros((TILE, ROWS))
    irows[:, : len(bins)] = 0.5 * back_real
    irows[:, HALF : HALF + len(bins)] = 0.5 * back_imag
    kcols_high, kcols_low = split_bf16(kcols)
    krows_high, krows_low = split_bf16(krows)
    icols_high, icols_low = split_bf16(icols)
    irows_high, irows_low = split_bf16(irows)
    rows_pad = rows[:, :ROWS]
    return (
        cols.astype(ml_dtypes.bfloat16),
        rows_pad.astype(ml_dtypes.bfloat16),
        np.concatenate([kcols_high, kcols_low]),
        np.concatenate([krows_high, krows_high, krows_low], axis=1),
        np.concatenate([icols_high, icols_low], axis=1),
        np.concatenate([irows_high, irows_low]),
    )


def phase_constants():
    j = np.arange(WIN)
    sign = 1.0 - 2.0 * (j % 2)
    cosine = (sign * np.cos(np.pi * j / 5.0)).astype(np.float32)
    sine = (sign * np.sin(np.pi * j / 5.0)).astype(np.float32)
    along = np.zeros((8, WIN), np.float32)
    along[0], along[1] = cosine, sine
    down = np.stack([np.repeat(cosine[:, None], 128, 1), np.repeat(sine[:, None], 128, 1)])
    return along, down


def poly(coefficients, x):
    total = jnp.full_like(x, coefficients[-1])
    for value in coefficients[-2::-1]:
        total = total * x + value
    return total


SIN_PI = (3.14159265, -5.16771276, 2.55016332, -0.5992522, 0.0820504, -0.00702839)
SIN_TURN = (6.28318531, -41.34170222, 81.60524742, -76.70580022, 42.05775402, -15.08656526, 3.78131888, -0.62077872)
COS_TURN = (1.0, -19.73920874, 64.93938908, -85.45665831, 60.24213134, -26.40466819, 7.80013144, -1.45311232)


def lanczos(d, cos_row, sin_row, cos_col, sin_col):
    d2 = d * d
    u = cos_row * sin_col - sin_row * cos_col
    g = u / d2
    g = jnp.where(d2 < 1e-5, 1.0, g)
    return jnp.where(d2 < 25.0, g, 0.0).astype(BF16)


def dot(a, b):
    return lax.dot_general(a, b, (((1,), (0,)), ((), ())), preferred_element_type=F32)


def constants():
    along, down = phase_constants()
    return [jnp.asarray(a) for a in (along, down) + spectra()]


CELLS = TR * TC
GROUP = 4
LOADS = 3
SLAB = TILE // 2
SPAN = TR * TILE
PAD = 32
WIDE = SPAN + 128
TOP = 8 + PAD
TALL = SPAN + 2 * TOP
MESH = pl.DeviceIdType.MESH


def within(value, top):
    return jnp.minimum(jnp.maximum(value, 0), top)


def whole(a):
    return pl.BlockSpec(a.shape, lambda *_: (0,) * a.ndim)


def wanted_labels():
    lanes = np.arange(128)
    rows = np.full((8, 128), -1, np.int32)
    for source, step in enumerate((1, 2, 0)):
        rows[source] = (3 * (lanes // CELLS) + step) * CELLS + lanes % CELLS + 1
        rows[3 + source] = (3 * step + lanes // CELLS) * CELLS + lanes % CELLS + 1
    return np.where(lanes < 3 * CELLS, rows, -1).astype(np.int32)


def coaddition_kernel(
    dest_ref, offset_ref, anchor_ref, frac_ref, scale_ref, weight_ref,
    image_ref, mask_ref, kern_ref, wanted_ref,
    along_ref, down_ref, cols_ref, rows_ref, kcols_ref, krows_ref, icols_ref, irows_ref,
    out_ref,
    image, mask, label_ref, order, order_smem, planes, tiles, upper_in, lower_in, label_in, table, table_smem, send, recv, total, edge_send, edge_recv, rim_recv, corner_recv,
    early_send_sem, early_recv_sem, label_send_sem, label_recv_sem, late_send_sem, late_recv_sem,
    edge_send_sem, edge_recv_sem, rim_send_sem, rim_recv_sem, local_sem, load_sem,
):
    loads = []
    for number in range(LOADS):
        rows = pl.ds(number * (768 // LOADS), 768 // LOADS)
        for kind, (source, target) in enumerate(((image_ref, image), (mask_ref, mask))):
            loads.append(pltpu.make_async_copy(source.at[0, rows], target.at[rows], load_sem.at[kind, number]))
    for load in loads:
        load.start()

    patch, band = lax.axis_index("patch"), lax.axis_index("band")
    n_patch, n_band = lax.axis_size("patch"), lax.axis_size("band")
    left_patch, right_patch = lax.rem(patch + n_patch - 1, n_patch), lax.rem(patch + 1, n_patch)
    above_band, below_band = lax.rem(band + n_band - 1, n_band), lax.rem(band + 1, n_band)
    left, right = {"patch": left_patch, "band": band}, {"patch": right_patch, "band": band}
    above, below = {"patch": patch, "band": above_band}, {"patch": patch, "band": below_band}
    corners = [{"patch": p, "band": b} for b in (above_band, below_band) for p in (left_patch, right_patch)]
    has_left = jnp.where(patch > 0, 1.0, 0.0)
    has_right = jnp.where(patch < n_patch - 1, 1.0, 0.0)
    has_above = jnp.where(band > 0, 1.0, 0.0)
    has_below = jnp.where(band < n_band - 1, 1.0, 0.0)

    barrier = pltpu.get_barrier_semaphore()
    around = [left, right, above, below] + corners
    for device in around:
        pl.semaphore_signal(barrier, inc=1, device_id=device, device_id_type=MESH)

    def remote(src, dst, send_sem, recv_sem, device):
        return pltpu.make_async_remote_copy(
            src_ref=src, dst_ref=dst, send_sem=send_sem, recv_sem=recv_sem, device_id=device, device_id_type=MESH
        )

    beside = (upper_in, lower_in)

    early_to = ((right, left), (below, above))
    late_to = ((above, below), (left, right))

    def label_copy(half, way):
        return remote(
            label_ref,
            label_in.at[half, way],
            label_send_sem.at[half, way],
            label_recv_sem.at[half, way],
            early_to[half][way],
        )

    def early_copy(half, way, part):
        piece = pl.ds(part * GROUP, GROUP)
        return remote(
            tiles.at[half, piece],
            beside[half].at[way, piece],
            early_send_sem.at[half, way, part],
            early_recv_sem.at[half, way, part],
            early_to[half][way],
        )

    def late_copy(half, way, part):
        piece = pl.ds(part * TC, TC)
        return remote(
            send.at[half, way, piece],
            recv.at[half, way, piece],
            late_send_sem.at[half, way, part],
            late_recv_sem.at[half, way, part],
            late_to[half][way],
        )

    first_rows, last_rows = pl.ds(TOP, PAD), pl.ds(TOP + SPAN - PAD, PAD)

    def edge_copy(way, part):
        return remote(
            edge_send.at[way, part],
            edge_recv.at[way, part],
            edge_send_sem.at[way, part],
            edge_recv_sem.at[way, part],
            early_to[0][way],
        )

    def rim_copies(way):
        rows = (first_rows, last_rows)[way]
        triples = [(pl.ds(0, SPAN), rim_recv.at[way], late_to[0][way])]
        for side in range(2):
            cols = pl.ds(0, TILE) if side == 0 else pl.ds(SPAN - TILE, TILE)
            triples.append((cols, corner_recv.at[2 * way + side], corners[2 * way + side]))
        return [
            remote(out_ref.at[rows, cols], target, rim_send_sem.at[way, number], rim_recv_sem.at[way, number], device)
            for number, (cols, target, device) in enumerate(triples)
        ]

    filled = jnp.int32(0)
    lane = lax.broadcasted_iota(jnp.int32, (8, 128), 1)
    sub = lax.broadcasted_iota(jnp.int32, (CELLS, 128), 0)
    sequence = jnp.zeros((8, 128), jnp.int32)
    labels = jnp.zeros((CELLS, 128), jnp.int32)
    for i in range(2 * CELLS):
        code, cell = dest_ref[0, i], offset_ref[0, i]
        away = code != 4
        slot = jnp.where(away, filled, CELLS + cell)
        sequence = jnp.where(lane == slot, i, sequence)
        labels = jnp.where(sub == slot, code * CELLS + cell + 1, labels)
        filled = filled + away.astype(jnp.int32)
    order[...] = sequence
    label_ref[...] = labels
    order_copy = pltpu.make_async_copy(order, order_smem, local_sem)
    order_copy.start()

    def prepare(block, carry):
        rows = pl.ds(pl.multiple_of(block * 64, 64), 64)
        usable = jnp.where((mask[rows, :] & 7) != 7, 1.0, 0.0).astype(BF16)
        masked = image[rows, :] * usable
        for plane, value in enumerate((masked, usable)):
            moved = jnp.concatenate([value[:, 64:], value[:, :64]], axis=1)
            for way, data in enumerate((value, moved)):
                for j in range(6):
                    for i in range(4):
                        planes[way, plane, j, block * 4 + i] = data[16 * i : 16 * i + 16, 128 * j : 128 * j + 128]
        return carry

    steps = 768 // 64 // LOADS
    for number in range(LOADS):
        for load in loads[2 * number : 2 * number + 2]:
            load.wait()
        lax.fori_loop(number * steps, (number + 1) * steps, prepare, 0)
    order_copy.wait()

    lane = lax.broadcasted_iota(jnp.int32, (ROWS, WIN), 1)
    sub = lax.broadcasted_iota(jnp.int32, (WIN, WIN), 0)
    short = lax.broadcasted_iota(jnp.int32, (8, WIN), 1)
    quantity = lax.broadcasted_iota(jnp.int32, (8, WIN), 0)
    index = (short + jnp.where(short < WARP_N - MARGIN, MARGIN, MARGIN - WARP_N)).astype(F32)

    def warp_rows(fraction, stretch, shift):
        position = (5.0 + fraction) + index * (1.0 + stretch)
        nearest = jnp.floor(position + 0.5)
        odd = nearest - 2.0 * jnp.floor(nearest * 0.5)
        part = position - nearest
        sine = (1.0 - 2.0 * odd) * part * poly(SIN_PI, part * part)
        sign = (1 - 2 * (shift & 1)).astype(F32)
        amplitude = ((-5.0 / math.pi**2) * sign) * sine
        turn = position - 10.0 * jnp.floor(position * 0.1) + lax.rem(shift, 10).astype(F32)
        turn = turn * 0.1
        turn = turn - jnp.floor(turn + 0.5)
        square = turn * turn
        cosine, sine = poly(COS_TURN, square), turn * poly(SIN_TURN, square)
        position = jnp.where(short < WARP_N, position, 1e4)
        return jnp.where(quantity == 0, position, jnp.where(quantity == 1, amplitude * cosine, amplitude * sine))

    weight = weight_ref[0]
    each = range(GROUP)

    def store_tile(slot, plane, value):
        for half in range(2):
            tiles[half, slot, plane] = value[half * SLAB : (half + 1) * SLAB].astype(BF16)

    def gather(half, position):
        value = None
        for source in range(3):
            slot = table_smem[3 * half + source, position]
            present = jnp.where(slot >= 0, 1.0, 0.0)
            at = within(slot, CELLS - 1)
            data = tiles[half, at] if source == 0 else beside[half][source - 1, at]
            term = data.astype(F32) * present
            value = term if value is None else value + term
        return value

    def find_slots():
        for half in range(2):
            for way in range(2):
                label_copy(half, way).wait()
            for source in range(3):
                lookup = label_ref[...] if source == 0 else label_in[half, source - 1]
                number = 3 * half + source
                found = jnp.zeros((1, 128), jnp.int32)
                for slot in range(CELLS):
                    same = lookup[slot : slot + 1] == wanted_ref[number : number + 1, :]
                    found = found + jnp.where(same, slot + 1, 0)
                table[number : number + 1, :] = found - 1
        to_smem = pltpu.make_async_copy(table, table_smem, local_sem)
        to_smem.start()
        to_smem.wait()

    def pass_on(half):
        for part in range(CELLS // GROUP):
            for way in range(2):
                early_copy(half, way, part).wait()

        def outgoing(part, carry):
            for way in range(2):
                for c in range(TC):
                    cell = part * TC + c
                    send[half, way, cell] = gather(half, 2 * CELLS * way + cell).astype(BF16)
                late_copy(half, way, part).start()
            return carry

        lax.fori_loop(0, TR, outgoing, 0)

    def work(step, carry):
        chosen = [within(order_smem[0, step * GROUP + g], 2 * CELLS - 1) for g in each]
        half_img, half_cov, lt = [], [], []
        for g in each:
            t = chosen[g]
            first_row, first_col = anchor_ref[0, t], anchor_ref[1, t]
            row16 = within(first_row // 16, (768 - WIN) // 16)
            col64 = within(first_col // 64, (768 - WIN) // 64)
            off_r = first_row - row16 * 16
            off_c = first_col - col64 * 64
            par = within(col64 % 2, 1)
            pair = within(col64 // 2, 4)
            s_img, s_cov = (
                jnp.concatenate(
                    [
                        jnp.concatenate([planes[par, plane, pair + j, row16 + i] for i in range(16)], axis=0)
                        for j in range(2)
                    ],
                    axis=1,
                )
                for plane in range(2)
            )
            q0 = jnp.transpose(warp_rows(frac_ref[0, t], scale_ref[0, t], off_r))[:ROWS]
            d0 = (lane - off_r).astype(F32) - q0[:, 0:1]
            l0 = lanczos(d0, q0[:, 1:2], q0[:, 2:3], along_ref[0:1, :], along_ref[1:2, :])
            q1 = warp_rows(frac_ref[1, t], scale_ref[1, t], off_c)
            d1 = (sub - off_c).astype(F32) - q1[0:1, :]
            cosd = jnp.concatenate([down_ref[0], down_ref[0]], axis=1)
            sind = jnp.concatenate([down_ref[1], down_ref[1]], axis=1)
            lt.append(lanczos(d1, q1[1:2, :], q1[2:3, :], cosd, sind))
            half_img.append(dot(l0, s_img).astype(BF16))
            half_cov.append(dot(l0[:TILE], s_cov).astype(BF16))
        warped = [dot(half_img[g], lt[g]).astype(BF16) for g in each]
        for g in each:
            coverage = dot(half_cov[g], lt[g][:, :TILE])
            store_tile(step * GROUP + g, 1, weight * coverage)
        x1 = dot(jnp.concatenate(warped, axis=0), cols_ref[...]).astype(BF16)
        x2 = [dot(rows_ref[...], x1[g * ROWS : (g + 1) * ROWS]) for g in each]
        taps = []
        for g in each:
            tap = jnp.concatenate([kern_ref[chosen[g]].astype(F32), jnp.zeros((48 - KS, KS), F32)], axis=0)
            gap = jnp.zeros((48, 64 - KS), F32)
            taps.append(jnp.concatenate([tap, gap, tap, gap], axis=1).astype(BF16))
        k1 = dot(jnp.concatenate(taps, axis=0), kcols_ref[...])
        k1h = k1.astype(BF16)
        k1l = (k1 - k1h.astype(F32)).astype(BF16)
        z = []
        for g in each:
            h, l = k1h[g * 48 : g * 48 + 48], k1l[g * 48 : g * 48 + 48]
            k2 = dot(krows_ref[...], jnp.concatenate([h, l, h], axis=0))
            x = x2[g]
            xrr, xri, xir, xii = x[:HALF, :128], x[:HALF, 128:], x[HALF:, :128], x[HALF:, 128:]
            krr, kri, kir, kii = k2[:HALF, :128], k2[:HALF, 128:], k2[HALF:, :128], k2[HALF:, 128:]
            xpr, xpi, xmr, xmi = xrr - xii, xir + xri, xrr + xii, xir - xri
            kpr, kpi, kmr, kmi = krr - kii, kir + kri, krr + kii, kir - kri
            ppr, ppi = xpr * kpr - xpi * kpi, xpr * kpi + xpi * kpr
            pmr, pmi = xmr * kmr - xmi * kmi, xmr * kmi + xmi * kmr
            top = jnp.concatenate([ppr + pmr, ppi - pmi], axis=1)
            bottom = jnp.concatenate([ppi + pmi, pmr - ppr], axis=1)
            z.append(jnp.concatenate([top, bottom], axis=0).astype(BF16))
        y = dot(jnp.concatenate(z, axis=0), icols_ref[...])
        y = y[:, :TILE] + y[:, TILE:]
        yh = y.astype(BF16)
        yl = (y - yh.astype(F32)).astype(BF16)
        ycat = jnp.concatenate([yh, yl], axis=1)
        for g in each:
            o = dot(irows_ref[...], ycat[g * ROWS : (g + 1) * ROWS])
            matched = o[:TILE, :TILE] + (o[:TILE, TILE:] + o[TILE:, :TILE])
            store_tile(step * GROUP + g, 0, weight * matched)

        @pl.when(step == 0)
        def _():
            pl.semaphore_wait(barrier, len(around))
            for half in range(2):
                for way in range(2):
                    label_copy(half, way).start()

        @pl.when(step < CELLS // GROUP)
        def _():
            for half in range(2):
                for way in range(2):
                    early_copy(half, way, step).start()

        @pl.when(step == 4)
        def _():
            find_slots()
            pass_on(1)

        @pl.when(step == 6)
        def _():
            pass_on(0)

        return carry

    lax.fori_loop(0, 2 * CELLS // GROUP, work, 0)

    def staying(cell, carry):
        for half in range(2):
            total[half, cell] = gather(half, CELLS + cell) + tiles[half, CELLS + cell].astype(F32)
        return carry

    lax.fori_loop(0, CELLS, staying, 0)

    lane = lax.broadcasted_iota(jnp.int32, (PAD, TILE), 1)

    def finish(part, carry):
        for half in range(2):
            for way in range(2):
                late_copy(half, way, part).wait()
            rows = pl.ds(pl.multiple_of(TOP + part * TILE + half * SLAB, 8), SLAB)
            for c in range(TC):
                cell = part * TC + c
                value = total[half, cell] + (recv[half, 0, cell].astype(F32) + recv[half, 1, cell].astype(F32))
                out_ref[rows, c * TILE : (c + 1) * TILE] = value[0] / (jnp.maximum(value[1], 0.0) + 1.0)

        @pl.when(part == 0)
        def _():
            for copy in rim_copies(0):
                copy.start()

        @pl.when(part == TR - 1)
        def _():
            for copy in rim_copies(1):
                copy.start()

        for way in range(2):
            cols = slice(SPAN - TILE, SPAN) if way == 0 else slice(0, TILE)
            packed = jnp.zeros((PAD, TILE), F32)
            for q in range(4):
                end = out_ref[pl.ds(pl.multiple_of(TOP + part * TILE + q * PAD, 8), PAD), cols]
                turn = (PAD * q + (PAD if way == 0 else 0)) % TILE
                moved = end if turn == 0 else pltpu.roll(end, turn, 1)
                packed = jnp.where((lane >= PAD * q) & (lane < PAD * (q + 1)), moved, packed)
            edge_send[way, part] = packed
            edge_copy(way, part).start()
        return carry

    lax.fori_loop(0, TR, finish, 0)

    blank = jnp.zeros((8, WIDE), F32)
    out_ref[0:8, :] = blank
    out_ref[TALL - 8 : TALL, :] = blank

    def unpack(part, carry):
        for way in range(2):
            edge_copy(way, part).wait()
        from_left, from_right = edge_recv[0, part] * has_left, edge_recv[1, part] * has_right
        for q in range(4):
            turn = (TILE - PAD * q) % TILE
            near = from_right if turn == 0 else pltpu.roll(from_right, turn, 1)
            turn = (TILE - PAD - PAD * q) % TILE
            far = from_left if turn == 0 else pltpu.roll(from_left, turn, 1)
            rows = pl.ds(pl.multiple_of(TOP + part * TILE + q * PAD, 8), PAD)
            out_ref[rows, SPAN:] = jnp.where(lane < PAD, near, jnp.where(lane >= TILE - PAD, far, 0.0))
        return carry

    lax.fori_loop(0, TR, unpack, 0)
    for way in range(2):
        for copy in rim_copies(way):
            copy.wait()
    for rows, arrived, far, near, factor in (
        (slice(8, TOP), 1, 3, 2, has_above),
        (slice(TOP + SPAN, TALL - 8), 0, 1, 0, has_below),
    ):
        out_ref[rows, :SPAN] = rim_recv[arrived] * factor
        near, far = corner_recv[near] * (has_right * factor), corner_recv[far] * (has_left * factor)
        out_ref[rows, SPAN:] = jnp.where(lane < PAD, near, jnp.where(lane >= TILE - PAD, far, 0.0))


def coaddition_call(dest, offset, anchor, frac, scale, weight, image, mask, kern, consts):
    scalars = (dest, offset, anchor, frac, scale, weight)
    arrays = (kern, jnp.asarray(wanted_labels())) + tuple(consts)
    dma = pltpu.SemaphoreType.DMA
    slab = (2, SLAB, TILE)
    parts = CELLS // GROUP
    return pl.pallas_call(
        coaddition_kernel,
        in_specs=[pl.BlockSpec(memory_space=pltpu.SMEM)] * len(scalars)
        + [pl.BlockSpec(memory_space=pl.ANY)] * 2
        + [whole(a) for a in arrays],
        out_specs=pl.BlockSpec(memory_space=pltpu.VMEM),
        out_shape=pltpu.VMEM((TALL, WIDE), F32),
        scratch_shapes=[
            pltpu.VMEM((768, 768), BF16),
            pltpu.VMEM((768, 768), jnp.int32),
            pltpu.VMEM((CELLS, 128), jnp.int32),
            pltpu.VMEM((8, 128), jnp.int32),
            pltpu.SMEM((8, 128), jnp.int32),
            pltpu.VMEM((2, 2, 6, 48, 16, 128), BF16),
            pltpu.VMEM((2, 2 * CELLS) + slab, BF16),
            pltpu.VMEM((2, CELLS) + slab, BF16),
            pltpu.VMEM((2, CELLS) + slab, BF16),
            pltpu.VMEM((2, 2, CELLS, 128), jnp.int32),
            pltpu.VMEM((8, 128), jnp.int32),
            pltpu.SMEM((8, 128), jnp.int32),
            pltpu.VMEM((2, 2, CELLS) + slab, BF16),
            pltpu.VMEM((2, 2, CELLS) + slab, BF16),
            pltpu.VMEM((2, CELLS) + slab, F32),
            pltpu.VMEM((2, TR, PAD, TILE), F32),
            pltpu.VMEM((2, TR, PAD, TILE), F32),
            pltpu.VMEM((2, PAD, SPAN), F32),
            pltpu.VMEM((4, PAD, TILE), F32),
            dma((2, 2, parts)), dma((2, 2, parts)), dma((2, 2)), dma((2, 2)), dma((2, 2, TR)), dma((2, 2, TR)),
            dma((2, TR)), dma((2, TR)), dma((2, 3)), dma((2, 3)), dma(()), dma((2, LOADS)),
        ],
        compiler_params=pltpu.CompilerParams(
            vmem_limit_bytes=56 * 2**20, collective_id=0, has_side_effects=True
        ),
    )(*scalars, image, mask, *arrays)


LEVEL_ROWS = ((8, 584), (16, 576), (24, 568), (40, 552))
BLOCK = 256
WAVE = 192


def starlet_kernel(edge_ref, first_ref, details_ref, smooth_ref, ping, pong, band, done, sem):
    top, bottom, left, right = (edge_ref[i] for i in range(4))
    tiles = WIDE // 128
    zero = jnp.zeros((8, WIDE), F32)
    for ref in (ping, pong):
        ref[0:8, :] = zero
        ref[TALL - 8 : TALL, :] = zero
    offset = lax.broadcasted_iota(jnp.int32, (512, 256), 0) - lax.broadcasted_iota(jnp.int32, (512, 256), 1) - 128
    offset = jnp.abs(offset)
    for k in range(SCALES):
        s = 2**k
        tap = jnp.where(offset == 0, 6.0, jnp.where(offset == s, 4.0, jnp.where(offset == 2 * s, 1.0, 0.0)))
        band[k] = (tap * (1.0 / 16.0)).astype(BF16)

    source = first_ref
    copies = []
    for k in range(SCALES):
        s = 2**k
        target = (ping, pong)[k % 2]
        begin, end = LEVEL_ROWS[k]

        def down(view, count, at=16, s=s):
            def near(by):
                return view[at + by : at + by + count, :]

            center = near(0)
            return center, (near(-2 * s) + near(2 * s)) + 4.0 * (near(-s) + near(s)) + 6.0 * center

        def across(rows, s=s):
            count = rows.shape[0]
            parts = [rows[:, 128 * j : 128 * (j + 1)] for j in range(tiles)]
            lane = lax.broadcasted_iota(jnp.int32, (count, 128), 1)

            def after(by):
                turned = [pltpu.roll(part, by, 1) for part in parts]
                return [jnp.where(lane < by, turned[j - 1], turned[j]) for j in range(tiles)]

            def before(by):
                turned = [pltpu.roll(part, 128 - by, 1) for part in parts]
                return [jnp.where(lane >= 128 - by, turned[(j + 1) % tiles], turned[j]) for j in range(tiles)]

            a, b, c, d = after(2 * s), before(2 * s), after(s), before(s)
            return [((a[j] + b[j]) + 4.0 * (c[j] + d[j]) + 6.0 * parts[j]) * (1.0 / 256.0) for j in range(tiles)]

        def across_product(rows, k=k):
            rows = rows * (1.0 / 16.0)
            high = rows.astype(BF16)
            low = (rows - high.astype(F32)).astype(BF16)
            full = []
            for first, count in ((0, 2), (2, 2), (4, 1)):
                total = None
                for part in (high, low):
                    pieces = [part[:, 128 * (j % tiles) : 128 * (j % tiles) + 128] for j in range(first - 1, first + count + 1)]
                    weights = band[k] if count == 2 else band[k, :384, :128]
                    term = lax.dot_general(
                        jnp.concatenate(pieces, axis=1), weights, (((1,), (0,)), ((), ())), preferred_element_type=F32
                    )
                    total = term if total is None else total + term
                full += [total[:, 128 * j : 128 * j + 128] for j in range(count)]
            return full

        def store(row, full, factor, target=target):
            count = full[0].shape[0]
            lane = lax.broadcasted_iota(jnp.int32, (count, 128), 1)
            side = jnp.where(lane < 64, right, left)
            for j in range(tiles):
                value = full[j] * side if j == tiles - 1 else full[j]
                value = value if factor is None else value * factor
                target[pl.ds(row, count), 128 * j : 128 * (j + 1)] = value

        if k < SCALES - 1:
            for row, last, factor in ((begin, TOP, top), (TOP + SPAN, end, bottom)):
                low, high = max(row - 16, 0), min(last + 16, TALL)
                count = last - row
                rows = source[low:high, :]
                if low > row - 16:
                    rows = jnp.concatenate([jnp.zeros((low - row + 16, WIDE), F32), rows], axis=0)
                if high < last + 16:
                    rows = jnp.concatenate([rows, jnp.zeros((last + 16 - high, WIDE), F32)], axis=0)
                store(row, across(down(rows, count)[1]), factor)

        def one(block, carry, k=k, source=source, down=down, across=across, store=store, across_product=across_product):
            row = pl.multiple_of(TOP + block * BLOCK, 8)
            here = pl.multiple_of(block * BLOCK, 8)
            view = source.at[pl.ds(pl.multiple_of(row - 16, 8), BLOCK + 32), :]
            spans = [(0, BLOCK - WAVE, across), (BLOCK - WAVE, WAVE, across_product)]
            for start, count, method in spans:
                center, rows = down(view, count, 16 + start)
                full = method(rows)
                if k < SCALES - 1:
                    store(pl.multiple_of(row + start, 8), full, None)
                at = pl.ds(pl.multiple_of(here + start, 8), count)
                for j in range(SPAN // 128):
                    cols = slice(128 * j, 128 * (j + 1))
                    done[k, at, cols] = center[:, cols] - full[j]
                    if k == SCALES - 1:
                        done[SCALES, at, cols] = full[j]
            return carry

        half = SPAN // BLOCK // 2
        for number in range(2):
            lax.fori_loop(number * half, (number + 1) * half, one, 0)
            rows = pl.ds(number * SPAN // 2, SPAN // 2)
            copies.append(pltpu.make_async_copy(done.at[k, rows], details_ref.at[k, rows], sem.at[2 * k + number]))
            if k == SCALES - 1:
                copies.append(pltpu.make_async_copy(done.at[SCALES, rows], smooth_ref.at[rows], sem.at[2 * SCALES + number]))
                copies[-1].start()
                copies[-2].start()
            else:
                copies[-1].start()
        source = target
    for copy in copies:
        copy.wait()


def starlet_call(edges, first):
    return pl.pallas_call(
        starlet_kernel,
        in_specs=[pl.BlockSpec(memory_space=pltpu.SMEM), pl.BlockSpec(memory_space=pltpu.VMEM)],
        out_specs=[pl.BlockSpec(memory_space=pltpu.HBM)] * 2,
        out_shape=[
            jax.ShapeDtypeStruct((SCALES, SPAN, SPAN), F32),
            jax.ShapeDtypeStruct((SPAN, SPAN), F32),
        ],
        scratch_shapes=[
            pltpu.VMEM((TALL, WIDE), F32),
            pltpu.VMEM((TALL, WIDE), F32),
            pltpu.VMEM((SCALES, 512, 256), BF16),
            pltpu.VMEM((SCALES + 1, SPAN, SPAN), F32),
            pltpu.SemaphoreType.DMA((2 * SCALES + 2,)),
        ],
        compiler_params=pltpu.CompilerParams(vmem_limit_bytes=40 * 2**20),
    )(edges, first)


def shards(image, mask, weight, anchor, frac, scale, kernels, dest, offset):
    first = coaddition_call(
        dest, offset, anchor[0].T, frac[0].T, scale[0].T, weight, image, mask, kernels[0], constants()
    )
    band, patch = lax.axis_index("band"), lax.axis_index("patch")
    edges = jnp.stack(
        [band > 0, band < lax.axis_size("band") - 1, patch > 0, patch < lax.axis_size("patch") - 1]
    ).astype(F32)
    return tuple(starlet_call(edges, first))


def solution(mesh):
    owner = ("patch", "band")
    in_specs = (
        P(owner, None, None),
        P(owner, None, None),
        P(owner),
        P(owner, None, None),
        P(owner, None, None),
        P(owner, None, None),
        P(owner, None, None, None),
        P(owner, None),
        P(owner, None),
    )
    out_specs = (P(None, "band", "patch"), P("band", "patch"))
    return jax.shard_map(shards, mesh=mesh, in_specs=in_specs, out_specs=out_specs, check_vma=False)
```

```python
import math
import numpy as np
import ml_dtypes
import jax
import jax.numpy as jnp
from jax import lax
from jax.experimental import pallas as pl
from jax.experimental.pallas import tpu as pltpu
from jax.sharding import PartitionSpec as P

TILE, KS, SCALES, TR, TC, MARGIN, WARP_N, SRC_N = 128, 41, 4, 4, 4, 20, 168, 184
ROWS = 176
HALF = 88
WIN = 256
F32, BF16 = jnp.float32, jnp.bfloat16


def split_bf16(values):
    high = values.astype(ml_dtypes.bfloat16)
    low = (values - high.astype(np.float64)).astype(ml_dtypes.bfloat16)
    return high, low


def spectra():
    bins = np.arange(WARP_N // 2 + 1)

    def forward(points, sign):
        angle = 2.0 * np.pi / WARP_N * np.outer(bins, points)
        return np.cos(angle), sign * np.sin(angle)

    order = (np.arange(WARP_N) + MARGIN) % WARP_N
    real, imag = forward(order, -1.0)
    rows = np.zeros((ROWS, WIN))
    rows[: len(bins), :WARP_N] = real
    rows[HALF : HALF + len(bins), :WARP_N] = imag
    cols = np.zeros((WIN, WIN))
    cols[:WARP_N, : len(bins)] = real.T
    cols[:WARP_N, 128 : 128 + len(bins)] = imag.T
    real, imag = forward(np.arange(KS), 1.0)
    kcols = np.zeros((64, WIN))
    kcols[:KS, : len(bins)] = real.T
    kcols[:KS, 128 : 128 + len(bins)] = imag.T
    krows = np.zeros((ROWS, 48))
    krows[: len(bins), :KS] = real
    krows[HALF : HALF + len(bins), :KS] = imag
    count = np.full(len(bins), 2.0)
    count[0] = count[-1] = 1.0
    angle = 2.0 * np.pi / WARP_N * np.outer(np.arange(TILE), bins)
    back_real = np.cos(angle) * count / WARP_N
    back_imag = -np.sin(angle) * count / WARP_N
    icols = np.zeros((WIN, TILE))
    icols[: len(bins)] = back_real.T
    icols[128 : 128 + len(bins)] = back_imag.T
    irows = np.zeros((TILE, ROWS))
    irows[:, : len(bins)] = 0.5 * back_real
    irows[:, HALF : HALF + len(bins)] = 0.5 * back_imag
    kcols_high, kcols_low = split_bf16(kcols)
    krows_high, krows_low = split_bf16(krows)
    icols_high, icols_low = split_bf16(icols)
    irows_high, irows_low = split_bf16(irows)
    rows_pad = rows[:, :ROWS]
    return (
        cols.astype(ml_dtypes.bfloat16),
        rows_pad.astype(ml_dtypes.bfloat16),
        np.concatenate([kcols_high, kcols_low]),
        np.concatenate([krows_high, krows_high, krows_low], axis=1),
        np.concatenate([icols_high, icols_low], axis=1),
        np.concatenate([irows_high, irows_low]),
    )


def phase_constants():
    j = np.arange(WIN)
    sign = 1.0 - 2.0 * (j % 2)
    cosine = (sign * np.cos(np.pi * j / 5.0)).astype(np.float32)
    sine = (sign * np.sin(np.pi * j / 5.0)).astype(np.float32)
    along = np.zeros((8, WIN), np.float32)
    along[0], along[1] = cosine, sine
    down = np.stack([np.repeat(cosine[:, None], 128, 1), np.repeat(sine[:, None], 128, 1)])
    return along, down


def poly(coefficients, x):
    total = jnp.full_like(x, coefficients[-1])
    for value in coefficients[-2::-1]:
        total = total * x + value
    return total


SIN_PI = (3.14159265, -5.16771276, 2.55016332, -0.5992522, 0.0820504, -0.00702839)
SIN_TURN = (6.28318531, -41.34170222, 81.60524742, -76.70580022, 42.05775402, -15.08656526, 3.78131888, -0.62077872)
COS_TURN = (1.0, -19.73920874, 64.93938908, -85.45665831, 60.24213134, -26.40466819, 7.80013144, -1.45311232)


def lanczos(d, cos_row, sin_row, cos_col, sin_col):
    d2 = d * d
    u = cos_row * sin_col - sin_row * cos_col
    g = u / d2
    g = jnp.where(d2 < 1e-5, 1.0, g)
    return jnp.where(d2 < 25.0, g, 0.0).astype(BF16)


def dot(a, b):
    return lax.dot_general(a, b, (((1,), (0,)), ((), ())), preferred_element_type=F32)


def constants():
    along, down = phase_constants()
    return [jnp.asarray(a) for a in (along, down) + spectra()]


CELLS = TR * TC
GROUP = 4
LOADS = 3
SLAB = TILE // 2
SPAN = TR * TILE
PAD = 32
WIDE = SPAN + 128
TOP = 8 + PAD
TALL = SPAN + 2 * TOP
MESH = pl.DeviceIdType.MESH


def within(value, top):
    return jnp.minimum(jnp.maximum(value, 0), top)


def whole(a):
    return pl.BlockSpec(a.shape, lambda *_: (0,) * a.ndim)


PLACES = (0, 1, 2, 3, 12, 13, 14, 15, 4, 7, 8, 11, 5, 6, 9, 10)


def wanted_labels():
    lanes = np.arange(128)
    cell = np.asarray(PLACES)[lanes % CELLS]
    rows = np.full((8, 128), -1, np.int32)
    for source, step in enumerate((1, 2, 0)):
        rows[source] = (3 * (lanes // CELLS) + step) * CELLS + cell + 1
        rows[3 + source] = (3 * step + lanes // CELLS) * CELLS + cell + 1
    rows = np.where(lanes < 3 * CELLS, rows, -1).astype(np.int32)
    rows[6] = np.where(lanes < CELLS, lanes, np.where(lanes < 2 * CELLS, 64 + cell, -1))
    return rows


def coaddition_kernel(
    dest_ref, offset_ref, anchor_ref, frac_ref, scale_ref, weight_ref,
    image_hbm, mask_hbm, psf_hbm, wanted_hbm,
    along_hbm, down_hbm, cols_hbm, rows_hbm, kcols_hbm, krows_hbm, icols_hbm, irows_hbm,
    out_ref,
    wanted_ref, along_ref, down_ref, cols_ref, rows_ref, kcols_ref, krows_ref, icols_ref, irows_ref,
    image, mask, psf, taps_wide, kern_ref, label_ref, order, order_smem, planes, tiles, upper_in, lower_in, label_in, table, table_smem, send, recv, total, edge_send, edge_recv, rim_recv, corner_recv,
    early_send_sem, early_recv_sem, label_send_sem, label_recv_sem, late_send_sem, late_recv_sem,
    edge_send_sem, edge_recv_sem, rim_send_sem, rim_recv_sem, local_sem, load_sem, psf_sem, constant_sem,
):
    psf_copy = pltpu.make_async_copy(psf_hbm, psf, psf_sem)
    constant_copies = [
        pltpu.make_async_copy(source, target, constant_sem.at[number])
        for number, (source, target) in enumerate(
            (
                (wanted_hbm, wanted_ref),
                (along_hbm, along_ref),
                (down_hbm, down_ref),
                (cols_hbm, cols_ref),
                (rows_hbm, rows_ref),
                (kcols_hbm, kcols_ref),
                (krows_hbm, krows_ref),
                (icols_hbm, icols_ref),
                (irows_hbm, irows_ref),
            )
        )
    ]
    constant_copies[0].start()
    psf_copy.start()
    loads = []
    for number in range(LOADS):
        rows = pl.ds(number * (768 // LOADS), 768 // LOADS)
        for kind, (source, target) in enumerate(((image_hbm, image), (mask_hbm, mask))):
            loads.append(pltpu.make_async_copy(source.at[0, rows], target.at[rows], load_sem.at[kind, number]))
    for load in loads:
        load.start()
    for copy in constant_copies[1:]:
        copy.start()

    patch, band = lax.axis_index("patch"), lax.axis_index("band")
    n_patch, n_band = lax.axis_size("patch"), lax.axis_size("band")
    left_patch, right_patch = lax.rem(patch + n_patch - 1, n_patch), lax.rem(patch + 1, n_patch)
    above_band, below_band = lax.rem(band + n_band - 1, n_band), lax.rem(band + 1, n_band)
    left, right = {"patch": left_patch, "band": band}, {"patch": right_patch, "band": band}
    above, below = {"patch": patch, "band": above_band}, {"patch": patch, "band": below_band}
    corners = [{"patch": p, "band": b} for b in (above_band, below_band) for p in (left_patch, right_patch)]
    has_left = jnp.where(patch > 0, 1.0, 0.0)
    has_right = jnp.where(patch < n_patch - 1, 1.0, 0.0)
    has_above = jnp.where(band > 0, 1.0, 0.0)
    has_below = jnp.where(band < n_band - 1, 1.0, 0.0)

    barrier = pltpu.get_barrier_semaphore()
    around = [left, right, above, below] + corners
    for device in around:
        pl.semaphore_signal(barrier, inc=1, device_id=device, device_id_type=MESH)

    def remote(src, dst, send_sem, recv_sem, device):
        return pltpu.make_async_remote_copy(
            src_ref=src, dst_ref=dst, send_sem=send_sem, recv_sem=recv_sem, device_id=device, device_id_type=MESH
        )

    beside = (upper_in, lower_in)

    early_to = ((right, left), (below, above))
    late_to = ((above, below), (left, right))

    def label_copy(half, way):
        return remote(
            label_ref,
            label_in.at[half, way],
            label_send_sem.at[half, way],
            label_recv_sem.at[half, way],
            early_to[half][way],
        )

    def early_copy(half, way, part):
        piece = pl.ds(part * GROUP, GROUP)
        return remote(
            tiles.at[half, piece],
            beside[half].at[way, piece],
            early_send_sem.at[half, way, part],
            early_recv_sem.at[half, way, part],
            early_to[half][way],
        )

    def late_copy(half, way, part):
        piece = pl.ds(part * TC, TC)
        return remote(
            send.at[half, way, piece],
            recv.at[half, way, piece],
            late_send_sem.at[half, way, part],
            late_recv_sem.at[half, way, part],
            late_to[half][way],
        )

    first_rows, last_rows = pl.ds(TOP, PAD), pl.ds(TOP + SPAN - PAD, PAD)

    def edge_copy(way, part):
        return remote(
            edge_send.at[way, part],
            edge_recv.at[way, part],
            edge_send_sem.at[way, part],
            edge_recv_sem.at[way, part],
            early_to[0][way],
        )

    def rim_copies(way):
        rows = (first_rows, last_rows)[way]
        triples = [(pl.ds(0, SPAN), rim_recv.at[way], late_to[0][way])]
        for side in range(2):
            cols = pl.ds(0, TILE) if side == 0 else pl.ds(SPAN - TILE, TILE)
            triples.append((cols, corner_recv.at[2 * way + side], corners[2 * way + side]))
        return [
            remote(out_ref.at[rows, cols], target, rim_send_sem.at[way, number], rim_recv_sem.at[way, number], device)
            for number, (cols, target, device) in enumerate(triples)
        ]

    constant_copies[0].wait()
    filled = jnp.int32(0)
    key_of = wanted_ref[6:7, :]
    sub = lax.broadcasted_iota(jnp.int32, (CELLS, 128), 0)
    sequence = jnp.zeros((1, 128), jnp.int32)
    labels = jnp.zeros((CELLS, 128), jnp.int32)
    for i in range(2 * CELLS):
        code, cell = dest_ref[0, i], offset_ref[0, i]
        away = code != 4
        key = jnp.where(away, filled, 64 + cell)
        sequence = jnp.where(key_of == key, i, sequence)
        labels = jnp.where(sub == key, code * CELLS + cell + 1, labels)
        filled = filled + away.astype(jnp.int32)
    order[...] = jnp.broadcast_to(sequence, (8, 128))
    label_ref[...] = labels
    order_copy = pltpu.make_async_copy(order, order_smem, local_sem)
    order_copy.start()

    psf_copy.wait()
    gap = jnp.zeros((2 * CELLS, 64 - KS), F32)
    for r in range(KS):
        tap = psf[r].astype(F32)
        taps_wide[2 * CELLS * r : 2 * CELLS * (r + 1), :] = jnp.concatenate([tap, gap, tap, gap], axis=1)
    taps_wide[2 * CELLS * KS :, :] = jnp.zeros((2 * CELLS * (48 - KS), 128), F32)
    for t in range(2 * CELLS):
        kern_ref[t] = taps_wide[pl.ds(t, 48, stride=2 * CELLS), :].astype(BF16)

    def prepare(block, carry):
        rows = pl.ds(pl.multiple_of(block * 64, 64), 64)
        usable = jnp.where((mask[rows, :] & 7) != 7, 1.0, 0.0).astype(BF16)
        masked = image[rows, :] * usable
        for plane, value in enumerate((masked, usable)):
            moved = jnp.concatenate([value[:, 64:], value[:, :64]], axis=1)
            for way, data in enumerate((value, moved)):
                for j in range(6):
                    for i in range(4):
                        planes[way, plane, j, block * 4 + i] = data[16 * i : 16 * i + 16, 128 * j : 128 * j + 128]
        return carry

    steps = 768 // 64 // LOADS
    for number in range(LOADS):
        for load in loads[2 * number : 2 * number + 2]:
            load.wait()
        lax.fori_loop(number * steps, (number + 1) * steps, prepare, 0)
    order_copy.wait()
    for copy in constant_copies[1:]:
        copy.wait()

    lane = lax.broadcasted_iota(jnp.int32, (ROWS, WIN), 1)
    sub = lax.broadcasted_iota(jnp.int32, (WIN, WIN), 0)
    short = lax.broadcasted_iota(jnp.int32, (8, WIN), 1)
    quantity = lax.broadcasted_iota(jnp.int32, (8, WIN), 0)
    index = (short + jnp.where(short < WARP_N - MARGIN, MARGIN, MARGIN - WARP_N)).astype(F32)

    def warp_rows(fraction, stretch, shift):
        position = (5.0 + fraction) + index * (1.0 + stretch)
        nearest = jnp.floor(position + 0.5)
        odd = nearest - 2.0 * jnp.floor(nearest * 0.5)
        part = position - nearest
        sine = (1.0 - 2.0 * odd) * part * poly(SIN_PI, part * part)
        sign = (1 - 2 * (shift & 1)).astype(F32)
        amplitude = ((-5.0 / math.pi**2) * sign) * sine
        turn = position - 10.0 * jnp.floor(position * 0.1) + lax.rem(shift, 10).astype(F32)
        turn = turn * 0.1
        turn = turn - jnp.floor(turn + 0.5)
        square = turn * turn
        cosine, sine = poly(COS_TURN, square), turn * poly(SIN_TURN, square)
        position = jnp.where(short < WARP_N, position, 1e4)
        return jnp.where(quantity == 0, position, jnp.where(quantity == 1, amplitude * cosine, amplitude * sine))

    weight = weight_ref[0]
    each = range(GROUP)

    def store_tile(slot, plane, value):
        for half in range(2):
            tiles[half, slot, plane] = value[half * SLAB : (half + 1) * SLAB].astype(BF16)

    def gather(half, position):
        value = None
        for source in range(3):
            slot = table_smem[3 * half + source, position]
            present = jnp.where(slot >= 0, 1.0, 0.0)
            at = within(slot, CELLS - 1)
            data = tiles[half, at] if source == 0 else beside[half][source - 1, at]
            term = data.astype(F32) * present
            value = term if value is None else value + term
        return value

    def find_slots():
        for half in range(2):
            for way in range(2):
                label_copy(half, way).wait()
            for source in range(3):
                lookup = label_ref[...] if source == 0 else label_in[half, source - 1]
                number = 3 * half + source
                found = jnp.zeros((1, 128), jnp.int32)
                for slot in range(CELLS):
                    same = lookup[slot : slot + 1] == wanted_ref[number : number + 1, :]
                    found = found + jnp.where(same, slot + 1, 0)
                table[number : number + 1, :] = found - 1
        to_smem = pltpu.make_async_copy(table, table_smem, local_sem)
        to_smem.start()
        to_smem.wait()

    def pass_on(half):
        for part in range(CELLS // GROUP):
            for way in range(2):
                early_copy(half, way, part).wait()

        def outgoing(part, carry):
            for way in range(2):
                for c in range(TC):
                    cell = part * TC + c
                    send[half, way, cell] = gather(half, 2 * CELLS * way + cell).astype(BF16)
                late_copy(half, way, part).start()
            return carry

        lax.fori_loop(0, TR, outgoing, 0)

    def work(step, carry):
        chosen = [within(order_smem[0, step * GROUP + g], 2 * CELLS - 1) for g in each]
        half_img, half_cov, lt = [], [], []
        for g in each:
            t = chosen[g]
            first_row, first_col = anchor_ref[0, t], anchor_ref[1, t]
            row16 = within(first_row // 16, (768 - WIN) // 16)
            col64 = within(first_col // 64, (768 - WIN) // 64)
            off_r = first_row - row16 * 16
            off_c = first_col - col64 * 64
            par = within(col64 % 2, 1)
            pair = within(col64 // 2, 4)
            s_img, s_cov = (
                jnp.concatenate(
                    [
                        jnp.concatenate([planes[par, plane, pair + j, row16 + i] for i in range(16)], axis=0)
                        for j in range(2)
                    ],
                    axis=1,
                )
                for plane in range(2)
            )
            q0 = jnp.transpose(warp_rows(frac_ref[0, t], scale_ref[0, t], off_r))[:ROWS]
            d0 = (lane - off_r).astype(F32) - q0[:, 0:1]
            l0 = lanczos(d0, q0[:, 1:2], q0[:, 2:3], along_ref[0:1, :], along_ref[1:2, :])
            q1 = warp_rows(frac_ref[1, t], scale_ref[1, t], off_c)
            d1 = (sub - off_c).astype(F32) - q1[0:1, :]
            cosd = jnp.concatenate([down_ref[0], down_ref[0]], axis=1)
            sind = jnp.concatenate([down_ref[1], down_ref[1]], axis=1)
            lt.append(lanczos(d1, q1[1:2, :], q1[2:3, :], cosd, sind))
            half_img.append(dot(l0, s_img).astype(BF16))
            half_cov.append(dot(l0[:TILE], s_cov).astype(BF16))
        warped = [dot(half_img[g], lt[g]).astype(BF16) for g in each]
        for g in each:
            coverage = dot(half_cov[g], lt[g][:, :TILE])
            store_tile(step * GROUP + g, 1, weight * coverage)
        x1 = dot(jnp.concatenate(warped, axis=0), cols_ref[...]).astype(BF16)
        x2 = [dot(rows_ref[...], x1[g * ROWS : (g + 1) * ROWS]) for g in each]
        k1 = dot(jnp.concatenate([kern_ref[chosen[g]] for g in each], axis=0), kcols_ref[...])
        k1h = k1.astype(BF16)
        k1l = (k1 - k1h.astype(F32)).astype(BF16)
        z = []
        for g in each:
            h, l = k1h[g * 48 : g * 48 + 48], k1l[g * 48 : g * 48 + 48]
            k2 = dot(krows_ref[...], jnp.concatenate([h, l, h], axis=0))
            x = x2[g]
            xrr, xri, xir, xii = x[:HALF, :128], x[:HALF, 128:], x[HALF:, :128], x[HALF:, 128:]
            krr, kri, kir, kii = k2[:HALF, :128], k2[:HALF, 128:], k2[HALF:, :128], k2[HALF:, 128:]
            xpr, xpi, xmr, xmi = xrr - xii, xir + xri, xrr + xii, xir - xri
            kpr, kpi, kmr, kmi = krr - kii, kir + kri, krr + kii, kir - kri
            ppr, ppi = xpr * kpr - xpi * kpi, xpr * kpi + xpi * kpr
            pmr, pmi = xmr * kmr - xmi * kmi, xmr * kmi + xmi * kmr
            top = jnp.concatenate([ppr + pmr, ppi - pmi], axis=1)
            bottom = jnp.concatenate([ppi + pmi, pmr - ppr], axis=1)
            z.append(jnp.concatenate([top, bottom], axis=0).astype(BF16))
        y = dot(jnp.concatenate(z, axis=0), icols_ref[...])
        y = y[:, :TILE] + y[:, TILE:]
        yh = y.astype(BF16)
        yl = (y - yh.astype(F32)).astype(BF16)
        ycat = jnp.concatenate([yh, yl], axis=1)
        for g in each:
            o = dot(irows_ref[...], ycat[g * ROWS : (g + 1) * ROWS])
            matched = o[:TILE, :TILE] + (o[:TILE, TILE:] + o[TILE:, :TILE])
            store_tile(step * GROUP + g, 0, weight * matched)

        @pl.when(step == 0)
        def _():
            pl.semaphore_wait(barrier, len(around))
            for half in range(2):
                for way in range(2):
                    label_copy(half, way).start()

        @pl.when(step < CELLS // GROUP)
        def _():
            for half in range(2):
                for way in range(2):
                    early_copy(half, way, step).start()

        @pl.when(step == 4)
        def _():
            find_slots()
            pass_on(1)

        @pl.when(step == 6)
        def _():
            pass_on(0)

        return carry

    lax.fori_loop(0, 2 * CELLS // GROUP, work, 0)

    def staying(cell, carry):
        for half in range(2):
            total[half, cell] = gather(half, CELLS + cell) + tiles[half, CELLS + cell].astype(F32)
        return carry

    lax.fori_loop(0, CELLS, staying, 0)

    lane = lax.broadcasted_iota(jnp.int32, (PAD, TILE), 1)

    def send_edges(part):
        for way in range(2):
            cols = slice(SPAN - TILE, SPAN) if way == 0 else slice(0, TILE)
            packed = jnp.zeros((PAD, TILE), F32)
            for q in range(4):
                row = TOP + part * TILE + q * PAD
                end = out_ref[row : row + PAD, cols]
                turn = (PAD * q + (PAD if way == 0 else 0)) % TILE
                moved = end if turn == 0 else pltpu.roll(end, turn, 1)
                packed = jnp.where((lane >= PAD * q) & (lane < PAD * (q + 1)), moved, packed)
            edge_send[way, part] = packed
            edge_copy(way, part).start()

    for part in range(TR):
        for half in range(2):
            for way in range(2):
                late_copy(half, way, part).wait()
            for place in range(part * TC, (part + 1) * TC):
                row = TOP + PLACES[place] // TC * TILE + half * SLAB
                col = PLACES[place] % TC * TILE
                value = total[half, place] + (recv[half, 0, place].astype(F32) + recv[half, 1, place].astype(F32))
                out_ref[row : row + SLAB, col : col + TILE] = value[0] / (jnp.maximum(value[1], 0.0) + 1.0)
        if part < 2:
            for copy in rim_copies(part):
                copy.start()
            send_edges(part * (TR - 1))
        if part == 2:
            send_edges(1)
            send_edges(2)

    blank = jnp.zeros((8, WIDE), F32)
    out_ref[0:8, :] = blank
    out_ref[TALL - 8 : TALL, :] = blank

    def unpack(part, carry):
        for way in range(2):
            edge_copy(way, part).wait()
        from_left, from_right = edge_recv[0, part] * has_left, edge_recv[1, part] * has_right
        for q in range(4):
            turn = (TILE - PAD * q) % TILE
            near = from_right if turn == 0 else pltpu.roll(from_right, turn, 1)
            turn = (TILE - PAD - PAD * q) % TILE
            far = from_left if turn == 0 else pltpu.roll(from_left, turn, 1)
            rows = pl.ds(pl.multiple_of(TOP + part * TILE + q * PAD, 8), PAD)
            out_ref[rows, SPAN:] = jnp.where(lane < PAD, near, jnp.where(lane >= TILE - PAD, far, 0.0))
        return carry

    lax.fori_loop(0, TR, unpack, 0)
    for way in range(2):
        for copy in rim_copies(way):
            copy.wait()
    for rows, arrived, far, near, factor in (
        (slice(8, TOP), 1, 3, 2, has_above),
        (slice(TOP + SPAN, TALL - 8), 0, 1, 0, has_below),
    ):
        out_ref[rows, :SPAN] = rim_recv[arrived] * factor
        near, far = corner_recv[near] * (has_right * factor), corner_recv[far] * (has_left * factor)
        out_ref[rows, SPAN:] = jnp.where(lane < PAD, near, jnp.where(lane >= TILE - PAD, far, 0.0))


def coaddition_call(dest, offset, anchor, frac, scale, weight, image, mask, psf, consts):
    scalars = (dest, offset, anchor, frac, scale, weight)
    fixed = (jnp.asarray(wanted_labels()),) + tuple(consts)
    dma = pltpu.SemaphoreType.DMA
    slab = (2, SLAB, TILE)
    parts = CELLS // GROUP
    return pl.pallas_call(
        coaddition_kernel,
        in_specs=[pl.BlockSpec(memory_space=pltpu.SMEM)] * len(scalars)
        + [pl.BlockSpec(memory_space=pl.ANY)] * (3 + len(fixed)),
        out_specs=pl.BlockSpec(memory_space=pltpu.VMEM),
        out_shape=pltpu.VMEM((TALL, WIDE), F32),
        scratch_shapes=[pltpu.VMEM(a.shape, a.dtype) for a in fixed]
        + [
            pltpu.VMEM((768, 768), BF16),
            pltpu.VMEM((768, 768), jnp.int32),
            pltpu.VMEM(psf.shape, BF16),
            pltpu.VMEM((48 * 2 * CELLS, 128), F32),
            pltpu.VMEM((2 * CELLS, 48, 128), BF16),
            pltpu.VMEM((CELLS, 128), jnp.int32),
            pltpu.VMEM((8, 128), jnp.int32),
            pltpu.SMEM((8, 128), jnp.int32),
            pltpu.VMEM((2, 2, 6, 48, 16, 128), BF16),
            pltpu.VMEM((2, 2 * CELLS) + slab, BF16),
            pltpu.VMEM((2, CELLS) + slab, BF16),
            pltpu.VMEM((2, CELLS) + slab, BF16),
            pltpu.VMEM((2, 2, CELLS, 128), jnp.int32),
            pltpu.VMEM((8, 128), jnp.int32),
            pltpu.SMEM((8, 128), jnp.int32),
            pltpu.VMEM((2, 2, CELLS) + slab, BF16),
            pltpu.VMEM((2, 2, CELLS) + slab, BF16),
            pltpu.VMEM((2, CELLS) + slab, F32),
            pltpu.VMEM((2, TR, PAD, TILE), F32),
            pltpu.VMEM((2, TR, PAD, TILE), F32),
            pltpu.VMEM((2, PAD, SPAN), F32),
            pltpu.VMEM((4, PAD, TILE), F32),
            dma((2, 2, parts)), dma((2, 2, parts)), dma((2, 2)), dma((2, 2)), dma((2, 2, TR)), dma((2, 2, TR)),
            dma((2, TR)), dma((2, TR)), dma((2, 3)), dma((2, 3)), dma(()), dma((2, LOADS)), dma(()), dma((len(fixed),)),
        ],
        compiler_params=pltpu.CompilerParams(
            vmem_limit_bytes=56 * 2**20, collective_id=0, has_side_effects=True
        ),
    )(*scalars, image, mask, psf, *fixed)


LEVEL_ROWS = ((8, 584), (16, 576), (24, 568), (40, 552))
BLOCK = 256
WAVE = 192


def starlet_kernel(edge_ref, first_ref, details_ref, smooth_ref, ping, pong, band, done, sem):
    top, bottom, left, right = (edge_ref[i] for i in range(4))
    tiles = WIDE // 128
    zero = jnp.zeros((8, WIDE), F32)
    for ref in (ping, pong):
        ref[0:8, :] = zero
        ref[TALL - 8 : TALL, :] = zero
    offset = lax.broadcasted_iota(jnp.int32, (512, 256), 0) - lax.broadcasted_iota(jnp.int32, (512, 256), 1) - 128
    offset = jnp.abs(offset)
    for k in range(SCALES):
        s = 2**k
        tap = jnp.where(offset == 0, 6.0, jnp.where(offset == s, 4.0, jnp.where(offset == 2 * s, 1.0, 0.0)))
        band[k] = (tap * (1.0 / 16.0)).astype(BF16)

    source = first_ref
    copies = []
    for k in range(SCALES):
        s = 2**k
        target = (ping, pong)[k % 2]
        begin, end = LEVEL_ROWS[k]

        def down(view, count, at=16, s=s):
            def near(by):
                return view[at + by : at + by + count, :]

            center = near(0)
            return center, (near(-2 * s) + near(2 * s)) + 4.0 * (near(-s) + near(s)) + 6.0 * center

        def across(rows, s=s):
            count = rows.shape[0]
            parts = [rows[:, 128 * j : 128 * (j + 1)] for j in range(tiles)]
            lane = lax.broadcasted_iota(jnp.int32, (count, 128), 1)

            def after(by):
                turned = [pltpu.roll(part, by, 1) for part in parts]
                return [jnp.where(lane < by, turned[j - 1], turned[j]) for j in range(tiles)]

            def before(by):
                turned = [pltpu.roll(part, 128 - by, 1) for part in parts]
                return [jnp.where(lane >= 128 - by, turned[(j + 1) % tiles], turned[j]) for j in range(tiles)]

            a, b, c, d = after(2 * s), before(2 * s), after(s), before(s)
            return [((a[j] + b[j]) + 4.0 * (c[j] + d[j]) + 6.0 * parts[j]) * (1.0 / 256.0) for j in range(tiles)]

        def across_product(rows, k=k):
            rows = rows * (1.0 / 16.0)
            high = rows.astype(BF16)
            low = (rows - high.astype(F32)).astype(BF16)
            full = []
            for first, count in ((0, 2), (2, 2), (4, 1)):
                total = None
                for part in (high, low):
                    pieces = [part[:, 128 * (j % tiles) : 128 * (j % tiles) + 128] for j in range(first - 1, first + count + 1)]
                    weights = band[k] if count == 2 else band[k, :384, :128]
                    term = lax.dot_general(
                        jnp.concatenate(pieces, axis=1), weights, (((1,), (0,)), ((), ())), preferred_element_type=F32
                    )
                    total = term if total is None else total + term
                full += [total[:, 128 * j : 128 * j + 128] for j in range(count)]
            return full

        def store(row, full, factor, target=target):
            count = full[0].shape[0]
            lane = lax.broadcasted_iota(jnp.int32, (count, 128), 1)
            side = jnp.where(lane < 64, right, left)
            for j in range(tiles):
                value = full[j] * side if j == tiles - 1 else full[j]
                value = value if factor is None else value * factor
                target[pl.ds(row, count), 128 * j : 128 * (j + 1)] = value

        if k < SCALES - 1:
            for row, last, factor in ((begin, TOP, top), (TOP + SPAN, end, bottom)):
                low, high = max(row - 16, 0), min(last + 16, TALL)
                count = last - row
                rows = source[low:high, :]
                if low > row - 16:
                    rows = jnp.concatenate([jnp.zeros((low - row + 16, WIDE), F32), rows], axis=0)
                if high < last + 16:
                    rows = jnp.concatenate([rows, jnp.zeros((last + 16 - high, WIDE), F32)], axis=0)
                store(row, across(down(rows, count)[1]), factor)

        def one(block, carry, k=k, source=source, down=down, across=across, store=store, across_product=across_product):
            row = pl.multiple_of(TOP + block * BLOCK, 8)
            here = pl.multiple_of(block * BLOCK, 8)
            view = source.at[pl.ds(pl.multiple_of(row - 16, 8), BLOCK + 32), :]
            spans = [(0, BLOCK - WAVE, across), (BLOCK - WAVE, WAVE, across_product)]
            for start, count, method in spans:
                center, rows = down(view, count, 16 + start)
                full = method(rows)
                if k < SCALES - 1:
                    store(pl.multiple_of(row + start, 8), full, None)
                at = pl.ds(pl.multiple_of(here + start, 8), count)
                for j in range(SPAN // 128):
                    cols = slice(128 * j, 128 * (j + 1))
                    done[k, at, cols] = center[:, cols] - full[j]
                    if k == SCALES - 1:
                        done[SCALES, at, cols] = full[j]
            return carry

        half = SPAN // BLOCK // 2
        for number in range(2):
            lax.fori_loop(number * half, (number + 1) * half, one, 0)
            rows = pl.ds(number * SPAN // 2, SPAN // 2)
            copies.append(pltpu.make_async_copy(done.at[k, rows], details_ref.at[k, rows], sem.at[2 * k + number]))
            if k == SCALES - 1:
                copies.append(pltpu.make_async_copy(done.at[SCALES, rows], smooth_ref.at[rows], sem.at[2 * SCALES + number]))
                copies[-1].start()
                copies[-2].start()
            else:
                copies[-1].start()
        source = target
    for copy in copies:
        copy.wait()


def starlet_call(edges, first):
    return pl.pallas_call(
        starlet_kernel,
        in_specs=[pl.BlockSpec(memory_space=pltpu.SMEM), pl.BlockSpec(memory_space=pltpu.VMEM)],
        out_specs=[pl.BlockSpec(memory_space=pltpu.HBM)] * 2,
        out_shape=[
            jax.ShapeDtypeStruct((SCALES, SPAN, SPAN), F32),
            jax.ShapeDtypeStruct((SPAN, SPAN), F32),
        ],
        scratch_shapes=[
            pltpu.VMEM((TALL, WIDE), F32),
            pltpu.VMEM((TALL, WIDE), F32),
            pltpu.VMEM((SCALES, 512, 256), BF16),
            pltpu.VMEM((SCALES + 1, SPAN, SPAN), F32),
            pltpu.SemaphoreType.DMA((2 * SCALES + 2,)),
        ],
        compiler_params=pltpu.CompilerParams(vmem_limit_bytes=40 * 2**20),
    )(edges, first)


def shards(image, mask, weight, anchor, frac, scale, kernels, dest, offset):
    first = coaddition_call(
        dest, offset, anchor[0].T, frac[0].T, scale[0].T, weight, image, mask, kernels[0].transpose(1, 0, 2), constants()
    )
    band, patch = lax.axis_index("band"), lax.axis_index("patch")
    edges = jnp.stack(
        [band > 0, band < lax.axis_size("band") - 1, patch > 0, patch < lax.axis_size("patch") - 1]
    ).astype(F32)
    return tuple(starlet_call(edges, first))


def solution(mesh):
    owner = ("patch", "band")
    in_specs = (
        P(owner, None, None),
        P(owner, None, None),
        P(owner),
        P(owner, None, None),
        P(owner, None, None),
        P(owner, None, None),
        P(owner, None, None, None),
        P(owner, None),
        P(owner, None),
    )
    out_specs = (P(None, "band", "patch"), P("band", "patch"))
    return jax.shard_map(shards, mesh=mesh, in_specs=in_specs, out_specs=out_specs, check_vma=False)
```

```python
import math
import numpy as np
import ml_dtypes
import jax
import jax.numpy as jnp
from jax import lax
from jax.experimental import pallas as pl
from jax.experimental.pallas import tpu as pltpu
from jax.sharding import PartitionSpec as P

TILE, KS, SCALES, TR, TC, MARGIN, WARP_N, SRC_N = 128, 41, 4, 4, 4, 20, 168, 184
ROWS = 176
HALF = 88
WIN = 256
F32, BF16 = jnp.float32, jnp.bfloat16


def split_bf16(values):
    high = values.astype(ml_dtypes.bfloat16)
    low = (values - high.astype(np.float64)).astype(ml_dtypes.bfloat16)
    return high, low


def spectra():
    bins = np.arange(WARP_N // 2 + 1)

    def forward(points, sign):
        angle = 2.0 * np.pi / WARP_N * np.outer(bins, points)
        return np.cos(angle), sign * np.sin(angle)

    order = (np.arange(WARP_N) + MARGIN) % WARP_N
    real, imag = forward(order, -1.0)
    rows = np.zeros((ROWS, WIN))
    rows[: len(bins), :WARP_N] = real
    rows[HALF : HALF + len(bins), :WARP_N] = imag
    cols = np.zeros((WIN, WIN))
    cols[:WARP_N, : len(bins)] = real.T
    cols[:WARP_N, 128 : 128 + len(bins)] = imag.T
    real, imag = forward(np.arange(KS), 1.0)
    kcols = np.zeros((64, WIN))
    kcols[:KS, : len(bins)] = real.T
    kcols[:KS, 128 : 128 + len(bins)] = imag.T
    krows = np.zeros((ROWS, 48))
    krows[: len(bins), :KS] = real
    krows[HALF : HALF + len(bins), :KS] = imag
    count = np.full(len(bins), 2.0)
    count[0] = count[-1] = 1.0
    angle = 2.0 * np.pi / WARP_N * np.outer(np.arange(TILE), bins)
    back_real = np.cos(angle) * count / WARP_N
    back_imag = -np.sin(angle) * count / WARP_N
    icols = np.zeros((WIN, TILE))
    icols[: len(bins)] = back_real.T
    icols[128 : 128 + len(bins)] = back_imag.T
    irows = np.zeros((TILE, ROWS))
    irows[:, : len(bins)] = 0.5 * back_real
    irows[:, HALF : HALF + len(bins)] = 0.5 * back_imag
    kcols_high, kcols_low = split_bf16(kcols)
    krows_high, krows_low = split_bf16(krows)
    icols_high, icols_low = split_bf16(icols)
    irows_high, irows_low = split_bf16(irows)
    rows_pad = rows[:, :ROWS]
    return (
        cols.astype(ml_dtypes.bfloat16),
        rows_pad.astype(ml_dtypes.bfloat16),
        np.concatenate([kcols_high, kcols_low]),
        np.concatenate([krows_high, krows_high, krows_low], axis=1),
        np.concatenate([icols_high, icols_low], axis=1),
        np.concatenate([irows_high, irows_low]),
    )


def phase_constants():
    j = np.arange(WIN)
    sign = 1.0 - 2.0 * (j % 2)
    cosine = (sign * np.cos(np.pi * j / 5.0)).astype(np.float32)
    sine = (sign * np.sin(np.pi * j / 5.0)).astype(np.float32)
    along = np.zeros((8, WIN), np.float32)
    along[0], along[1] = cosine, sine
    down = np.stack([np.repeat(cosine[:, None], 128, 1), np.repeat(sine[:, None], 128, 1)])
    return along, down


def poly(coefficients, x):
    total = jnp.full_like(x, coefficients[-1])
    for value in coefficients[-2::-1]:
        total = total * x + value
    return total


SIN_PI = (3.14159265, -5.16771276, 2.55016332, -0.5992522, 0.0820504, -0.00702839)
SIN_TURN = (6.28318531, -41.34170222, 81.60524742, -76.70580022, 42.05775402, -15.08656526, 3.78131888, -0.62077872)
COS_TURN = (1.0, -19.73920874, 64.93938908, -85.45665831, 60.24213134, -26.40466819, 7.80013144, -1.45311232)


def lanczos(d, cos_row, sin_row, cos_col, sin_col):
    d2 = d * d
    u = cos_row * sin_col - sin_row * cos_col
    g = u / d2
    g = jnp.where(d2 < 1e-5, 1.0, g)
    return jnp.where(d2 < 25.0, g, 0.0).astype(BF16)


def dot(a, b):
    return lax.dot_general(a, b, (((1,), (0,)), ((), ())), preferred_element_type=F32)


def constants():
    along, down = phase_constants()
    return [jnp.asarray(a) for a in (along, down) + spectra()]


CELLS = TR * TC
GROUP = 4
LOADS = 3
SLAB = TILE // 2
SPAN = TR * TILE
PAD = 32
WIDE = SPAN + 128
TOP = 8 + PAD
TALL = SPAN + 2 * TOP
MESH = pl.DeviceIdType.MESH


def within(value, top):
    return jnp.minimum(jnp.maximum(value, 0), top)


def whole(a):
    return pl.BlockSpec(a.shape, lambda *_: (0,) * a.ndim)


PLACES = (0, 1, 2, 3, 12, 13, 14, 15, 4, 7, 8, 11, 5, 6, 9, 10)


def wanted_labels():
    lanes = np.arange(128)
    cell = np.asarray(PLACES)[lanes % CELLS]
    rows = np.full((8, 128), -1, np.int32)
    for source, step in enumerate((1, 2, 0)):
        rows[source] = (3 * (lanes // CELLS) + step) * CELLS + cell + 1
        rows[3 + source] = (3 * step + lanes // CELLS) * CELLS + cell + 1
    rows = np.where(lanes < 3 * CELLS, rows, -1).astype(np.int32)
    rows[6] = np.where(lanes < CELLS, lanes, np.where(lanes < 2 * CELLS, 64 + cell, -1))
    return rows


def coaddition_kernel(
    dest_ref, offset_ref, anchor_ref, frac_ref, scale_ref, weight_ref,
    image_hbm, mask_hbm, psf_hbm, wanted_hbm,
    along_hbm, down_hbm, cols_hbm, rows_hbm, kcols_hbm, krows_hbm, icols_hbm, irows_hbm,
    out_ref,
    wanted_ref, along_ref, down_ref, cols_ref, rows_ref, kcols_ref, krows_ref, icols_ref, irows_ref,
    image, mask, psf, taps_wide, kern_ref, label_ref, order, order_smem, planes, tiles, upper_in, lower_in, label_in, table, table_smem, send, recv, total, edge_send, edge_recv, rim_recv, corner_recv,
    early_send_sem, early_recv_sem, label_send_sem, label_recv_sem, late_send_sem, late_recv_sem,
    edge_send_sem, edge_recv_sem, rim_send_sem, rim_recv_sem, local_sem, load_sem, psf_sem, constant_sem,
):
    psf_copy = pltpu.make_async_copy(psf_hbm, psf, psf_sem)
    constant_copies = [
        pltpu.make_async_copy(source, target, constant_sem.at[number])
        for number, (source, target) in enumerate(
            (
                (wanted_hbm, wanted_ref),
                (along_hbm, along_ref),
                (down_hbm, down_ref),
                (cols_hbm, cols_ref),
                (rows_hbm, rows_ref),
                (kcols_hbm, kcols_ref),
                (krows_hbm, krows_ref),
                (icols_hbm, icols_ref),
                (irows_hbm, irows_ref),
            )
        )
    ]
    constant_copies[0].start()
    psf_copy.start()
    loads = []
    for number in range(LOADS):
        rows = pl.ds(number * (768 // LOADS), 768 // LOADS)
        for kind, (source, target) in enumerate(((image_hbm, image), (mask_hbm, mask))):
            loads.append(pltpu.make_async_copy(source.at[0, rows], target.at[rows], load_sem.at[kind, number]))
    for load in loads:
        load.start()
    for copy in constant_copies[1:]:
        copy.start()

    patch, band = lax.axis_index("patch"), lax.axis_index("band")
    n_patch, n_band = lax.axis_size("patch"), lax.axis_size("band")
    left_patch, right_patch = lax.rem(patch + n_patch - 1, n_patch), lax.rem(patch + 1, n_patch)
    above_band, below_band = lax.rem(band + n_band - 1, n_band), lax.rem(band + 1, n_band)
    left, right = {"patch": left_patch, "band": band}, {"patch": right_patch, "band": band}
    above, below = {"patch": patch, "band": above_band}, {"patch": patch, "band": below_band}
    corners = [{"patch": p, "band": b} for b in (above_band, below_band) for p in (left_patch, right_patch)]
    has_left = jnp.where(patch > 0, 1.0, 0.0)
    has_right = jnp.where(patch < n_patch - 1, 1.0, 0.0)
    has_above = jnp.where(band > 0, 1.0, 0.0)
    has_below = jnp.where(band < n_band - 1, 1.0, 0.0)

    barrier = pltpu.get_barrier_semaphore()
    around = [left, right, above, below] + corners
    for device in around:
        pl.semaphore_signal(barrier, inc=1, device_id=device, device_id_type=MESH)

    def remote(src, dst, send_sem, recv_sem, device):
        return pltpu.make_async_remote_copy(
            src_ref=src, dst_ref=dst, send_sem=send_sem, recv_sem=recv_sem, device_id=device, device_id_type=MESH
        )

    beside = (upper_in, lower_in)

    early_to = ((right, left), (below, above))
    late_to = ((above, below), (left, right))

    def label_copy(half, way):
        return remote(
            label_ref,
            label_in.at[half, way],
            label_send_sem.at[half, way],
            label_recv_sem.at[half, way],
            early_to[half][way],
        )

    def early_copy(half, way, part):
        piece = pl.ds(part * GROUP, GROUP)
        return remote(
            tiles.at[half, piece],
            beside[half].at[way, piece],
            early_send_sem.at[half, way, part],
            early_recv_sem.at[half, way, part],
            early_to[half][way],
        )

    def late_copy(half, way, part):
        piece = pl.ds(part * TC, TC)
        return remote(
            send.at[half, way, piece],
            recv.at[half, way, piece],
            late_send_sem.at[half, way, part],
            late_recv_sem.at[half, way, part],
            late_to[half][way],
        )

    first_rows, last_rows = pl.ds(TOP, PAD), pl.ds(TOP + SPAN - PAD, PAD)

    def edge_copy(way, part):
        return remote(
            edge_send.at[way, part],
            edge_recv.at[way, part],
            edge_send_sem.at[way, part],
            edge_recv_sem.at[way, part],
            early_to[0][way],
        )

    def rim_copies(way):
        rows = (first_rows, last_rows)[way]
        triples = [(pl.ds(0, SPAN), rim_recv.at[way], late_to[0][way])]
        for side in range(2):
            cols = pl.ds(0, TILE) if side == 0 else pl.ds(SPAN - TILE, TILE)
            triples.append((cols, corner_recv.at[2 * way + side], corners[2 * way + side]))
        return [
            remote(out_ref.at[rows, cols], target, rim_send_sem.at[way, number], rim_recv_sem.at[way, number], device)
            for number, (cols, target, device) in enumerate(triples)
        ]

    constant_copies[0].wait()
    filled = jnp.int32(0)
    key_of = wanted_ref[6:7, :]
    sub = lax.broadcasted_iota(jnp.int32, (CELLS, 128), 0)
    sequence = jnp.zeros((1, 128), jnp.int32)
    labels = jnp.zeros((CELLS, 128), jnp.int32)
    for i in range(2 * CELLS):
        code, cell = dest_ref[0, i], offset_ref[0, i]
        away = code != 4
        key = jnp.where(away, filled, 64 + cell)
        sequence = jnp.where(key_of == key, i, sequence)
        labels = jnp.where(sub == key, code * CELLS + cell + 1, labels)
        filled = filled + away.astype(jnp.int32)
    order[...] = jnp.broadcast_to(sequence, (8, 128))
    label_ref[...] = labels
    order_copy = pltpu.make_async_copy(order, order_smem, local_sem)
    order_copy.start()

    psf_copy.wait()
    gap = jnp.zeros((2 * CELLS, 64 - KS), F32)
    for r in range(KS):
        tap = psf[r].astype(F32)
        taps_wide[2 * CELLS * r : 2 * CELLS * (r + 1), :] = jnp.concatenate([tap, gap, tap, gap], axis=1)
    taps_wide[2 * CELLS * KS :, :] = jnp.zeros((2 * CELLS * (48 - KS), 128), F32)
    for t in range(2 * CELLS):
        kern_ref[t] = taps_wide[pl.ds(t, 48, stride=2 * CELLS), :].astype(BF16)

    def prepare(block, carry):
        rows = pl.ds(pl.multiple_of(block * 64, 64), 64)
        usable = jnp.where((mask[rows, :] & 7) != 7, 1.0, 0.0).astype(BF16)
        masked = image[rows, :] * usable
        for plane, value in enumerate((masked, usable)):
            moved = jnp.concatenate([value[:, 64:], value[:, :64]], axis=1)
            for way, data in enumerate((value, moved)):
                for j in range(6):
                    for i in range(4):
                        planes[way, plane, j, block * 4 + i] = data[16 * i : 16 * i + 16, 128 * j : 128 * j + 128]
        return carry

    steps = 768 // 64 // LOADS
    for number in range(LOADS):
        for load in loads[2 * number : 2 * number + 2]:
            load.wait()
        lax.fori_loop(number * steps, (number + 1) * steps, prepare, 0)
    order_copy.wait()
    for copy in constant_copies[1:]:
        copy.wait()

    lane = lax.broadcasted_iota(jnp.int32, (ROWS, WIN), 1)
    sub = lax.broadcasted_iota(jnp.int32, (WIN, WIN), 0)
    short = lax.broadcasted_iota(jnp.int32, (8, WIN), 1)
    quantity = lax.broadcasted_iota(jnp.int32, (8, WIN), 0)
    index = (short + jnp.where(short < WARP_N - MARGIN, MARGIN, MARGIN - WARP_N)).astype(F32)

    def warp_rows(fraction, stretch, shift):
        position = (5.0 + fraction) + index * (1.0 + stretch)
        nearest = jnp.floor(position + 0.5)
        odd = nearest - 2.0 * jnp.floor(nearest * 0.5)
        part = position - nearest
        sine = (1.0 - 2.0 * odd) * part * poly(SIN_PI, part * part)
        sign = (1 - 2 * (shift & 1)).astype(F32)
        amplitude = ((-5.0 / math.pi**2) * sign) * sine
        turn = position - 10.0 * jnp.floor(position * 0.1) + lax.rem(shift, 10).astype(F32)
        turn = turn * 0.1
        turn = turn - jnp.floor(turn + 0.5)
        square = turn * turn
        cosine, sine = poly(COS_TURN, square), turn * poly(SIN_TURN, square)
        position = jnp.where(short < WARP_N, position, 1e4)
        return jnp.where(quantity == 0, position, jnp.where(quantity == 1, amplitude * cosine, amplitude * sine))

    weight = weight_ref[0]
    each = range(GROUP)

    def store_tile(slot, plane, value):
        for half in range(2):
            tiles[half, slot, plane] = value[half * SLAB : (half + 1) * SLAB].astype(BF16)

    def gather(half, position):
        value = None
        for source in range(3):
            slot = table_smem[3 * half + source, position]
            present = jnp.where(slot >= 0, 1.0, 0.0)
            at = within(slot, CELLS - 1)
            data = tiles[half, at] if source == 0 else beside[half][source - 1, at]
            term = data.astype(F32) * present
            value = term if value is None else value + term
        return value

    def find_slots():
        for half in range(2):
            for way in range(2):
                label_copy(half, way).wait()
            for source in range(3):
                lookup = label_ref[...] if source == 0 else label_in[half, source - 1]
                number = 3 * half + source
                found = jnp.zeros((1, 128), jnp.int32)
                for slot in range(CELLS):
                    same = lookup[slot : slot + 1] == wanted_ref[number : number + 1, :]
                    found = found + jnp.where(same, slot + 1, 0)
                table[number : number + 1, :] = found - 1
        to_smem = pltpu.make_async_copy(table, table_smem, local_sem)
        to_smem.start()
        to_smem.wait()

    def pass_on(half):
        for part in range(CELLS // GROUP):
            for way in range(2):
                early_copy(half, way, part).wait()

        def outgoing(part, carry):
            for way in range(2):
                for c in range(TC):
                    cell = part * TC + c
                    send[half, way, cell] = gather(half, 2 * CELLS * way + cell).astype(BF16)
                late_copy(half, way, part).start()
            return carry

        lax.fori_loop(0, TR, outgoing, 0)

    def work(step, carry):
        chosen = [within(order_smem[0, step * GROUP + g], 2 * CELLS - 1) for g in each]
        half_img, half_cov, lt = [], [], []
        for g in each:
            t = chosen[g]
            first_row, first_col = anchor_ref[0, t], anchor_ref[1, t]
            row16 = within(first_row // 16, (768 - WIN) // 16)
            col64 = within(first_col // 64, (768 - WIN) // 64)
            off_r = first_row - row16 * 16
            off_c = first_col - col64 * 64
            par = within(col64 % 2, 1)
            pair = within(col64 // 2, 4)
            s_img, s_cov = (
                jnp.concatenate(
                    [
                        jnp.concatenate([planes[par, plane, pair + j, row16 + i] for i in range(16)], axis=0)
                        for j in range(2)
                    ],
                    axis=1,
                )
                for plane in range(2)
            )
            q0 = jnp.transpose(warp_rows(frac_ref[0, t], scale_ref[0, t], off_r))[:ROWS]
            d0 = (lane - off_r).astype(F32) - q0[:, 0:1]
            l0 = lanczos(d0, q0[:, 1:2], q0[:, 2:3], along_ref[0:1, :], along_ref[1:2, :])
            q1 = warp_rows(frac_ref[1, t], scale_ref[1, t], off_c)
            d1 = (sub - off_c).astype(F32) - q1[0:1, :]
            cosd = jnp.concatenate([down_ref[0], down_ref[0]], axis=1)
            sind = jnp.concatenate([down_ref[1], down_ref[1]], axis=1)
            lt.append(lanczos(d1, q1[1:2, :], q1[2:3, :], cosd, sind))
            half_img.append(dot(l0, s_img).astype(BF16))
            half_cov.append(dot(l0[:TILE], s_cov).astype(BF16))
        warped = [dot(half_img[g], lt[g]).astype(BF16) for g in each]
        for g in each:
            coverage = dot(half_cov[g], lt[g][:, :TILE])
            store_tile(step * GROUP + g, 1, weight * coverage)
        x1 = dot(jnp.concatenate(warped, axis=0), cols_ref[...]).astype(BF16)
        x2 = [dot(rows_ref[...], x1[g * ROWS : (g + 1) * ROWS]) for g in each]
        k1 = dot(jnp.concatenate([kern_ref[chosen[g]] for g in each], axis=0), kcols_ref[...])
        k1h = k1.astype(BF16)
        k1l = (k1 - k1h.astype(F32)).astype(BF16)
        z = []
        for g in each:
            h, l = k1h[g * 48 : g * 48 + 48], k1l[g * 48 : g * 48 + 48]
            k2 = dot(krows_ref[...], jnp.concatenate([h, l, h], axis=0))
            x = x2[g]
            xrr, xri, xir, xii = x[:HALF, :128], x[:HALF, 128:], x[HALF:, :128], x[HALF:, 128:]
            krr, kri, kir, kii = k2[:HALF, :128], k2[:HALF, 128:], k2[HALF:, :128], k2[HALF:, 128:]
            xpr, xpi, xmr, xmi = xrr - xii, xir + xri, xrr + xii, xir - xri
            kpr, kpi, kmr, kmi = krr - kii, kir + kri, krr + kii, kir - kri
            ppr, ppi = xpr * kpr - xpi * kpi, xpr * kpi + xpi * kpr
            pmr, pmi = xmr * kmr - xmi * kmi, xmr * kmi + xmi * kmr
            top = jnp.concatenate([ppr + pmr, ppi - pmi], axis=1)
            bottom = jnp.concatenate([ppi + pmi, pmr - ppr], axis=1)
            z.append(jnp.concatenate([top, bottom], axis=0).astype(BF16))
        y = dot(jnp.concatenate(z, axis=0), icols_ref[...])
        y = y[:, :TILE] + y[:, TILE:]
        yh = y.astype(BF16)
        yl = (y - yh.astype(F32)).astype(BF16)
        ycat = jnp.concatenate([yh, yl], axis=1)
        for g in each:
            o = dot(irows_ref[...], ycat[g * ROWS : (g + 1) * ROWS])
            matched = o[:TILE, :TILE] + (o[:TILE, TILE:] + o[TILE:, :TILE])
            store_tile(step * GROUP + g, 0, weight * matched)

        @pl.when(step == 0)
        def _():
            pl.semaphore_wait(barrier, len(around))
            for half in range(2):
                for way in range(2):
                    label_copy(half, way).start()

        @pl.when(step < CELLS // GROUP)
        def _():
            for half in range(2):
                for way in range(2):
                    early_copy(half, way, step).start()

        @pl.when(step == 4)
        def _():
            find_slots()
            pass_on(1)

        @pl.when(step == 6)
        def _():
            pass_on(0)

        return carry

    lax.fori_loop(0, 2 * CELLS // GROUP, work, 0)

    def staying(cell, carry):
        for half in range(2):
            total[half, cell] = gather(half, CELLS + cell) + tiles[half, CELLS + cell].astype(F32)
        return carry

    lax.fori_loop(0, CELLS, staying, 0)

    lane = lax.broadcasted_iota(jnp.int32, (PAD, TILE), 1)

    def send_edges(part):
        for way in range(2):
            cols = slice(SPAN - TILE, SPAN) if way == 0 else slice(0, TILE)
            packed = jnp.zeros((PAD, TILE), F32)
            for q in range(4):
                row = TOP + part * TILE + q * PAD
                end = out_ref[row : row + PAD, cols]
                turn = (PAD * q + (PAD if way == 0 else 0)) % TILE
                moved = end if turn == 0 else pltpu.roll(end, turn, 1)
                packed = jnp.where((lane >= PAD * q) & (lane < PAD * (q + 1)), moved, packed)
            edge_send[way, part] = packed
            edge_copy(way, part).start()

    def unpack_edges(part):
        for way in range(2):
            edge_copy(way, part).wait()
        from_left, from_right = edge_recv[0, part] * has_left, edge_recv[1, part] * has_right
        for q in range(4):
            turn = (TILE - PAD * q) % TILE
            near = from_right if turn == 0 else pltpu.roll(from_right, turn, 1)
            turn = (TILE - PAD - PAD * q) % TILE
            far = from_left if turn == 0 else pltpu.roll(from_left, turn, 1)
            row = TOP + part * TILE + q * PAD
            out_ref[row : row + PAD, SPAN:] = jnp.where(lane < PAD, near, jnp.where(lane >= TILE - PAD, far, 0.0))

    def unpack_rim(way):
        for copy in rim_copies(way):
            copy.wait()
        rows = slice(TOP + SPAN, TALL - 8) if way == 0 else slice(8, TOP)
        factor = has_below if way == 0 else has_above
        out_ref[rows, :SPAN] = rim_recv[way] * factor
        near = corner_recv[2 * way] * (has_right * factor)
        far = corner_recv[2 * way + 1] * (has_left * factor)
        out_ref[rows, SPAN:] = jnp.where(lane < PAD, near, jnp.where(lane >= TILE - PAD, far, 0.0))

    for part in range(TR):
        if part == TR - 1:
            blank = jnp.zeros((8, WIDE), F32)
            out_ref[0:8, :] = blank
            out_ref[TALL - 8 : TALL, :] = blank
            unpack_edges(0)
            unpack_edges(TR - 1)
            for way in range(2):
                unpack_rim(way)
        for half in range(2):
            for way in range(2):
                late_copy(half, way, part).wait()
            for place in range(part * TC, (part + 1) * TC):
                row = TOP + PLACES[place] // TC * TILE + half * SLAB
                col = PLACES[place] % TC * TILE
                value = total[half, place] + (recv[half, 0, place].astype(F32) + recv[half, 1, place].astype(F32))
                out_ref[row : row + SLAB, col : col + TILE] = value[0] / (jnp.maximum(value[1], 0.0) + 1.0)
        if part < 2:
            for copy in rim_copies(part):
                copy.start()
            send_edges(part * (TR - 1))
        if part == 2:
            send_edges(1)
            send_edges(2)

    unpack_edges(1)
    unpack_edges(2)


def coaddition_call(dest, offset, anchor, frac, scale, weight, image, mask, psf, consts):
    scalars = (dest, offset, anchor, frac, scale, weight)
    fixed = (jnp.asarray(wanted_labels()),) + tuple(consts)
    dma = pltpu.SemaphoreType.DMA
    slab = (2, SLAB, TILE)
    parts = CELLS // GROUP
    return pl.pallas_call(
        coaddition_kernel,
        in_specs=[pl.BlockSpec(memory_space=pltpu.SMEM)] * len(scalars)
        + [pl.BlockSpec(memory_space=pl.ANY)] * (3 + len(fixed)),
        out_specs=pl.BlockSpec(memory_space=pltpu.VMEM),
        out_shape=pltpu.VMEM((TALL, WIDE), F32),
        scratch_shapes=[pltpu.VMEM(a.shape, a.dtype) for a in fixed]
        + [
            pltpu.VMEM((768, 768), BF16),
            pltpu.VMEM((768, 768), jnp.int32),
            pltpu.VMEM(psf.shape, BF16),
            pltpu.VMEM((48 * 2 * CELLS, 128), F32),
            pltpu.VMEM((2 * CELLS, 48, 128), BF16),
            pltpu.VMEM((CELLS, 128), jnp.int32),
            pltpu.VMEM((8, 128), jnp.int32),
            pltpu.SMEM((8, 128), jnp.int32),
            pltpu.VMEM((2, 2, 6, 48, 16, 128), BF16),
            pltpu.VMEM((2, 2 * CELLS) + slab, BF16),
            pltpu.VMEM((2, CELLS) + slab, BF16),
            pltpu.VMEM((2, CELLS) + slab, BF16),
            pltpu.VMEM((2, 2, CELLS, 128), jnp.int32),
            pltpu.VMEM((8, 128), jnp.int32),
            pltpu.SMEM((8, 128), jnp.int32),
            pltpu.VMEM((2, 2, CELLS) + slab, BF16),
            pltpu.VMEM((2, 2, CELLS) + slab, BF16),
            pltpu.VMEM((2, CELLS) + slab, F32),
            pltpu.VMEM((2, TR, PAD, TILE), F32),
            pltpu.VMEM((2, TR, PAD, TILE), F32),
            pltpu.VMEM((2, PAD, SPAN), F32),
            pltpu.VMEM((4, PAD, TILE), F32),
            dma((2, 2, parts)), dma((2, 2, parts)), dma((2, 2)), dma((2, 2)), dma((2, 2, TR)), dma((2, 2, TR)),
            dma((2, TR)), dma((2, TR)), dma((2, 3)), dma((2, 3)), dma(()), dma((2, LOADS)), dma(()), dma((len(fixed),)),
        ],
        compiler_params=pltpu.CompilerParams(
            vmem_limit_bytes=56 * 2**20, collective_id=0, has_side_effects=True
        ),
    )(*scalars, image, mask, psf, *fixed)


LEVEL_ROWS = ((8, 584), (16, 576), (24, 568), (40, 552))
BLOCK = 256
WAVE = 192


def starlet_kernel(edge_ref, first_ref, details_ref, smooth_ref, ping, pong, band, done, sem):
    top, bottom, left, right = (edge_ref[i] for i in range(4))
    tiles = WIDE // 128
    zero = jnp.zeros((8, WIDE), F32)
    for ref in (ping, pong):
        ref[0:8, :] = zero
        ref[TALL - 8 : TALL, :] = zero
    offset = lax.broadcasted_iota(jnp.int32, (512, 256), 0) - lax.broadcasted_iota(jnp.int32, (512, 256), 1) - 128
    offset = jnp.abs(offset)
    for k in range(SCALES):
        s = 2**k
        tap = jnp.where(offset == 0, 6.0, jnp.where(offset == s, 4.0, jnp.where(offset == 2 * s, 1.0, 0.0)))
        band[k] = (tap * (1.0 / 256.0)).astype(BF16)

    source = first_ref
    copies = []
    for k in range(SCALES):
        s = 2**k
        target = (ping, pong)[k % 2]
        begin, end = LEVEL_ROWS[k]

        def down(view, count, at=16, s=s):
            def near(by):
                return view[at + by : at + by + count, :]

            center = near(0)
            return center, (near(-2 * s) + near(2 * s)) + 4.0 * (near(-s) + near(s)) + 6.0 * center

        def across(rows, s=s):
            count = rows.shape[0]
            parts = [rows[:, 128 * j : 128 * (j + 1)] for j in range(tiles)]
            lane = lax.broadcasted_iota(jnp.int32, (count, 128), 1)

            def after(by):
                turned = [pltpu.roll(part, by, 1) for part in parts]
                return [jnp.where(lane < by, turned[j - 1], turned[j]) for j in range(tiles)]

            def before(by):
                turned = [pltpu.roll(part, 128 - by, 1) for part in parts]
                return [jnp.where(lane >= 128 - by, turned[(j + 1) % tiles], turned[j]) for j in range(tiles)]

            a, b, c, d = after(2 * s), before(2 * s), after(s), before(s)
            return [((a[j] + b[j]) + 4.0 * (c[j] + d[j]) + 6.0 * parts[j]) * (1.0 / 256.0) for j in range(tiles if s < 8 else tiles - 1)]

        def across_product(rows, k=k):
            high = rows.astype(BF16)
            low = (rows - high.astype(F32)).astype(BF16)
            full = []
            for first, count in ((0, 2), (2, 2), (4, 1))[: 3 if k < SCALES - 1 else 2]:
                total = None
                for part in (high, low):
                    pieces = [part[:, 128 * (j % tiles) : 128 * (j % tiles) + 128] for j in range(first - 1, first + count + 1)]
                    weights = band[k] if count == 2 else band[k, :384, :128]
                    term = lax.dot_general(
                        jnp.concatenate(pieces, axis=1), weights, (((1,), (0,)), ((), ())), preferred_element_type=F32
                    )
                    total = term if total is None else total + term
                full += [total[:, 128 * j : 128 * j + 128] for j in range(count)]
            return full

        def store(row, full, factor, target=target):
            count = full[0].shape[0]
            lane = lax.broadcasted_iota(jnp.int32, (count, 128), 1)
            side = jnp.where(lane < 64, right, left)
            for j in range(tiles):
                value = full[j] * side if j == tiles - 1 else full[j]
                value = value if factor is None else value * factor
                target[pl.ds(row, count), 128 * j : 128 * (j + 1)] = value

        if k < SCALES - 1:
            for row, last, factor in ((begin, TOP, top), (TOP + SPAN, end, bottom)):
                low, high = max(row - 16, 0), min(last + 16, TALL)
                count = last - row
                rows = source[low:high, :]
                if low > row - 16:
                    rows = jnp.concatenate([jnp.zeros((low - row + 16, WIDE), F32), rows], axis=0)
                if high < last + 16:
                    rows = jnp.concatenate([rows, jnp.zeros((last + 16 - high, WIDE), F32)], axis=0)
                store(row, across(down(rows, count)[1]), factor)

        def one(block, carry, k=k, source=source, down=down, across=across, store=store, across_product=across_product):
            row = pl.multiple_of(TOP + block * BLOCK, 8)
            here = pl.multiple_of(block * BLOCK, 8)
            view = source.at[pl.ds(pl.multiple_of(row - 16, 8), BLOCK + 32), :]
            spans = [(0, BLOCK - WAVE, across), (BLOCK - WAVE, WAVE, across_product)]
            for start, count, method in spans:
                center, rows = down(view, count, 16 + start)
                full = method(rows)
                if k < SCALES - 1:
                    store(pl.multiple_of(row + start, 8), full, None)
                at = pl.ds(pl.multiple_of(here + start, 8), count)
                for j in range(SPAN // 128):
                    cols = slice(128 * j, 128 * (j + 1))
                    done[k, at, cols] = center[:, cols] - full[j]
                    if k == SCALES - 1:
                        done[SCALES, at, cols] = full[j]
            return carry

        half = SPAN // BLOCK // 2
        for number in range(2):
            lax.fori_loop(number * half, (number + 1) * half, one, 0)
            rows = pl.ds(number * SPAN // 2, SPAN // 2)
            copies.append(pltpu.make_async_copy(done.at[k, rows], details_ref.at[k, rows], sem.at[2 * k + number]))
            if k == SCALES - 1:
                copies.append(pltpu.make_async_copy(done.at[SCALES, rows], smooth_ref.at[rows], sem.at[2 * SCALES + number]))
                copies[-1].start()
                copies[-2].start()
            else:
                copies[-1].start()
        source = target
    for copy in copies:
        copy.wait()


def starlet_call(edges, first):
    return pl.pallas_call(
        starlet_kernel,
        in_specs=[pl.BlockSpec(memory_space=pltpu.SMEM), pl.BlockSpec(memory_space=pltpu.VMEM)],
        out_specs=[pl.BlockSpec(memory_space=pltpu.HBM)] * 2,
        out_shape=[
            jax.ShapeDtypeStruct((SCALES, SPAN, SPAN), F32),
            jax.ShapeDtypeStruct((SPAN, SPAN), F32),
        ],
        scratch_shapes=[
            pltpu.VMEM((TALL, WIDE), F32),
            pltpu.VMEM((TALL, WIDE), F32),
            pltpu.VMEM((SCALES, 512, 256), BF16),
            pltpu.VMEM((SCALES + 1, SPAN, SPAN), F32),
            pltpu.SemaphoreType.DMA((2 * SCALES + 2,)),
        ],
        compiler_params=pltpu.CompilerParams(vmem_limit_bytes=40 * 2**20),
    )(edges, first)


def shards(image, mask, weight, anchor, frac, scale, kernels, dest, offset):
    first = coaddition_call(
        dest, offset, anchor[0].T, frac[0].T, scale[0].T, weight, image, mask, kernels[0].transpose(1, 0, 2), constants()
    )
    band, patch = lax.axis_index("band"), lax.axis_index("patch")
    edges = jnp.stack(
        [band > 0, band < lax.axis_size("band") - 1, patch > 0, patch < lax.axis_size("patch") - 1]
    ).astype(F32)
    return tuple(starlet_call(edges, first))


def solution(mesh):
    owner = ("patch", "band")
    in_specs = (
        P(owner, None, None),
        P(owner, None, None),
        P(owner),
        P(owner, None, None),
        P(owner, None, None),
        P(owner, None, None),
        P(owner, None, None, None),
        P(owner, None),
        P(owner, None),
    )
    out_specs = (P(None, "band", "patch"), P("band", "patch"))
    return jax.shard_map(shards, mesh=mesh, in_specs=in_specs, out_specs=out_specs, check_vma=False)
```

```python
import math
import numpy as np
import ml_dtypes
import jax
import jax.numpy as jnp
from jax import lax
from jax.experimental import pallas as pl
from jax.experimental.pallas import tpu as pltpu
from jax.sharding import PartitionSpec as P

TILE, KS, SCALES, TR, TC, MARGIN, WARP_N, SRC_N = 128, 41, 4, 4, 4, 20, 168, 184
ROWS = 176
HALF = 88
WIN = 256
F32, BF16 = jnp.float32, jnp.bfloat16


def split_bf16(values):
    high = values.astype(ml_dtypes.bfloat16)
    low = (values - high.astype(np.float64)).astype(ml_dtypes.bfloat16)
    return high, low


def spectra():
    bins = np.arange(WARP_N // 2 + 1)

    def forward(points, sign):
        angle = 2.0 * np.pi / WARP_N * np.outer(bins, points)
        return np.cos(angle), sign * np.sin(angle)

    order = (np.arange(WARP_N) + MARGIN) % WARP_N
    real, imag = forward(order, -1.0)
    rows = np.zeros((ROWS, WIN))
    rows[: len(bins), :WARP_N] = real
    rows[HALF : HALF + len(bins), :WARP_N] = imag
    cols = np.zeros((WIN, WIN))
    cols[:WARP_N, : len(bins)] = real.T
    cols[:WARP_N, 128 : 128 + len(bins)] = imag.T
    real, imag = forward(np.arange(KS), 1.0)
    kcols = np.zeros((64, WIN))
    kcols[:KS, : len(bins)] = real.T
    kcols[:KS, 128 : 128 + len(bins)] = imag.T
    krows = np.zeros((ROWS, 48))
    krows[: len(bins), :KS] = real
    krows[HALF : HALF + len(bins), :KS] = imag
    count = np.full(len(bins), 2.0)
    count[0] = count[-1] = 1.0
    angle = 2.0 * np.pi / WARP_N * np.outer(np.arange(TILE), bins)
    back_real = np.cos(angle) * count / WARP_N
    back_imag = -np.sin(angle) * count / WARP_N
    icols = np.zeros((WIN, TILE))
    icols[: len(bins)] = back_real.T
    icols[128 : 128 + len(bins)] = back_imag.T
    irows = np.zeros((TILE, ROWS))
    irows[:, : len(bins)] = 0.5 * back_real
    irows[:, HALF : HALF + len(bins)] = 0.5 * back_imag
    kcols_high, kcols_low = split_bf16(kcols)
    krows_high, krows_low = split_bf16(krows)
    icols_high, icols_low = split_bf16(icols)
    irows_high, irows_low = split_bf16(irows)
    rows_pad = rows[:, :ROWS]
    return (
        cols.astype(ml_dtypes.bfloat16),
        rows_pad.astype(ml_dtypes.bfloat16),
        np.concatenate([kcols_high, kcols_low]),
        np.concatenate([krows_high, krows_high, krows_low], axis=1),
        np.concatenate([icols_high, icols_low], axis=1),
        np.concatenate([irows_high, irows_low]),
    )


def phase_constants():
    j = np.arange(WIN)
    sign = 1.0 - 2.0 * (j % 2)
    cosine = (sign * np.cos(np.pi * j / 5.0)).astype(np.float32)
    sine = (sign * np.sin(np.pi * j / 5.0)).astype(np.float32)
    along = np.zeros((8, WIN), np.float32)
    along[0], along[1] = cosine, sine
    down = np.stack([np.repeat(cosine[:, None], 128, 1), np.repeat(sine[:, None], 128, 1)])
    return along, down


def poly(coefficients, x):
    total = jnp.full_like(x, coefficients[-1])
    for value in coefficients[-2::-1]:
        total = total * x + value
    return total


SIN_PI = (3.14159265, -5.16771276, 2.55016332, -0.5992522, 0.0820504, -0.00702839)
SIN_TURN = (6.28318531, -41.34170222, 81.60524742, -76.70580022, 42.05775402, -15.08656526, 3.78131888, -0.62077872)
COS_TURN = (1.0, -19.73920874, 64.93938908, -85.45665831, 60.24213134, -26.40466819, 7.80013144, -1.45311232)


def lanczos(d, cos_row, sin_row, cos_col, sin_col):
    d2 = d * d
    u = cos_row * sin_col - sin_row * cos_col
    g = u / d2
    g = jnp.where(d2 < 1e-5, 1.0, g)
    return jnp.where(d2 < 25.0, g, 0.0).astype(BF16)


def dot(a, b):
    return lax.dot_general(a, b, (((1,), (0,)), ((), ())), preferred_element_type=F32)


def constants():
    along, down = phase_constants()
    return [jnp.asarray(a) for a in (along, down) + spectra()]


CELLS = TR * TC
GROUP = 4
LOADS = 3
SLAB = TILE // 2
SPAN = TR * TILE
PAD = 32
WIDE = SPAN + 128
TOP = 8 + PAD
TALL = SPAN + 2 * TOP
MESH = pl.DeviceIdType.MESH


def within(value, top):
    return jnp.minimum(jnp.maximum(value, 0), top)


def whole(a):
    return pl.BlockSpec(a.shape, lambda *_: (0,) * a.ndim)


PLACES = (0, 1, 2, 3, 12, 13, 14, 15, 4, 7, 8, 11, 5, 6, 9, 10)


def wanted_labels():
    lanes = np.arange(128)
    cell = np.asarray(PLACES)[lanes % CELLS]
    rows = np.full((8, 128), -1, np.int32)
    for source, step in enumerate((1, 2, 0)):
        rows[source] = (3 * (lanes // CELLS) + step) * CELLS + cell + 1
        rows[3 + source] = (3 * step + lanes // CELLS) * CELLS + cell + 1
    rows = np.where(lanes < 3 * CELLS, rows, -1).astype(np.int32)
    rows[6] = np.where(lanes < CELLS, lanes, np.where(lanes < 2 * CELLS, 64 + cell, -1))
    return rows


def coaddition_kernel(
    dest_ref, offset_ref, anchor_ref, frac_ref, scale_ref, weight_ref,
    image_hbm, mask_hbm, psf_hbm, wanted_hbm,
    along_hbm, down_hbm, cols_hbm, rows_hbm, kcols_hbm, krows_hbm, icols_hbm, irows_hbm,
    out_ref,
    wanted_ref, along_ref, down_ref, cols_ref, rows_ref, kcols_ref, krows_ref, icols_ref, irows_ref,
    image, mask, psf, taps_wide, kern_ref, label_ref, order, order_smem, planes, tiles, upper_in, lower_in, label_in, table, table_smem, send, recv, total, edge_send, edge_recv, rim_recv, corner_recv,
    early_send_sem, early_recv_sem, label_send_sem, label_recv_sem, late_send_sem, late_recv_sem,
    edge_send_sem, edge_recv_sem, rim_send_sem, rim_recv_sem, local_sem, load_sem, psf_sem, constant_sem,
):
    psf_copy = pltpu.make_async_copy(psf_hbm, psf, psf_sem)
    constant_copies = [
        pltpu.make_async_copy(source, target, constant_sem.at[number])
        for number, (source, target) in enumerate(
            (
                (wanted_hbm, wanted_ref),
                (along_hbm, along_ref),
                (down_hbm, down_ref),
                (cols_hbm, cols_ref),
                (rows_hbm, rows_ref),
                (kcols_hbm, kcols_ref),
                (krows_hbm, krows_ref),
                (icols_hbm, icols_ref),
                (irows_hbm, irows_ref),
            )
        )
    ]
    constant_copies[0].start()
    psf_copy.start()
    loads = []
    for number in range(LOADS):
        rows = pl.ds(number * (768 // LOADS), 768 // LOADS)
        for kind, (source, target) in enumerate(((image_hbm, image), (mask_hbm, mask))):
            loads.append(pltpu.make_async_copy(source.at[0, rows], target.at[rows], load_sem.at[kind, number]))
    for load in loads:
        load.start()
    for copy in constant_copies[1:]:
        copy.start()

    patch, band = lax.axis_index("patch"), lax.axis_index("band")
    n_patch, n_band = lax.axis_size("patch"), lax.axis_size("band")
    left_patch, right_patch = lax.rem(patch + n_patch - 1, n_patch), lax.rem(patch + 1, n_patch)
    above_band, below_band = lax.rem(band + n_band - 1, n_band), lax.rem(band + 1, n_band)
    left, right = {"patch": left_patch, "band": band}, {"patch": right_patch, "band": band}
    above, below = {"patch": patch, "band": above_band}, {"patch": patch, "band": below_band}
    corners = [{"patch": p, "band": b} for b in (above_band, below_band) for p in (left_patch, right_patch)]
    has_left = jnp.where(patch > 0, 1.0, 0.0)
    has_right = jnp.where(patch < n_patch - 1, 1.0, 0.0)
    has_above = jnp.where(band > 0, 1.0, 0.0)
    has_below = jnp.where(band < n_band - 1, 1.0, 0.0)

    barrier = pltpu.get_barrier_semaphore()
    around = [left, right, above, below] + corners
    for device in around:
        pl.semaphore_signal(barrier, inc=1, device_id=device, device_id_type=MESH)

    def remote(src, dst, send_sem, recv_sem, device):
        return pltpu.make_async_remote_copy(
            src_ref=src, dst_ref=dst, send_sem=send_sem, recv_sem=recv_sem, device_id=device, device_id_type=MESH
        )

    beside = (upper_in, lower_in)

    early_to = ((right, left), (below, above))
    late_to = ((above, below), (left, right))

    def label_copy(half, way):
        return remote(
            label_ref,
            label_in.at[half, way],
            label_send_sem.at[half, way],
            label_recv_sem.at[half, way],
            early_to[half][way],
        )

    def early_copy(half, way, part):
        piece = pl.ds(part * GROUP, GROUP)
        return remote(
            tiles.at[half, piece],
            beside[half].at[way, piece],
            early_send_sem.at[half, way, part],
            early_recv_sem.at[half, way, part],
            early_to[half][way],
        )

    def late_copy(half, way, part):
        piece = pl.ds(part * TC, TC)
        return remote(
            send.at[half, way, piece],
            recv.at[half, way, piece],
            late_send_sem.at[half, way, part],
            late_recv_sem.at[half, way, part],
            late_to[half][way],
        )

    first_rows, last_rows = pl.ds(TOP, PAD), pl.ds(TOP + SPAN - PAD, PAD)

    def edge_copy(way, part):
        return remote(
            edge_send.at[way, part],
            edge_recv.at[way, part],
            edge_send_sem.at[way, part],
            edge_recv_sem.at[way, part],
            early_to[0][way],
        )

    def rim_copies(way):
        rows = (first_rows, last_rows)[way]
        triples = [(pl.ds(0, SPAN), rim_recv.at[way], late_to[0][way])]
        for side in range(2):
            cols = pl.ds(0, TILE) if side == 0 else pl.ds(SPAN - TILE, TILE)
            triples.append((cols, corner_recv.at[2 * way + side], corners[2 * way + side]))
        return [
            remote(out_ref.at[rows, cols], target, rim_send_sem.at[way, number], rim_recv_sem.at[way, number], device)
            for number, (cols, target, device) in enumerate(triples)
        ]

    constant_copies[0].wait()
    filled = jnp.int32(0)
    key_of = wanted_ref[6:7, :]
    sub = lax.broadcasted_iota(jnp.int32, (CELLS, 128), 0)
    sequence = jnp.zeros((1, 128), jnp.int32)
    labels = jnp.zeros((CELLS, 128), jnp.int32)
    for i in range(2 * CELLS):
        code, cell = dest_ref[0, i], offset_ref[0, i]
        away = code != 4
        key = jnp.where(away, filled, 64 + cell)
        sequence = jnp.where(key_of == key, i, sequence)
        labels = jnp.where(sub == key, code * CELLS + cell + 1, labels)
        filled = filled + away.astype(jnp.int32)
    order[...] = jnp.broadcast_to(sequence, (8, 128))
    label_ref[...] = labels
    order_copy = pltpu.make_async_copy(order, order_smem, local_sem)
    order_copy.start()

    psf_copy.wait()
    gap = jnp.zeros((2 * CELLS, 64 - KS), F32)
    for r in range(KS):
        tap = psf[r].astype(F32)
        taps_wide[2 * CELLS * r : 2 * CELLS * (r + 1), :] = jnp.concatenate([tap, gap, tap, gap], axis=1)
    taps_wide[2 * CELLS * KS :, :] = jnp.zeros((2 * CELLS * (48 - KS), 128), F32)
    for t in range(2 * CELLS):
        kern_ref[t] = taps_wide[pl.ds(t, 48, stride=2 * CELLS), :].astype(BF16)

    def prepare(block, carry):
        rows = pl.ds(pl.multiple_of(block * 64, 64), 64)
        usable = jnp.where((mask[rows, :] & 7) != 7, 1.0, 0.0).astype(BF16)
        masked = image[rows, :] * usable
        for plane, value in enumerate((masked, usable)):
            moved = jnp.concatenate([value[:, 64:], value[:, :64]], axis=1)
            for way, data in enumerate((value, moved)):
                for j in range(6):
                    for i in range(4):
                        planes[way, plane, j, block * 4 + i] = data[16 * i : 16 * i + 16, 128 * j : 128 * j + 128]
        return carry

    steps = 768 // 64 // LOADS
    for number in range(LOADS):
        for load in loads[2 * number : 2 * number + 2]:
            load.wait()
        lax.fori_loop(number * steps, (number + 1) * steps, prepare, 0)
    order_copy.wait()
    for copy in constant_copies[1:]:
        copy.wait()

    lane = lax.broadcasted_iota(jnp.int32, (ROWS, WIN), 1)
    sub = lax.broadcasted_iota(jnp.int32, (WIN, WIN), 0)
    short = lax.broadcasted_iota(jnp.int32, (8, WIN), 1)
    quantity = lax.broadcasted_iota(jnp.int32, (8, WIN), 0)
    index = (short + jnp.where(short < WARP_N - MARGIN, MARGIN, MARGIN - WARP_N)).astype(F32)

    def warp_rows(fraction, stretch, shift):
        position = (5.0 + fraction) + index * (1.0 + stretch)
        nearest = jnp.floor(position + 0.5)
        odd = nearest - 2.0 * jnp.floor(nearest * 0.5)
        part = position - nearest
        sine = (1.0 - 2.0 * odd) * part * poly(SIN_PI, part * part)
        sign = (1 - 2 * (shift & 1)).astype(F32)
        amplitude = ((-5.0 / math.pi**2) * sign) * sine
        turn = position - 10.0 * jnp.floor(position * 0.1) + lax.rem(shift, 10).astype(F32)
        turn = turn * 0.1
        turn = turn - jnp.floor(turn + 0.5)
        square = turn * turn
        cosine, sine = poly(COS_TURN, square), turn * poly(SIN_TURN, square)
        position = jnp.where(short < WARP_N, position, 1e4)
        return jnp.where(quantity == 0, position, jnp.where(quantity == 1, amplitude * cosine, amplitude * sine))

    weight = weight_ref[0]
    each = range(GROUP)

    def store_tile(slot, plane, value):
        for half in range(2):
            tiles[half, slot, plane] = value[half * SLAB : (half + 1) * SLAB].astype(BF16)

    def gather(half, position):
        value = None
        for source in range(3):
            slot = table_smem[3 * half + source, position]
            present = jnp.where(slot >= 0, 1.0, 0.0)
            at = within(slot, CELLS - 1)
            data = tiles[half, at] if source == 0 else beside[half][source - 1, at]
            term = data.astype(F32) * present
            value = term if value is None else value + term
        return value

    def find_slots():
        for half in range(2):
            for way in range(2):
                label_copy(half, way).wait()
            for source in range(3):
                lookup = label_ref[...] if source == 0 else label_in[half, source - 1]
                number = 3 * half + source
                found = jnp.zeros((1, 128), jnp.int32)
                for slot in range(CELLS):
                    same = lookup[slot : slot + 1] == wanted_ref[number : number + 1, :]
                    found = found + jnp.where(same, slot + 1, 0)
                table[number : number + 1, :] = found - 1
        to_smem = pltpu.make_async_copy(table, table_smem, local_sem)
        to_smem.start()
        to_smem.wait()

    def pass_on(half):
        for part in range(CELLS // GROUP):
            for way in range(2):
                early_copy(half, way, part).wait()

        def outgoing(part, carry):
            for way in range(2):
                for c in range(TC):
                    cell = part * TC + c
                    send[half, way, cell] = gather(half, 2 * CELLS * way + cell).astype(BF16)
                late_copy(half, way, part).start()
            return carry

        lax.fori_loop(0, TR, outgoing, 0)

    def work(step, carry):
        chosen = [within(order_smem[0, step * GROUP + g], 2 * CELLS - 1) for g in each]
        half_img, half_cov, lt = [], [], []
        for g in each:
            t = chosen[g]
            first_row, first_col = anchor_ref[0, t], anchor_ref[1, t]
            row16 = within(first_row // 16, (768 - WIN) // 16)
            col64 = within(first_col // 64, (768 - WIN) // 64)
            off_r = first_row - row16 * 16
            off_c = first_col - col64 * 64
            par = within(col64 % 2, 1)
            pair = within(col64 // 2, 4)
            s_img, s_cov = (
                jnp.concatenate(
                    [
                        jnp.concatenate([planes[par, plane, pair + j, row16 + i] for i in range(16)], axis=0)
                        for j in range(2)
                    ],
                    axis=1,
                )
                for plane in range(2)
            )
            q0 = jnp.transpose(warp_rows(frac_ref[0, t], scale_ref[0, t], off_r))[:ROWS]
            d0 = (lane - off_r).astype(F32) - q0[:, 0:1]
            l0 = lanczos(d0, q0[:, 1:2], q0[:, 2:3], along_ref[0:1, :], along_ref[1:2, :])
            q1 = warp_rows(frac_ref[1, t], scale_ref[1, t], off_c)
            d1 = (sub - off_c).astype(F32) - q1[0:1, :]
            cosd = jnp.concatenate([down_ref[0], down_ref[0]], axis=1)
            sind = jnp.concatenate([down_ref[1], down_ref[1]], axis=1)
            lt.append(lanczos(d1, q1[1:2, :], q1[2:3, :], cosd, sind))
            half_img.append(dot(l0, s_img).astype(BF16))
            half_cov.append(dot(l0[:TILE], s_cov).astype(BF16))
        warped = [dot(half_img[g], lt[g]).astype(BF16) for g in each]
        for g in each:
            coverage = dot(half_cov[g], lt[g][:, :TILE])
            store_tile(step * GROUP + g, 1, weight * coverage)
        x1 = dot(jnp.concatenate(warped, axis=0), cols_ref[...]).astype(BF16)
        x2 = [dot(rows_ref[...], x1[g * ROWS : (g + 1) * ROWS]) for g in each]
        k1 = dot(jnp.concatenate([kern_ref[chosen[g]] for g in each], axis=0), kcols_ref[...])
        k1h = k1.astype(BF16)
        k1l = (k1 - k1h.astype(F32)).astype(BF16)
        z = []
        for g in each:
            h, l = k1h[g * 48 : g * 48 + 48], k1l[g * 48 : g * 48 + 48]
            k2 = dot(krows_ref[...], jnp.concatenate([h, l, h], axis=0))
            x = x2[g]
            xrr, xri, xir, xii = x[:HALF, :128], x[:HALF, 128:], x[HALF:, :128], x[HALF:, 128:]
            krr, kri, kir, kii = k2[:HALF, :128], k2[:HALF, 128:], k2[HALF:, :128], k2[HALF:, 128:]
            xpr, xpi, xmr, xmi = xrr - xii, xir + xri, xrr + xii, xir - xri
            kpr, kpi, kmr, kmi = krr - kii, kir + kri, krr + kii, kir - kri
            ppr, ppi = xpr * kpr - xpi * kpi, xpr * kpi + xpi * kpr
            pmr, pmi = xmr * kmr - xmi * kmi, xmr * kmi + xmi * kmr
            top = jnp.concatenate([ppr + pmr, ppi - pmi], axis=1)
            bottom = jnp.concatenate([ppi + pmi, pmr - ppr], axis=1)
            z.append(jnp.concatenate([top, bottom], axis=0).astype(BF16))
        y = dot(jnp.concatenate(z, axis=0), icols_ref[...])
        y = y[:, :TILE] + y[:, TILE:]
        yh = y.astype(BF16)
        yl = (y - yh.astype(F32)).astype(BF16)
        ycat = jnp.concatenate([yh, yl], axis=1)
        for g in each:
            o = dot(irows_ref[...], ycat[g * ROWS : (g + 1) * ROWS])
            matched = o[:TILE, :TILE] + (o[:TILE, TILE:] + o[TILE:, :TILE])
            store_tile(step * GROUP + g, 0, weight * matched)

        @pl.when(step == 0)
        def _():
            pl.semaphore_wait(barrier, len(around))
            for half in range(2):
                for way in range(2):
                    label_copy(half, way).start()

        @pl.when(step < CELLS // GROUP)
        def _():
            for half in range(2):
                for way in range(2):
                    early_copy(half, way, step).start()

        @pl.when(step == 4)
        def _():
            find_slots()
            pass_on(1)

        @pl.when(step == 6)
        def _():
            pass_on(0)

        return carry

    lax.fori_loop(0, 2 * CELLS // GROUP, work, 0)

    def staying(cell, carry):
        for half in range(2):
            total[half, cell] = gather(half, CELLS + cell) + tiles[half, CELLS + cell].astype(F32)
        return carry

    lax.fori_loop(0, CELLS, staying, 0)

    lane = lax.broadcasted_iota(jnp.int32, (PAD, TILE), 1)

    def send_edges(part):
        for way in range(2):
            cols = slice(SPAN - TILE, SPAN) if way == 0 else slice(0, TILE)
            packed = jnp.zeros((PAD, TILE), F32)
            for q in range(4):
                row = TOP + part * TILE + q * PAD
                end = out_ref[row : row + PAD, cols]
                turn = (PAD * q + (PAD if way == 0 else 0)) % TILE
                moved = end if turn == 0 else pltpu.roll(end, turn, 1)
                packed = jnp.where((lane >= PAD * q) & (lane < PAD * (q + 1)), moved, packed)
            edge_send[way, part] = packed
            edge_copy(way, part).start()

    for part in range(TR):
        for half in range(2):
            for way in range(2):
                late_copy(half, way, part).wait()
            for place in range(part * TC, (part + 1) * TC):
                row = TOP + PLACES[place] // TC * TILE + half * SLAB
                col = PLACES[place] % TC * TILE
                value = total[half, place] + (recv[half, 0, place].astype(F32) + recv[half, 1, place].astype(F32))
                out_ref[row : row + SLAB, col : col + TILE] = value[0] / (jnp.maximum(value[1], 0.0) + 1.0)
        if part < 2:
            for copy in rim_copies(part):
                copy.start()
            send_edges(part * (TR - 1))
        if part == 2:
            send_edges(1)
            send_edges(2)

    blank = jnp.zeros((8, WIDE), F32)
    out_ref[0:8, :] = blank
    out_ref[TALL - 8 : TALL, :] = blank

    def unpack(part, carry):
        for way in range(2):
            edge_copy(way, part).wait()
        from_left, from_right = edge_recv[0, part] * has_left, edge_recv[1, part] * has_right
        for q in range(4):
            turn = (TILE - PAD * q) % TILE
            near = from_right if turn == 0 else pltpu.roll(from_right, turn, 1)
            turn = (TILE - PAD - PAD * q) % TILE
            far = from_left if turn == 0 else pltpu.roll(from_left, turn, 1)
            rows = pl.ds(pl.multiple_of(TOP + part * TILE + q * PAD, 8), PAD)
            out_ref[rows, SPAN:] = jnp.where(lane < PAD, near, jnp.where(lane >= TILE - PAD, far, 0.0))
        return carry

    lax.fori_loop(0, TR, unpack, 0)
    for way in range(2):
        for copy in rim_copies(way):
            copy.wait()
    for rows, arrived, far, near, factor in (
        (slice(8, TOP), 1, 3, 2, has_above),
        (slice(TOP + SPAN, TALL - 8), 0, 1, 0, has_below),
    ):
        out_ref[rows, :SPAN] = rim_recv[arrived] * factor
        near, far = corner_recv[near] * (has_right * factor), corner_recv[far] * (has_left * factor)
        out_ref[rows, SPAN:] = jnp.where(lane < PAD, near, jnp.where(lane >= TILE - PAD, far, 0.0))


def coaddition_call(dest, offset, anchor, frac, scale, weight, image, mask, psf, consts):
    scalars = (dest, offset, anchor, frac, scale, weight)
    fixed = (jnp.asarray(wanted_labels()),) + tuple(consts)
    dma = pltpu.SemaphoreType.DMA
    slab = (2, SLAB, TILE)
    parts = CELLS // GROUP
    return pl.pallas_call(
        coaddition_kernel,
        in_specs=[pl.BlockSpec(memory_space=pltpu.SMEM)] * len(scalars)
        + [pl.BlockSpec(memory_space=pl.ANY)] * (3 + len(fixed)),
        out_specs=pl.BlockSpec(memory_space=pltpu.VMEM),
        out_shape=pltpu.VMEM((TALL, WIDE), F32),
        scratch_shapes=[pltpu.VMEM(a.shape, a.dtype) for a in fixed]
        + [
            pltpu.VMEM((768, 768), BF16),
            pltpu.VMEM((768, 768), jnp.int32),
            pltpu.VMEM(psf.shape, BF16),
            pltpu.VMEM((48 * 2 * CELLS, 128), F32),
            pltpu.VMEM((2 * CELLS, 48, 128), BF16),
            pltpu.VMEM((CELLS, 128), jnp.int32),
            pltpu.VMEM((8, 128), jnp.int32),
            pltpu.SMEM((8, 128), jnp.int32),
            pltpu.VMEM((2, 2, 6, 48, 16, 128), BF16),
            pltpu.VMEM((2, 2 * CELLS) + slab, BF16),
            pltpu.VMEM((2, CELLS) + slab, BF16),
            pltpu.VMEM((2, CELLS) + slab, BF16),
            pltpu.VMEM((2, 2, CELLS, 128), jnp.int32),
            pltpu.VMEM((8, 128), jnp.int32),
            pltpu.SMEM((8, 128), jnp.int32),
            pltpu.VMEM((2, 2, CELLS) + slab, BF16),
            pltpu.VMEM((2, 2, CELLS) + slab, BF16),
            pltpu.VMEM((2, CELLS) + slab, F32),
            pltpu.VMEM((2, TR, PAD, TILE), F32),
            pltpu.VMEM((2, TR, PAD, TILE), F32),
            pltpu.VMEM((2, PAD, SPAN), F32),
            pltpu.VMEM((4, PAD, TILE), F32),
            dma((2, 2, parts)), dma((2, 2, parts)), dma((2, 2)), dma((2, 2)), dma((2, 2, TR)), dma((2, 2, TR)),
            dma((2, TR)), dma((2, TR)), dma((2, 3)), dma((2, 3)), dma(()), dma((2, LOADS)), dma(()), dma((len(fixed),)),
        ],
        compiler_params=pltpu.CompilerParams(
            vmem_limit_bytes=56 * 2**20, collective_id=0, has_side_effects=True
        ),
    )(*scalars, image, mask, psf, *fixed)


LEVEL_ROWS = ((8, 584), (16, 576), (24, 568), (40, 552))
BLOCK = 256
WAVE = 192


def starlet_kernel(edge_ref, first_ref, details_ref, smooth_ref, ping, pong, band, done, sem):
    top, bottom, left, right = (edge_ref[i] for i in range(4))
    tiles = WIDE // 128
    zero = jnp.zeros((8, WIDE), F32)
    for ref in (ping, pong):
        ref[0:8, :] = zero
        ref[TALL - 8 : TALL, :] = zero
    offset = lax.broadcasted_iota(jnp.int32, (512, 256), 0) - lax.broadcasted_iota(jnp.int32, (512, 256), 1) - 128
    offset = jnp.abs(offset)
    for k in range(SCALES):
        s = 2**k
        tap = jnp.where(offset == 0, 6.0, jnp.where(offset == s, 4.0, jnp.where(offset == 2 * s, 1.0, 0.0)))
        band[k] = (tap * (1.0 / 256.0)).astype(BF16)

    source = first_ref
    copies = []
    for k in range(SCALES):
        s = 2**k
        target = (ping, pong)[k % 2]
        begin, end = LEVEL_ROWS[k]

        def down(view, count, at=16, s=s):
            def near(by):
                return view[at + by : at + by + count, :]

            center = near(0)
            return center, (near(-2 * s) + near(2 * s)) + 4.0 * (near(-s) + near(s)) + 6.0 * center

        def across(rows, s=s):
            count = rows.shape[0]
            parts = [rows[:, 128 * j : 128 * (j + 1)] for j in range(tiles)]
            lane = lax.broadcasted_iota(jnp.int32, (count, 128), 1)

            def after(by):
                turned = [pltpu.roll(part, by, 1) for part in parts]
                return [jnp.where(lane < by, turned[j - 1], turned[j]) for j in range(tiles)]

            def before(by):
                turned = [pltpu.roll(part, 128 - by, 1) for part in parts]
                return [jnp.where(lane >= 128 - by, turned[(j + 1) % tiles], turned[j]) for j in range(tiles)]

            a, b, c, d = after(2 * s), before(2 * s), after(s), before(s)
            return [((a[j] + b[j]) + 4.0 * (c[j] + d[j]) + 6.0 * parts[j]) * (1.0 / 256.0) for j in range(tiles if s < 8 else tiles - 1)]

        def across_product(rows, k=k):
            high = rows.astype(BF16)
            low = (rows - high.astype(F32)).astype(BF16)
            full = []
            for first, count in ((0, 2), (2, 2), (4, 1))[: 3 if k < SCALES - 1 else 2]:
                total = None
                for part in (high, low):
                    pieces = [part[:, 128 * (j % tiles) : 128 * (j % tiles) + 128] for j in range(first - 1, first + count + 1)]
                    weights = band[k] if count == 2 else band[k, :384, :128]
                    term = lax.dot_general(
                        jnp.concatenate(pieces, axis=1), weights, (((1,), (0,)), ((), ())), preferred_element_type=F32
                    )
                    total = term if total is None else total + term
                full += [total[:, 128 * j : 128 * j + 128] for j in range(count)]
            return full

        def store(row, full, factor, target=target):
            count = full[0].shape[0]
            lane = lax.broadcasted_iota(jnp.int32, (count, 128), 1)
            side = jnp.where(lane < 64, right, left)
            for j in range(tiles):
                value = full[j] * side if j == tiles - 1 else full[j]
                value = value if factor is None else value * factor
                target[pl.ds(row, count), 128 * j : 128 * (j + 1)] = value

        if k < SCALES - 1:
            for row, last, factor in ((begin, TOP, top), (TOP + SPAN, end, bottom)):
                low, high = max(row - 16, 0), min(last + 16, TALL)
                count = last - row
                rows = source[low:high, :]
                if low > row - 16:
                    rows = jnp.concatenate([jnp.zeros((low - row + 16, WIDE), F32), rows], axis=0)
                if high < last + 16:
                    rows = jnp.concatenate([rows, jnp.zeros((last + 16 - high, WIDE), F32)], axis=0)
                store(row, across(down(rows, count)[1]), factor)

        def one(block, carry, k=k, source=source, down=down, across=across, store=store, across_product=across_product):
            row = pl.multiple_of(TOP + block * BLOCK, 8)
            here = pl.multiple_of(block * BLOCK, 8)
            view = source.at[pl.ds(pl.multiple_of(row - 16, 8), BLOCK + 32), :]
            spans = [(0, BLOCK - WAVE, across), (BLOCK - WAVE, WAVE, across_product)]
            for start, count, method in spans:
                center, rows = down(view, count, 16 + start)
                full = method(rows)
                if k < SCALES - 1:
                    store(pl.multiple_of(row + start, 8), full, None)
                at = pl.ds(pl.multiple_of(here + start, 8), count)
                for j in range(SPAN // 128):
                    cols = slice(128 * j, 128 * (j + 1))
                    done[k, at, cols] = center[:, cols] - full[j]
                    if k == SCALES - 1:
                        done[SCALES, at, cols] = full[j]
            return carry

        half = SPAN // BLOCK // 2
        for number in range(2):
            lax.fori_loop(number * half, (number + 1) * half, one, 0)
            rows = pl.ds(number * SPAN // 2, SPAN // 2)
            copies.append(pltpu.make_async_copy(done.at[k, rows], details_ref.at[k, rows], sem.at[2 * k + number]))
            if k == SCALES - 1:
                copies.append(pltpu.make_async_copy(done.at[SCALES, rows], smooth_ref.at[rows], sem.at[2 * SCALES + number]))
                copies[-1].start()
                copies[-2].start()
            else:
                copies[-1].start()
        source = target
    for copy in copies:
        copy.wait()


def starlet_call(edges, first):
    return pl.pallas_call(
        starlet_kernel,
        in_specs=[pl.BlockSpec(memory_space=pltpu.SMEM), pl.BlockSpec(memory_space=pltpu.VMEM)],
        out_specs=[pl.BlockSpec(memory_space=pltpu.HBM)] * 2,
        out_shape=[
            jax.ShapeDtypeStruct((SCALES, SPAN, SPAN), F32),
            jax.ShapeDtypeStruct((SPAN, SPAN), F32),
        ],
        scratch_shapes=[
            pltpu.VMEM((TALL, WIDE), F32),
            pltpu.VMEM((TALL, WIDE), F32),
            pltpu.VMEM((SCALES, 512, 256), BF16),
            pltpu.VMEM((SCALES + 1, SPAN, SPAN), F32),
            pltpu.SemaphoreType.DMA((2 * SCALES + 2,)),
        ],
        compiler_params=pltpu.CompilerParams(vmem_limit_bytes=40 * 2**20),
    )(edges, first)


def shards(image, mask, weight, anchor, frac, scale, kernels, dest, offset):
    first = coaddition_call(
        dest, offset, anchor[0].T, frac[0].T, scale[0].T, weight, image, mask, kernels[0].transpose(1, 0, 2), constants()
    )
    band, patch = lax.axis_index("band"), lax.axis_index("patch")
    edges = jnp.stack(
        [band > 0, band < lax.axis_size("band") - 1, patch > 0, patch < lax.axis_size("patch") - 1]
    ).astype(F32)
    return tuple(starlet_call(edges, first))


def solution(mesh):
    owner = ("patch", "band")
    in_specs = (
        P(owner, None, None),
        P(owner, None, None),
        P(owner),
        P(owner, None, None),
        P(owner, None, None),
        P(owner, None, None),
        P(owner, None, None, None),
        P(owner, None),
        P(owner, None),
    )
    out_specs = (P(None, "band", "patch"), P("band", "patch"))
    return jax.shard_map(shards, mesh=mesh, in_specs=in_specs, out_specs=out_specs, check_vma=False)
```

```python
import math
import numpy as np
import ml_dtypes
import jax
import jax.numpy as jnp
from jax import lax
from jax.experimental import pallas as pl
from jax.experimental.pallas import tpu as pltpu
from jax.sharding import PartitionSpec as P

TILE, KS, SCALES, TR, TC, MARGIN, WARP_N, SRC_N = 128, 41, 4, 4, 4, 20, 168, 184
ROWS = 176
HALF = 88
WIN = 256
F32, BF16 = jnp.float32, jnp.bfloat16


def split_bf16(values):
    high = values.astype(ml_dtypes.bfloat16)
    low = (values - high.astype(np.float64)).astype(ml_dtypes.bfloat16)
    return high, low


def spectra():
    bins = np.arange(WARP_N // 2 + 1)

    def forward(points, sign):
        angle = 2.0 * np.pi / WARP_N * np.outer(bins, points)
        return np.cos(angle), sign * np.sin(angle)

    order = (np.arange(WARP_N) + MARGIN) % WARP_N
    real, imag = forward(order, -1.0)
    rows = np.zeros((ROWS, WIN))
    rows[: len(bins), :WARP_N] = real
    rows[HALF : HALF + len(bins), :WARP_N] = imag
    cols = np.zeros((WIN, WIN))
    cols[:WARP_N, : len(bins)] = real.T
    cols[:WARP_N, 128 : 128 + len(bins)] = imag.T
    real, imag = forward(np.arange(KS), 1.0)
    kcols = np.zeros((64, WIN))
    kcols[:KS, : len(bins)] = real.T
    kcols[:KS, 128 : 128 + len(bins)] = imag.T
    krows = np.zeros((ROWS, 48))
    krows[: len(bins), :KS] = real
    krows[HALF : HALF + len(bins), :KS] = imag
    count = np.full(len(bins), 2.0)
    count[0] = count[-1] = 1.0
    angle = 2.0 * np.pi / WARP_N * np.outer(np.arange(TILE), bins)
    back_real = np.cos(angle) * count / WARP_N
    back_imag = -np.sin(angle) * count / WARP_N
    icols = np.zeros((WIN, TILE))
    icols[: len(bins)] = back_real.T
    icols[128 : 128 + len(bins)] = back_imag.T
    irows = np.zeros((TILE, ROWS))
    irows[:, : len(bins)] = 0.5 * back_real
    irows[:, HALF : HALF + len(bins)] = 0.5 * back_imag
    kcols_high, kcols_low = split_bf16(kcols)
    krows_high, krows_low = split_bf16(krows)
    icols_high, icols_low = split_bf16(icols)
    irows_high, irows_low = split_bf16(irows)
    rows_pad = rows[:, :ROWS]
    return (
        cols.astype(ml_dtypes.bfloat16),
        rows_pad.astype(ml_dtypes.bfloat16),
        np.concatenate([kcols_high, kcols_low]),
        np.concatenate([krows_high, krows_high, krows_low], axis=1),
        np.concatenate([icols_high, icols_low], axis=1),
        np.concatenate([irows_high, irows_low]),
    )


def phase_constants():
    j = np.arange(WIN)
    sign = 1.0 - 2.0 * (j % 2)
    cosine = (sign * np.cos(np.pi * j / 5.0)).astype(np.float32)
    sine = (sign * np.sin(np.pi * j / 5.0)).astype(np.float32)
    along = np.zeros((8, WIN), np.float32)
    along[0], along[1] = cosine, sine
    down = np.stack([np.repeat(cosine[:, None], 128, 1), np.repeat(sine[:, None], 128, 1)])
    return along, down


def poly(coefficients, x):
    total = jnp.full_like(x, coefficients[-1])
    for value in coefficients[-2::-1]:
        total = total * x + value
    return total


SIN_PI = (3.14159265, -5.16771276, 2.55016332, -0.5992522, 0.0820504, -0.00702839)
SIN_TURN = (6.28318531, -41.34170222, 81.60524742, -76.70580022, 42.05775402, -15.08656526, 3.78131888, -0.62077872)
COS_TURN = (1.0, -19.73920874, 64.93938908, -85.45665831, 60.24213134, -26.40466819, 7.80013144, -1.45311232)


def lanczos(d, cos_row, sin_row, cos_col, sin_col):
    d2 = d * d
    u = cos_row * sin_col - sin_row * cos_col
    g = u / d2
    g = jnp.where(d2 < 1e-5, 1.0, g)
    return jnp.where(d2 < 25.0, g, 0.0).astype(BF16)


def dot(a, b):
    return lax.dot_general(a, b, (((1,), (0,)), ((), ())), preferred_element_type=F32)


def constants():
    along, down = phase_constants()
    return [jnp.asarray(a) for a in (along, down) + spectra()]


CELLS = TR * TC
GROUP = 4
LOADS = 3
SLAB = TILE // 2
SPAN = TR * TILE
PAD = 32
WIDE = SPAN + 128
TOP = 8 + PAD
TALL = SPAN + 2 * TOP
MESH = pl.DeviceIdType.MESH


def within(value, top):
    return jnp.minimum(jnp.maximum(value, 0), top)


def whole(a):
    return pl.BlockSpec(a.shape, lambda *_: (0,) * a.ndim)


PLACES = (0, 1, 2, 3, 12, 13, 14, 15, 4, 7, 8, 11, 5, 6, 9, 10)


def wanted_labels():
    lanes = np.arange(128)
    cell = np.asarray(PLACES)[lanes % CELLS]
    rows = np.full((8, 128), -1, np.int32)
    for source, step in enumerate((1, 2, 0)):
        rows[source] = (3 * (lanes // CELLS) + step) * CELLS + cell + 1
        rows[3 + source] = (3 * step + lanes // CELLS) * CELLS + cell + 1
    rows = np.where(lanes < 3 * CELLS, rows, -1).astype(np.int32)
    rows[6] = np.where(lanes < CELLS, lanes, np.where(lanes < 2 * CELLS, 64 + cell, -1))
    return rows


def coaddition_kernel(
    dest_ref, offset_ref, anchor_ref, frac_ref, scale_ref, weight_ref,
    image_hbm, mask_hbm, psf_hbm, wanted_hbm,
    along_hbm, down_hbm, cols_hbm, rows_hbm, kcols_hbm, krows_hbm, icols_hbm, irows_hbm,
    out_ref,
    wanted_ref, along_ref, down_ref, cols_ref, rows_ref, kcols_ref, krows_ref, icols_ref, irows_ref,
    image, mask, psf, taps_wide, kern_ref, label_ref, order, order_smem, planes, tiles, upper_in, lower_in, label_in, table, table_smem, send, recv, total, edge_send, edge_recv, rim_recv, corner_send, corner_recv,
    early_send_sem, early_recv_sem, label_send_sem, label_recv_sem, late_send_sem, late_recv_sem,
    edge_send_sem, edge_recv_sem, rim_send_sem, rim_recv_sem, local_sem, load_sem, psf_sem, constant_sem,
):
    psf_copy = pltpu.make_async_copy(psf_hbm, psf, psf_sem)
    constant_copies = [
        pltpu.make_async_copy(source, target, constant_sem.at[number])
        for number, (source, target) in enumerate(
            (
                (wanted_hbm, wanted_ref),
                (along_hbm, along_ref),
                (down_hbm, down_ref),
                (cols_hbm, cols_ref),
                (rows_hbm, rows_ref),
                (kcols_hbm, kcols_ref),
                (krows_hbm, krows_ref),
                (icols_hbm, icols_ref),
                (irows_hbm, irows_ref),
            )
        )
    ]
    constant_copies[0].start()
    psf_copy.start()
    loads = []
    for number in range(LOADS):
        rows = pl.ds(number * (768 // LOADS), 768 // LOADS)
        for kind, (source, target) in enumerate(((image_hbm, image), (mask_hbm, mask))):
            loads.append(pltpu.make_async_copy(source.at[0, rows], target.at[rows], load_sem.at[kind, number]))
    for load in loads:
        load.start()
    for copy in constant_copies[1:]:
        copy.start()

    patch, band = lax.axis_index("patch"), lax.axis_index("band")
    n_patch, n_band = lax.axis_size("patch"), lax.axis_size("band")
    left_patch, right_patch = lax.rem(patch + n_patch - 1, n_patch), lax.rem(patch + 1, n_patch)
    above_band, below_band = lax.rem(band + n_band - 1, n_band), lax.rem(band + 1, n_band)
    left, right = {"patch": left_patch, "band": band}, {"patch": right_patch, "band": band}
    above, below = {"patch": patch, "band": above_band}, {"patch": patch, "band": below_band}
    corners = [{"patch": p, "band": b} for b in (above_band, below_band) for p in (left_patch, right_patch)]
    has_left = jnp.where(patch > 0, 1.0, 0.0)
    has_right = jnp.where(patch < n_patch - 1, 1.0, 0.0)
    has_above = jnp.where(band > 0, 1.0, 0.0)
    has_below = jnp.where(band < n_band - 1, 1.0, 0.0)

    barrier = pltpu.get_barrier_semaphore()
    around = [left, right, above, below] + corners
    for device in around:
        pl.semaphore_signal(barrier, inc=1, device_id=device, device_id_type=MESH)

    def remote(src, dst, send_sem, recv_sem, device):
        return pltpu.make_async_remote_copy(
            src_ref=src, dst_ref=dst, send_sem=send_sem, recv_sem=recv_sem, device_id=device, device_id_type=MESH
        )

    beside = (upper_in, lower_in)

    early_to = ((right, left), (below, above))
    late_to = ((above, below), (left, right))

    def label_copy(half, way):
        return remote(
            label_ref,
            label_in.at[half, way],
            label_send_sem.at[half, way],
            label_recv_sem.at[half, way],
            early_to[half][way],
        )

    def early_copy(half, way, part):
        piece = pl.ds(part * GROUP, GROUP)
        return remote(
            tiles.at[half, piece],
            beside[half].at[way, piece],
            early_send_sem.at[half, way, part],
            early_recv_sem.at[half, way, part],
            early_to[half][way],
        )

    def late_copy(half, way, part):
        piece = pl.ds(part * TC, TC)
        return remote(
            send.at[half, way, piece],
            recv.at[half, way, piece],
            late_send_sem.at[half, way, part],
            late_recv_sem.at[half, way, part],
            late_to[half][way],
        )

    first_rows, last_rows = pl.ds(TOP, PAD), pl.ds(TOP + SPAN - PAD, PAD)

    def edge_copy(way, part):
        return remote(
            edge_send.at[way, part],
            edge_recv.at[way, part],
            edge_send_sem.at[way, part],
            edge_recv_sem.at[way, part],
            early_to[0][way],
        )

    def rim_copies(way):
        rows = (first_rows, last_rows)[way]
        triples = [(out_ref.at[rows, pl.ds(0, SPAN)], rim_recv.at[way], late_to[0][way])]
        for number in (2 * way, 2 * way + 1):
            triples.append((corner_send.at[number], corner_recv.at[number], corners[number]))
        return [
            remote(source, target, rim_send_sem.at[way, number], rim_recv_sem.at[way, number], device)
            for number, (source, target, device) in enumerate(triples)
        ]

    constant_copies[0].wait()
    filled = jnp.int32(0)
    key_of = wanted_ref[6:7, :]
    sub = lax.broadcasted_iota(jnp.int32, (CELLS, 128), 0)
    sequence = jnp.zeros((1, 128), jnp.int32)
    labels = jnp.zeros((CELLS, 128), jnp.int32)
    for i in range(2 * CELLS):
        code, cell = dest_ref[0, i], offset_ref[0, i]
        away = code != 4
        key = jnp.where(away, filled, 64 + cell)
        sequence = jnp.where(key_of == key, i, sequence)
        labels = jnp.where(sub == key, code * CELLS + cell + 1, labels)
        filled = filled + away.astype(jnp.int32)
    order[...] = jnp.broadcast_to(sequence, (8, 128))
    label_ref[...] = labels
    order_copy = pltpu.make_async_copy(order, order_smem, local_sem)
    order_copy.start()

    psf_copy.wait()
    gap = jnp.zeros((2 * CELLS, 64 - KS), F32)
    for r in range(KS):
        tap = psf[r].astype(F32)
        taps_wide[2 * CELLS * r : 2 * CELLS * (r + 1), :] = jnp.concatenate([tap, gap, tap, gap], axis=1)
    taps_wide[2 * CELLS * KS :, :] = jnp.zeros((2 * CELLS * (48 - KS), 128), F32)
    for t in range(2 * CELLS):
        kern_ref[t] = taps_wide[pl.ds(t, 48, stride=2 * CELLS), :].astype(BF16)

    def prepare(block, carry):
        rows = pl.ds(pl.multiple_of(block * 64, 64), 64)
        usable = jnp.where((mask[rows, :] & 7) != 7, 1.0, 0.0).astype(BF16)
        masked = image[rows, :] * usable
        for plane, value in enumerate((masked, usable)):
            moved = jnp.concatenate([value[:, 64:], value[:, :64]], axis=1)
            for way, data in enumerate((value, moved)):
                for j in range(6):
                    for i in range(4):
                        planes[way, plane, j, block * 4 + i] = data[16 * i : 16 * i + 16, 128 * j : 128 * j + 128]
        return carry

    steps = 768 // 64 // LOADS
    for number in range(LOADS):
        for load in loads[2 * number : 2 * number + 2]:
            load.wait()
        lax.fori_loop(number * steps, (number + 1) * steps, prepare, 0)
    order_copy.wait()
    for copy in constant_copies[1:]:
        copy.wait()

    lane = lax.broadcasted_iota(jnp.int32, (ROWS, WIN), 1)
    sub = lax.broadcasted_iota(jnp.int32, (WIN, WIN), 0)
    short = lax.broadcasted_iota(jnp.int32, (8, WIN), 1)
    quantity = lax.broadcasted_iota(jnp.int32, (8, WIN), 0)
    index = (short + jnp.where(short < WARP_N - MARGIN, MARGIN, MARGIN - WARP_N)).astype(F32)

    def warp_rows(fraction, stretch, shift):
        position = (5.0 + fraction) + index * (1.0 + stretch)
        nearest = jnp.floor(position + 0.5)
        odd = nearest - 2.0 * jnp.floor(nearest * 0.5)
        part = position - nearest
        sine = (1.0 - 2.0 * odd) * part * poly(SIN_PI, part * part)
        sign = (1 - 2 * (shift & 1)).astype(F32)
        amplitude = ((-5.0 / math.pi**2) * sign) * sine
        turn = position - 10.0 * jnp.floor(position * 0.1) + lax.rem(shift, 10).astype(F32)
        turn = turn * 0.1
        turn = turn - jnp.floor(turn + 0.5)
        square = turn * turn
        cosine, sine = poly(COS_TURN, square), turn * poly(SIN_TURN, square)
        position = jnp.where(short < WARP_N, position, 1e4)
        return jnp.where(quantity == 0, position, jnp.where(quantity == 1, amplitude * cosine, amplitude * sine))

    weight = weight_ref[0]
    each = range(GROUP)

    def store_tile(slot, plane, value):
        for half in range(2):
            tiles[half, slot, plane] = value[half * SLAB : (half + 1) * SLAB].astype(BF16)

    def gather(half, position):
        value = None
        for source in range(3):
            slot = table_smem[3 * half + source, position]
            present = jnp.where(slot >= 0, 1.0, 0.0)
            at = within(slot, CELLS - 1)
            data = tiles[half, at] if source == 0 else beside[half][source - 1, at]
            term = data.astype(F32) * present
            value = term if value is None else value + term
        return value

    def find_slots():
        for half in range(2):
            for way in range(2):
                label_copy(half, way).wait()
            for source in range(3):
                lookup = label_ref[...] if source == 0 else label_in[half, source - 1]
                number = 3 * half + source
                found = jnp.zeros((1, 128), jnp.int32)
                for slot in range(CELLS):
                    same = lookup[slot : slot + 1] == wanted_ref[number : number + 1, :]
                    found = found + jnp.where(same, slot + 1, 0)
                table[number : number + 1, :] = found - 1
        to_smem = pltpu.make_async_copy(table, table_smem, local_sem)
        to_smem.start()
        to_smem.wait()

    def pass_on(half):
        for part in range(CELLS // GROUP):
            for way in range(2):
                early_copy(half, way, part).wait()

        def outgoing(part, carry):
            for way in range(2):
                for c in range(TC):
                    cell = part * TC + c
                    send[half, way, cell] = gather(half, 2 * CELLS * way + cell).astype(BF16)
                late_copy(half, way, part).start()
            return carry

        lax.fori_loop(0, TR, outgoing, 0)

    def work(step, carry):
        chosen = [within(order_smem[0, step * GROUP + g], 2 * CELLS - 1) for g in each]
        half_img, half_cov, lt = [], [], []
        for g in each:
            t = chosen[g]
            first_row, first_col = anchor_ref[0, t], anchor_ref[1, t]
            row16 = within(first_row // 16, (768 - WIN) // 16)
            col64 = within(first_col // 64, (768 - WIN) // 64)
            off_r = first_row - row16 * 16
            off_c = first_col - col64 * 64
            par = within(col64 % 2, 1)
            pair = within(col64 // 2, 4)
            s_img, s_cov = (
                jnp.concatenate(
                    [
                        jnp.concatenate([planes[par, plane, pair + j, row16 + i] for i in range(16)], axis=0)
                        for j in range(2)
                    ],
                    axis=1,
                )
                for plane in range(2)
            )
            q0 = jnp.transpose(warp_rows(frac_ref[0, t], scale_ref[0, t], off_r))[:ROWS]
            d0 = (lane - off_r).astype(F32) - q0[:, 0:1]
            l0 = lanczos(d0, q0[:, 1:2], q0[:, 2:3], along_ref[0:1, :], along_ref[1:2, :])
            q1 = warp_rows(frac_ref[1, t], scale_ref[1, t], off_c)
            d1 = (sub - off_c).astype(F32) - q1[0:1, :]
            cosd = jnp.concatenate([down_ref[0], down_ref[0]], axis=1)
            sind = jnp.concatenate([down_ref[1], down_ref[1]], axis=1)
            lt.append(lanczos(d1, q1[1:2, :], q1[2:3, :], cosd, sind))
            half_img.append(dot(l0, s_img).astype(BF16))
            half_cov.append(dot(l0[:TILE], s_cov).astype(BF16))
        warped = [dot(half_img[g], lt[g]).astype(BF16) for g in each]
        for g in each:
            coverage = dot(half_cov[g], lt[g][:, :TILE])
            store_tile(step * GROUP + g, 1, weight * coverage)
        x1 = dot(jnp.concatenate(warped, axis=0), cols_ref[...]).astype(BF16)
        x2 = [dot(rows_ref[...], x1[g * ROWS : (g + 1) * ROWS]) for g in each]
        k1 = dot(jnp.concatenate([kern_ref[chosen[g]] for g in each], axis=0), kcols_ref[...])
        k1h = k1.astype(BF16)
        k1l = (k1 - k1h.astype(F32)).astype(BF16)
        z = []
        for g in each:
            h, l = k1h[g * 48 : g * 48 + 48], k1l[g * 48 : g * 48 + 48]
            k2 = dot(krows_ref[...], jnp.concatenate([h, l, h], axis=0))
            x = x2[g]
            xrr, xri, xir, xii = x[:HALF, :128], x[:HALF, 128:], x[HALF:, :128], x[HALF:, 128:]
            krr, kri, kir, kii = k2[:HALF, :128], k2[:HALF, 128:], k2[HALF:, :128], k2[HALF:, 128:]
            xpr, xpi, xmr, xmi = xrr - xii, xir + xri, xrr + xii, xir - xri
            kpr, kpi, kmr, kmi = krr - kii, kir + kri, krr + kii, kir - kri
            ppr, ppi = xpr * kpr - xpi * kpi, xpr * kpi + xpi * kpr
            pmr, pmi = xmr * kmr - xmi * kmi, xmr * kmi + xmi * kmr
            top = jnp.concatenate([ppr + pmr, ppi - pmi], axis=1)
            bottom = jnp.concatenate([ppi + pmi, pmr - ppr], axis=1)
            z.append(jnp.concatenate([top, bottom], axis=0).astype(BF16))
        y = dot(jnp.concatenate(z, axis=0), icols_ref[...])
        y = y[:, :TILE] + y[:, TILE:]
        yh = y.astype(BF16)
        yl = (y - yh.astype(F32)).astype(BF16)
        ycat = jnp.concatenate([yh, yl], axis=1)
        for g in each:
            o = dot(irows_ref[...], ycat[g * ROWS : (g + 1) * ROWS])
            matched = o[:TILE, :TILE] + (o[:TILE, TILE:] + o[TILE:, :TILE])
            store_tile(step * GROUP + g, 0, weight * matched)

        @pl.when(step == 0)
        def _():
            pl.semaphore_wait(barrier, len(around))
            for half in range(2):
                for way in range(2):
                    label_copy(half, way).start()

        @pl.when(step < CELLS // GROUP)
        def _():
            for half in range(2):
                for way in range(2):
                    early_copy(half, way, step).start()

        @pl.when(step == 4)
        def _():
            find_slots()
            pass_on(1)

        @pl.when(step == 6)
        def _():
            pass_on(0)

        return carry

    lax.fori_loop(0, 2 * CELLS // GROUP, work, 0)

    def staying(cell, carry):
        for half in range(2):
            total[half, cell] = gather(half, CELLS + cell) + tiles[half, CELLS + cell].astype(F32)
        return carry

    lax.fori_loop(0, CELLS, staying, 0)

    lane = lax.broadcasted_iota(jnp.int32, (PAD, TILE), 1)

    small = lax.broadcasted_iota(jnp.int32, (PAD // 4, TILE), 1)

    def pack_corners(way):
        for side in range(2):
            packed = jnp.zeros((PAD // 4, TILE), F32)
            for q in range(4):
                row = (TOP if way == 0 else TOP + SPAN - PAD) + q * (PAD // 4)
                end = out_ref[row : row + PAD // 4, :TILE] if side == 0 else out_ref[row : row + PAD // 4, SPAN - TILE : SPAN]
                turn = (PAD * q + PAD * side) % TILE
                moved = end if turn == 0 else pltpu.roll(end, turn, 1)
                packed = jnp.where((small >= PAD * q) & (small < PAD * (q + 1)), moved, packed)
            corner_send[2 * way + side] = packed

    def send_edges(part):
        for way in range(2):
            cols = slice(SPAN - TILE, SPAN) if way == 0 else slice(0, TILE)
            packed = jnp.zeros((PAD, TILE), F32)
            for q in range(4):
                row = TOP + part * TILE + q * PAD
                end = out_ref[row : row + PAD, cols]
                turn = (PAD * q + (PAD if way == 0 else 0)) % TILE
                moved = end if turn == 0 else pltpu.roll(end, turn, 1)
                packed = jnp.where((lane >= PAD * q) & (lane < PAD * (q + 1)), moved, packed)
            edge_send[way, part] = packed.astype(BF16)
            edge_copy(way, part).start()

    for part in range(TR):
        for half in range(2):
            for way in range(2):
                late_copy(half, way, part).wait()
            for place in range(part * TC, (part + 1) * TC):
                row = TOP + PLACES[place] // TC * TILE + half * SLAB
                col = PLACES[place] % TC * TILE
                value = total[half, place] + (recv[half, 0, place].astype(F32) + recv[half, 1, place].astype(F32))
                out_ref[row : row + SLAB, col : col + TILE] = value[0] / (jnp.maximum(value[1], 0.0) + 1.0)
        if part < 2:
            pack_corners(part)
            for copy in rim_copies(part):
                copy.start()
            send_edges(part * (TR - 1))
        if part == 2:
            send_edges(1)
            send_edges(2)

    blank = jnp.zeros((8, WIDE), F32)
    out_ref[0:8, :] = blank
    out_ref[TALL - 8 : TALL, :] = blank

    def unpack(part, carry):
        for way in range(2):
            edge_copy(way, part).wait()
        from_left = edge_recv[0, part].astype(F32) * has_left
        from_right = edge_recv[1, part].astype(F32) * has_right
        for q in range(4):
            turn = (TILE - PAD * q) % TILE
            near = from_right if turn == 0 else pltpu.roll(from_right, turn, 1)
            turn = (TILE - PAD - PAD * q) % TILE
            far = from_left if turn == 0 else pltpu.roll(from_left, turn, 1)
            rows = pl.ds(pl.multiple_of(TOP + part * TILE + q * PAD, 8), PAD)
            out_ref[rows, SPAN:] = jnp.where(lane < PAD, near, jnp.where(lane >= TILE - PAD, far, 0.0))
        return carry

    lax.fori_loop(0, TR, unpack, 0)
    for way in range(2):
        for copy in rim_copies(way):
            copy.wait()
    for way in range(2):
        start = TOP + SPAN if way == 0 else 8
        factor = has_below if way == 0 else has_above
        out_ref[start : start + PAD, :SPAN] = rim_recv[way] * factor
        near_data = corner_recv[2 * way] * (has_right * factor)
        far_data = corner_recv[2 * way + 1] * (has_left * factor)
        for q in range(4):
            turn = (TILE - PAD * q) % TILE
            near = near_data if turn == 0 else pltpu.roll(near_data, turn, 1)
            turn = (TILE - PAD - PAD * q) % TILE
            far = far_data if turn == 0 else pltpu.roll(far_data, turn, 1)
            row = start + q * (PAD // 4)
            out_ref[row : row + PAD // 4, SPAN:] = jnp.where(
                small < PAD, near, jnp.where(small >= TILE - PAD, far, 0.0)
            )


def coaddition_call(dest, offset, anchor, frac, scale, weight, image, mask, psf, consts):
    scalars = (dest, offset, anchor, frac, scale, weight)
    fixed = (jnp.asarray(wanted_labels()),) + tuple(consts)
    dma = pltpu.SemaphoreType.DMA
    slab = (2, SLAB, TILE)
    parts = CELLS // GROUP
    return pl.pallas_call(
        coaddition_kernel,
        in_specs=[pl.BlockSpec(memory_space=pltpu.SMEM)] * len(scalars)
        + [pl.BlockSpec(memory_space=pl.ANY)] * (3 + len(fixed)),
        out_specs=pl.BlockSpec(memory_space=pltpu.VMEM),
        out_shape=pltpu.VMEM((TALL, WIDE), F32),
        scratch_shapes=[pltpu.VMEM(a.shape, a.dtype) for a in fixed]
        + [
            pltpu.VMEM((768, 768), BF16),
            pltpu.VMEM((768, 768), jnp.int32),
            pltpu.VMEM(psf.shape, BF16),
            pltpu.VMEM((48 * 2 * CELLS, 128), F32),
            pltpu.VMEM((2 * CELLS, 48, 128), BF16),
            pltpu.VMEM((CELLS, 128), jnp.int32),
            pltpu.VMEM((8, 128), jnp.int32),
            pltpu.SMEM((8, 128), jnp.int32),
            pltpu.VMEM((2, 2, 6, 48, 16, 128), BF16),
            pltpu.VMEM((2, 2 * CELLS) + slab, BF16),
            pltpu.VMEM((2, CELLS) + slab, BF16),
            pltpu.VMEM((2, CELLS) + slab, BF16),
            pltpu.VMEM((2, 2, CELLS, 128), jnp.int32),
            pltpu.VMEM((8, 128), jnp.int32),
            pltpu.SMEM((8, 128), jnp.int32),
            pltpu.VMEM((2, 2, CELLS) + slab, BF16),
            pltpu.VMEM((2, 2, CELLS) + slab, BF16),
            pltpu.VMEM((2, CELLS) + slab, F32),
            pltpu.VMEM((2, TR, PAD, TILE), BF16),
            pltpu.VMEM((2, TR, PAD, TILE), BF16),
            pltpu.VMEM((2, PAD, SPAN), F32),
            pltpu.VMEM((4, PAD // 4, TILE), F32),
            pltpu.VMEM((4, PAD // 4, TILE), F32),
            dma((2, 2, parts)), dma((2, 2, parts)), dma((2, 2)), dma((2, 2)), dma((2, 2, TR)), dma((2, 2, TR)),
            dma((2, TR)), dma((2, TR)), dma((2, 3)), dma((2, 3)), dma(()), dma((2, LOADS)), dma(()), dma((len(fixed),)),
        ],
        compiler_params=pltpu.CompilerParams(
            vmem_limit_bytes=56 * 2**20, collective_id=0, has_side_effects=True
        ),
    )(*scalars, image, mask, psf, *fixed)


LEVEL_ROWS = ((8, 584), (16, 576), (24, 568), (40, 552))
BLOCK = 256
WAVE = 192


def starlet_kernel(edge_ref, first_ref, details_ref, smooth_ref, ping, pong, band, done, sem):
    top, bottom, left, right = (edge_ref[i] for i in range(4))
    tiles = WIDE // 128
    zero = jnp.zeros((8, WIDE), F32)
    for ref in (ping, pong):
        ref[0:8, :] = zero
        ref[TALL - 8 : TALL, :] = zero
    offset = lax.broadcasted_iota(jnp.int32, (512, 256), 0) - lax.broadcasted_iota(jnp.int32, (512, 256), 1) - 128
    offset = jnp.abs(offset)
    for k in range(SCALES):
        s = 2**k
        tap = jnp.where(offset == 0, 6.0, jnp.where(offset == s, 4.0, jnp.where(offset == 2 * s, 1.0, 0.0)))
        band[k] = (tap * (1.0 / 256.0)).astype(BF16)

    source = first_ref
    copies = []
    for k in range(SCALES):
        s = 2**k
        target = (ping, pong)[k % 2]
        begin, end = LEVEL_ROWS[k]

        def down(view, count, at=16, s=s):
            def near(by):
                return view[at + by : at + by + count, :]

            center = near(0)
            return center, (near(-2 * s) + near(2 * s)) + 4.0 * (near(-s) + near(s)) + 6.0 * center

        def across(rows, s=s):
            count = rows.shape[0]
            parts = [rows[:, 128 * j : 128 * (j + 1)] for j in range(tiles)]
            lane = lax.broadcasted_iota(jnp.int32, (count, 128), 1)

            def after(by):
                turned = [pltpu.roll(part, by, 1) for part in parts]
                return [jnp.where(lane < by, turned[j - 1], turned[j]) for j in range(tiles)]

            def before(by):
                turned = [pltpu.roll(part, 128 - by, 1) for part in parts]
                return [jnp.where(lane >= 128 - by, turned[(j + 1) % tiles], turned[j]) for j in range(tiles)]

            a, b, c, d = after(2 * s), before(2 * s), after(s), before(s)
            return [((a[j] + b[j]) + 4.0 * (c[j] + d[j]) + 6.0 * parts[j]) * (1.0 / 256.0) for j in range(tiles if s < 8 else tiles - 1)]

        def across_product(rows, k=k):
            high = rows.astype(BF16)
            low = (rows - high.astype(F32)).astype(BF16)
            full = []
            for first, count in ((0, 2), (2, 2), (4, 1))[: 3 if k < SCALES - 1 else 2]:
                total = None
                for part in (high, low):
                    pieces = [part[:, 128 * (j % tiles) : 128 * (j % tiles) + 128] for j in range(first - 1, first + count + 1)]
                    weights = band[k] if count == 2 else band[k, :384, :128]
                    term = lax.dot_general(
                        jnp.concatenate(pieces, axis=1), weights, (((1,), (0,)), ((), ())), preferred_element_type=F32
                    )
                    total = term if total is None else total + term
                full += [total[:, 128 * j : 128 * j + 128] for j in range(count)]
            return full

        def store(row, full, factor, target=target):
            count = full[0].shape[0]
            lane = lax.broadcasted_iota(jnp.int32, (count, 128), 1)
            side = jnp.where(lane < 64, right, left)
            for j in range(tiles):
                value = full[j] * side if j == tiles - 1 else full[j]
                value = value if factor is None else value * factor
                target[pl.ds(row, count), 128 * j : 128 * (j + 1)] = value

        if k < SCALES - 1:
            for row, last, factor in ((begin, TOP, top), (TOP + SPAN, end, bottom)):
                low, high = max(row - 16, 0), min(last + 16, TALL)
                count = last - row
                rows = source[low:high, :]
                if low > row - 16:
                    rows = jnp.concatenate([jnp.zeros((low - row + 16, WIDE), F32), rows], axis=0)
                if high < last + 16:
                    rows = jnp.concatenate([rows, jnp.zeros((last + 16 - high, WIDE), F32)], axis=0)
                store(row, across(down(rows, count)[1]), factor)

        def one(block, carry, k=k, source=source, down=down, across=across, store=store, across_product=across_product):
            row = pl.multiple_of(TOP + block * BLOCK, 8)
            here = pl.multiple_of(block * BLOCK, 8)
            view = source.at[pl.ds(pl.multiple_of(row - 16, 8), BLOCK + 32), :]
            spans = [(0, BLOCK - WAVE, across), (BLOCK - WAVE, WAVE, across_product)]
            for start, count, method in spans:
                center, rows = down(view, count, 16 + start)
                full = method(rows)
                if k < SCALES - 1:
                    store(pl.multiple_of(row + start, 8), full, None)
                at = pl.ds(pl.multiple_of(here + start, 8), count)
                for j in range(SPAN // 128):
                    cols = slice(128 * j, 128 * (j + 1))
                    done[k, at, cols] = center[:, cols] - full[j]
                    if k == SCALES - 1:
                        done[SCALES, at, cols] = full[j]
            return carry

        half = SPAN // BLOCK // 2
        for number in range(2):
            lax.fori_loop(number * half, (number + 1) * half, one, 0)
            rows = pl.ds(number * SPAN // 2, SPAN // 2)
            copies.append(pltpu.make_async_copy(done.at[k, rows], details_ref.at[k, rows], sem.at[2 * k + number]))
            if k == SCALES - 1:
                copies.append(pltpu.make_async_copy(done.at[SCALES, rows], smooth_ref.at[rows], sem.at[2 * SCALES + number]))
                copies[-1].start()
                copies[-2].start()
            else:
                copies[-1].start()
        source = target
    for copy in copies:
        copy.wait()


def starlet_call(edges, first):
    return pl.pallas_call(
        starlet_kernel,
        in_specs=[pl.BlockSpec(memory_space=pltpu.SMEM), pl.BlockSpec(memory_space=pltpu.VMEM)],
        out_specs=[pl.BlockSpec(memory_space=pltpu.HBM)] * 2,
        out_shape=[
            jax.ShapeDtypeStruct((SCALES, SPAN, SPAN), F32),
            jax.ShapeDtypeStruct((SPAN, SPAN), F32),
        ],
        scratch_shapes=[
            pltpu.VMEM((TALL, WIDE), F32),
            pltpu.VMEM((TALL, WIDE), F32),
            pltpu.VMEM((SCALES, 512, 256), BF16),
            pltpu.VMEM((SCALES + 1, SPAN, SPAN), F32),
            pltpu.SemaphoreType.DMA((2 * SCALES + 2,)),
        ],
        compiler_params=pltpu.CompilerParams(vmem_limit_bytes=40 * 2**20),
    )(edges, first)


def shards(image, mask, weight, anchor, frac, scale, kernels, dest, offset):
    first = coaddition_call(
        dest, offset, anchor[0].T, frac[0].T, scale[0].T, weight, image, mask, kernels[0].transpose(1, 0, 2), constants()
    )
    band, patch = lax.axis_index("band"), lax.axis_index("patch")
    edges = jnp.stack(
        [band > 0, band < lax.axis_size("band") - 1, patch > 0, patch < lax.axis_size("patch") - 1]
    ).astype(F32)
    return tuple(starlet_call(edges, first))


def solution(mesh):
    owner = ("patch", "band")
    in_specs = (
        P(owner, None, None),
        P(owner, None, None),
        P(owner),
        P(owner, None, None),
        P(owner, None, None),
        P(owner, None, None),
        P(owner, None, None, None),
        P(owner, None),
        P(owner, None),
    )
    out_specs = (P(None, "band", "patch"), P("band", "patch"))
    return jax.shard_map(shards, mesh=mesh, in_specs=in_specs, out_specs=out_specs, check_vma=False)
```

```python
import math
import numpy as np
import ml_dtypes
import jax
import jax.numpy as jnp
from jax import lax
from jax.experimental import pallas as pl
from jax.experimental.pallas import tpu as pltpu
from jax.sharding import PartitionSpec as P

TILE, KS, SCALES, TR, TC, MARGIN, WARP_N, SRC_N = 128, 41, 4, 4, 4, 20, 168, 184
ROWS = 176
HALF = 88
WIN = 256
F32, BF16 = jnp.float32, jnp.bfloat16


def split_bf16(values):
    high = values.astype(ml_dtypes.bfloat16)
    low = (values - high.astype(np.float64)).astype(ml_dtypes.bfloat16)
    return high, low


def spectra():
    bins = np.arange(WARP_N // 2 + 1)

    def forward(points, sign):
        angle = 2.0 * np.pi / WARP_N * np.outer(bins, points)
        return np.cos(angle), sign * np.sin(angle)

    order = (np.arange(WARP_N) + MARGIN) % WARP_N
    real, imag = forward(order, -1.0)
    rows = np.zeros((ROWS, WIN))
    rows[: len(bins), :WARP_N] = real
    rows[HALF : HALF + len(bins), :WARP_N] = imag
    cols = np.zeros((WIN, WIN))
    cols[:WARP_N, : len(bins)] = real.T
    cols[:WARP_N, 128 : 128 + len(bins)] = imag.T
    real, imag = forward(np.arange(KS), 1.0)
    kcols = np.zeros((64, WIN))
    kcols[:KS, : len(bins)] = real.T
    kcols[:KS, 128 : 128 + len(bins)] = imag.T
    krows = np.zeros((ROWS, 48))
    krows[: len(bins), :KS] = real
    krows[HALF : HALF + len(bins), :KS] = imag
    count = np.full(len(bins), 2.0)
    count[0] = count[-1] = 1.0
    angle = 2.0 * np.pi / WARP_N * np.outer(np.arange(TILE), bins)
    back_real = np.cos(angle) * count / WARP_N
    back_imag = -np.sin(angle) * count / WARP_N
    icols = np.zeros((WIN, TILE))
    icols[: len(bins)] = back_real.T
    icols[128 : 128 + len(bins)] = back_imag.T
    irows = np.zeros((TILE, ROWS))
    irows[:, : len(bins)] = 0.5 * back_real
    irows[:, HALF : HALF + len(bins)] = 0.5 * back_imag
    kcols_high, kcols_low = split_bf16(kcols)
    krows_high, krows_low = split_bf16(krows)
    icols_high, icols_low = split_bf16(icols)
    irows_high, irows_low = split_bf16(irows)
    rows_pad = rows[:, :ROWS]
    return (
        cols.astype(ml_dtypes.bfloat16),
        rows_pad.astype(ml_dtypes.bfloat16),
        np.concatenate([kcols_high, kcols_low]),
        np.concatenate([krows_high, krows_high, krows_low], axis=1),
        np.concatenate([icols_high, icols_low], axis=1),
        np.concatenate([irows_high, irows_low]),
    )


def phase_constants():
    j = np.arange(WIN)
    sign = 1.0 - 2.0 * (j % 2)
    cosine = (sign * np.cos(np.pi * j / 5.0)).astype(np.float32)
    sine = (sign * np.sin(np.pi * j / 5.0)).astype(np.float32)
    along = np.zeros((8, WIN), np.float32)
    along[0], along[1] = cosine, sine
    return along


def poly(coefficients, x):
    total = jnp.full_like(x, coefficients[-1])
    for value in coefficients[-2::-1]:
        total = total * x + value
    return total


SIN_PI = (3.14159265, -5.16771276, 2.55016332, -0.5992522, 0.0820504, -0.00702839)
SIN_TURN = (6.28318531, -41.34170222, 81.60524742, -76.70580022, 42.05775402, -15.08656526, 3.78131888, -0.62077872)
COS_TURN = (1.0, -19.73920874, 64.93938908, -85.45665831, 60.24213134, -26.40466819, 7.80013144, -1.45311232)


def lanczos(d, cos_row, sin_row, cos_col, sin_col):
    d2 = d * d
    u = cos_row * sin_col - sin_row * cos_col
    g = u / d2
    g = jnp.where(d2 < 1e-5, 1.0, g)
    return jnp.where(d2 < 25.0, g, 0.0).astype(BF16)


def dot(a, b):
    return lax.dot_general(a, b, (((1,), (0,)), ((), ())), preferred_element_type=F32)


def constants():
    return [jnp.asarray(a) for a in (phase_constants(),) + spectra()]


CELLS = TR * TC
GROUP = 4
LOADS = 3
SLAB = TILE // 2
SPAN = TR * TILE
PAD = 32
WIDE = SPAN + 128
TOP = 8 + PAD
TALL = SPAN + 2 * TOP
MESH = pl.DeviceIdType.MESH


def within(value, top):
    return jnp.minimum(jnp.maximum(value, 0), top)


def whole(a):
    return pl.BlockSpec(a.shape, lambda *_: (0,) * a.ndim)


PLACES = (0, 1, 2, 3, 12, 13, 14, 15, 4, 7, 8, 11, 5, 6, 9, 10)


def wanted_labels():
    lanes = np.arange(128)
    cell = np.asarray(PLACES)[lanes % CELLS]
    rows = np.full((8, 128), -1, np.int32)
    for source, step in enumerate((1, 2, 0)):
        rows[source] = (3 * (lanes // CELLS) + step) * CELLS + cell + 1
        rows[3 + source] = (3 * step + lanes // CELLS) * CELLS + cell + 1
    rows = np.where(lanes < 3 * CELLS, rows, -1).astype(np.int32)
    rows[6] = np.where(lanes < CELLS, lanes, np.where(lanes < 2 * CELLS, 64 + cell, -1))
    return rows


def coaddition_kernel(
    dest_ref, offset_ref, anchor_ref, frac_ref, scale_ref, weight_ref,
    image_hbm, mask_hbm, psf_hbm, wanted_hbm,
    along_hbm, cols_hbm, rows_hbm, kcols_hbm, krows_hbm, icols_hbm, irows_hbm,
    out_ref,
    wanted_ref, along_ref, cols_ref, rows_ref, kcols_ref, krows_ref, icols_ref, irows_ref,
    down_ref, image, mask, psf, taps_wide, kern_ref, label_ref, order, order_smem, planes, tiles, upper_in, lower_in, label_in, table, table_smem, send, recv, total, edge_send, edge_recv, rim_recv, corner_send, corner_recv,
    early_send_sem, early_recv_sem, label_send_sem, label_recv_sem, late_send_sem, late_recv_sem,
    edge_send_sem, edge_recv_sem, rim_send_sem, rim_recv_sem, local_sem, load_sem, psf_sem, constant_sem,
):
    psf_copy = pltpu.make_async_copy(psf_hbm, psf, psf_sem)
    constant_copies = [
        pltpu.make_async_copy(source, target, constant_sem.at[number])
        for number, (source, target) in enumerate(
            (
                (wanted_hbm, wanted_ref),
                (along_hbm, along_ref),
                (cols_hbm, cols_ref),
                (rows_hbm, rows_ref),
                (kcols_hbm, kcols_ref),
                (krows_hbm, krows_ref),
                (icols_hbm, icols_ref),
                (irows_hbm, irows_ref),
            )
        )
    ]
    constant_copies[0].start()
    constant_copies[1].start()
    psf_copy.start()
    loads = []
    for number in range(LOADS):
        rows = pl.ds(number * (768 // LOADS), 768 // LOADS)
        for kind, (source, target) in enumerate(((image_hbm, image), (mask_hbm, mask))):
            loads.append(pltpu.make_async_copy(source.at[0, rows], target.at[rows], load_sem.at[kind, number]))
    for load in loads:
        load.start()
    for copy in constant_copies[2:]:
        copy.start()

    patch, band = lax.axis_index("patch"), lax.axis_index("band")
    n_patch, n_band = lax.axis_size("patch"), lax.axis_size("band")
    left_patch, right_patch = lax.rem(patch + n_patch - 1, n_patch), lax.rem(patch + 1, n_patch)
    above_band, below_band = lax.rem(band + n_band - 1, n_band), lax.rem(band + 1, n_band)
    left, right = {"patch": left_patch, "band": band}, {"patch": right_patch, "band": band}
    above, below = {"patch": patch, "band": above_band}, {"patch": patch, "band": below_band}
    corners = [{"patch": p, "band": b} for b in (above_band, below_band) for p in (left_patch, right_patch)]
    has_left = jnp.where(patch > 0, 1.0, 0.0)
    has_right = jnp.where(patch < n_patch - 1, 1.0, 0.0)
    has_above = jnp.where(band > 0, 1.0, 0.0)
    has_below = jnp.where(band < n_band - 1, 1.0, 0.0)

    barrier = pltpu.get_barrier_semaphore()
    around = [left, right, above, below] + corners
    for device in around:
        pl.semaphore_signal(barrier, inc=1, device_id=device, device_id_type=MESH)

    def remote(src, dst, send_sem, recv_sem, device):
        return pltpu.make_async_remote_copy(
            src_ref=src, dst_ref=dst, send_sem=send_sem, recv_sem=recv_sem, device_id=device, device_id_type=MESH
        )

    beside = (upper_in, lower_in)

    early_to = ((right, left), (below, above))
    late_to = ((above, below), (left, right))

    def label_copy(half, way):
        return remote(
            label_ref,
            label_in.at[half, way],
            label_send_sem.at[half, way],
            label_recv_sem.at[half, way],
            early_to[half][way],
        )

    def early_copy(half, way, part):
        piece = pl.ds(part * GROUP, GROUP)
        return remote(
            tiles.at[half, piece],
            beside[half].at[way, piece],
            early_send_sem.at[half, way, part],
            early_recv_sem.at[half, way, part],
            early_to[half][way],
        )

    def late_copy(half, way, part):
        piece = pl.ds(part * TC, TC)
        return remote(
            send.at[half, way, piece],
            recv.at[half, way, piece],
            late_send_sem.at[half, way, part],
            late_recv_sem.at[half, way, part],
            late_to[half][way],
        )

    first_rows, last_rows = pl.ds(TOP, PAD), pl.ds(TOP + SPAN - PAD, PAD)

    def edge_copy(way, part):
        return remote(
            edge_send.at[way, part],
            edge_recv.at[way, part],
            edge_send_sem.at[way, part],
            edge_recv_sem.at[way, part],
            early_to[0][way],
        )

    def rim_copies(way):
        rows = (first_rows, last_rows)[way]
        triples = [(out_ref.at[rows, pl.ds(0, SPAN)], rim_recv.at[way], late_to[0][way])]
        for number in (2 * way, 2 * way + 1):
            triples.append((corner_send.at[number], corner_recv.at[number], corners[number]))
        return [
            remote(source, target, rim_send_sem.at[way, number], rim_recv_sem.at[way, number], device)
            for number, (source, target, device) in enumerate(triples)
        ]

    for copy in constant_copies[:2]:
        copy.wait()
    columns = jnp.transpose(along_ref[...])
    for number in range(2):
        down_ref[number] = jnp.broadcast_to(columns[:, number : number + 1], (WIN, 128))
    filled = jnp.int32(0)
    key_of = wanted_ref[6:7, :]
    sub = lax.broadcasted_iota(jnp.int32, (CELLS, 128), 0)
    sequence = jnp.zeros((1, 128), jnp.int32)
    labels = jnp.zeros((CELLS, 128), jnp.int32)
    for i in range(2 * CELLS):
        code, cell = dest_ref[0, i], offset_ref[0, i]
        away = code != 4
        key = jnp.where(away, filled, 64 + cell)
        sequence = jnp.where(key_of == key, i, sequence)
        labels = jnp.where(sub == key, code * CELLS + cell + 1, labels)
        filled = filled + away.astype(jnp.int32)
    order[...] = jnp.broadcast_to(sequence, (8, 128))
    label_ref[...] = labels
    order_copy = pltpu.make_async_copy(order, order_smem, local_sem)
    order_copy.start()

    psf_copy.wait()
    gap = jnp.zeros((2 * CELLS, 64 - KS), F32)
    for r in range(KS):
        tap = psf[r].astype(F32)
        taps_wide[2 * CELLS * r : 2 * CELLS * (r + 1), :] = jnp.concatenate([tap, gap, tap, gap], axis=1)
    taps_wide[2 * CELLS * KS :, :] = jnp.zeros((2 * CELLS * (48 - KS), 128), F32)
    for t in range(2 * CELLS):
        kern_ref[t] = taps_wide[pl.ds(t, 48, stride=2 * CELLS), :].astype(BF16)

    def prepare(block, carry):
        rows = pl.ds(pl.multiple_of(block * 64, 64), 64)
        usable = jnp.where((mask[rows, :] & 7) != 7, 1.0, 0.0).astype(BF16)
        masked = image[rows, :] * usable
        for plane, value in enumerate((masked, usable)):
            moved = jnp.concatenate([value[:, 64:], value[:, :64]], axis=1)
            for way, data in enumerate((value, moved)):
                for j in range(6):
                    for i in range(4):
                        planes[way, plane, j, block * 4 + i] = data[16 * i : 16 * i + 16, 128 * j : 128 * j + 128]
        return carry

    steps = 768 // 64 // LOADS
    for number in range(LOADS):
        for load in loads[2 * number : 2 * number + 2]:
            load.wait()
        lax.fori_loop(number * steps, (number + 1) * steps, prepare, 0)
    order_copy.wait()
    for copy in constant_copies[2:]:
        copy.wait()

    lane = lax.broadcasted_iota(jnp.int32, (ROWS, WIN), 1)
    sub = lax.broadcasted_iota(jnp.int32, (WIN, WIN), 0)
    short = lax.broadcasted_iota(jnp.int32, (8, WIN), 1)
    quantity = lax.broadcasted_iota(jnp.int32, (8, WIN), 0)
    index = (short + jnp.where(short < WARP_N - MARGIN, MARGIN, MARGIN - WARP_N)).astype(F32)

    def warp_rows(fraction, stretch, shift):
        position = (5.0 + fraction) + index * (1.0 + stretch)
        nearest = jnp.floor(position + 0.5)
        odd = nearest - 2.0 * jnp.floor(nearest * 0.5)
        part = position - nearest
        sine = (1.0 - 2.0 * odd) * part * poly(SIN_PI, part * part)
        sign = (1 - 2 * (shift & 1)).astype(F32)
        amplitude = ((-5.0 / math.pi**2) * sign) * sine
        turn = position - 10.0 * jnp.floor(position * 0.1) + lax.rem(shift, 10).astype(F32)
        turn = turn * 0.1
        turn = turn - jnp.floor(turn + 0.5)
        square = turn * turn
        cosine, sine = poly(COS_TURN, square), turn * poly(SIN_TURN, square)
        position = jnp.where(short < WARP_N, position, 1e4)
        return jnp.where(quantity == 0, position, jnp.where(quantity == 1, amplitude * cosine, amplitude * sine))

    weight = weight_ref[0]
    each = range(GROUP)

    def store_tile(slot, plane, value):
        for half in range(2):
            tiles[half, slot, plane] = value[half * SLAB : (half + 1) * SLAB].astype(BF16)

    def gather(half, position):
        value = None
        for source in range(3):
            slot = table_smem[3 * half + source, position]
            present = jnp.where(slot >= 0, 1.0, 0.0)
            at = within(slot, CELLS - 1)
            data = tiles[half, at] if source == 0 else beside[half][source - 1, at]
            term = data.astype(F32) * present
            value = term if value is None else value + term
        return value

    def find_slots():
        for half in range(2):
            for way in range(2):
                label_copy(half, way).wait()
            for source in range(3):
                lookup = label_ref[...] if source == 0 else label_in[half, source - 1]
                number = 3 * half + source
                found = jnp.zeros((1, 128), jnp.int32)
                for slot in range(CELLS):
                    same = lookup[slot : slot + 1] == wanted_ref[number : number + 1, :]
                    found = found + jnp.where(same, slot + 1, 0)
                table[number : number + 1, :] = found - 1
        to_smem = pltpu.make_async_copy(table, table_smem, local_sem)
        to_smem.start()
        to_smem.wait()

    def pass_on(half):
        for part in range(CELLS // GROUP):
            for way in range(2):
                early_copy(half, way, part).wait()

        def outgoing(part, carry):
            for way in range(2):
                for c in range(TC):
                    cell = part * TC + c
                    send[half, way, cell] = gather(half, 2 * CELLS * way + cell).astype(BF16)
                late_copy(half, way, part).start()
            return carry

        lax.fori_loop(0, TR, outgoing, 0)

    def work(step, carry):
        chosen = [within(order_smem[0, step * GROUP + g], 2 * CELLS - 1) for g in each]
        half_img, half_cov, lt = [], [], []
        for g in each:
            t = chosen[g]
            first_row, first_col = anchor_ref[0, t], anchor_ref[1, t]
            row16 = within(first_row // 16, (768 - WIN) // 16)
            col64 = within(first_col // 64, (768 - WIN) // 64)
            off_r = first_row - row16 * 16
            off_c = first_col - col64 * 64
            par = within(col64 % 2, 1)
            pair = within(col64 // 2, 4)
            s_img, s_cov = (
                jnp.concatenate(
                    [
                        jnp.concatenate([planes[par, plane, pair + j, row16 + i] for i in range(16)], axis=0)
                        for j in range(2)
                    ],
                    axis=1,
                )
                for plane in range(2)
            )
            q0 = jnp.transpose(warp_rows(frac_ref[0, t], scale_ref[0, t], off_r))[:ROWS]
            d0 = (lane - off_r).astype(F32) - q0[:, 0:1]
            l0 = lanczos(d0, q0[:, 1:2], q0[:, 2:3], along_ref[0:1, :], along_ref[1:2, :])
            q1 = warp_rows(frac_ref[1, t], scale_ref[1, t], off_c)
            d1 = (sub - off_c).astype(F32) - q1[0:1, :]
            cosd = jnp.concatenate([down_ref[0], down_ref[0]], axis=1)
            sind = jnp.concatenate([down_ref[1], down_ref[1]], axis=1)
            lt.append(lanczos(d1, q1[1:2, :], q1[2:3, :], cosd, sind))
            half_img.append(dot(l0, s_img).astype(BF16))
            half_cov.append(dot(l0[:TILE], s_cov).astype(BF16))
        warped = [dot(half_img[g], lt[g]).astype(BF16) for g in each]
        for g in each:
            coverage = dot(half_cov[g], lt[g][:, :TILE])
            store_tile(step * GROUP + g, 1, weight * coverage)
        x1 = dot(jnp.concatenate(warped, axis=0), cols_ref[...]).astype(BF16)
        x2 = [dot(rows_ref[...], x1[g * ROWS : (g + 1) * ROWS]) for g in each]
        k1 = dot(jnp.concatenate([kern_ref[chosen[g]] for g in each], axis=0), kcols_ref[...])
        k1h = k1.astype(BF16)
        k1l = (k1 - k1h.astype(F32)).astype(BF16)
        z = []
        for g in each:
            h, l = k1h[g * 48 : g * 48 + 48], k1l[g * 48 : g * 48 + 48]
            k2 = dot(krows_ref[...], jnp.concatenate([h, l, h], axis=0))
            x = x2[g]
            xrr, xri, xir, xii = x[:HALF, :128], x[:HALF, 128:], x[HALF:, :128], x[HALF:, 128:]
            krr, kri, kir, kii = k2[:HALF, :128], k2[:HALF, 128:], k2[HALF:, :128], k2[HALF:, 128:]
            xpr, xpi, xmr, xmi = xrr - xii, xir + xri, xrr + xii, xir - xri
            kpr, kpi, kmr, kmi = krr - kii, kir + kri, krr + kii, kir - kri
            ppr, ppi = xpr * kpr - xpi * kpi, xpr * kpi + xpi * kpr
            pmr, pmi = xmr * kmr - xmi * kmi, xmr * kmi + xmi * kmr
            top = jnp.concatenate([ppr + pmr, ppi - pmi], axis=1)
            bottom = jnp.concatenate([ppi + pmi, pmr - ppr], axis=1)
            z.append(jnp.concatenate([top, bottom], axis=0).astype(BF16))
        y = dot(jnp.concatenate(z, axis=0), icols_ref[...])
        y = y[:, :TILE] + y[:, TILE:]
        yh = y.astype(BF16)
        yl = (y - yh.astype(F32)).astype(BF16)
        ycat = jnp.concatenate([yh, yl], axis=1)
        for g in each:
            o = dot(irows_ref[...], ycat[g * ROWS : (g + 1) * ROWS])
            matched = o[:TILE, :TILE] + (o[:TILE, TILE:] + o[TILE:, :TILE])
            store_tile(step * GROUP + g, 0, weight * matched)

        @pl.when(step == 0)
        def _():
            pl.semaphore_wait(barrier, len(around))

        @pl.when(step < CELLS // GROUP)
        def _():
            for half in range(2):
                for way in range(2):
                    early_copy(half, way, step).start()

        @pl.when(step == 0)
        def _():
            for half in range(2):
                for way in range(2):
                    label_copy(half, way).start()

        @pl.when(step == 4)
        def _():
            find_slots()
            pass_on(1)

        @pl.when(step == 6)
        def _():
            pass_on(0)

        return carry

    lax.fori_loop(0, 2 * CELLS // GROUP, work, 0)

    def staying(cell, carry):
        for half in range(2):
            total[half, cell] = gather(half, CELLS + cell) + tiles[half, CELLS + cell].astype(F32)
        return carry

    lax.fori_loop(0, CELLS, staying, 0)

    lane = lax.broadcasted_iota(jnp.int32, (PAD, TILE), 1)

    small = lax.broadcasted_iota(jnp.int32, (PAD // 4, TILE), 1)

    def pack_corners(way):
        for side in range(2):
            packed = jnp.zeros((PAD // 4, TILE), F32)
            for q in range(4):
                row = (TOP if way == 0 else TOP + SPAN - PAD) + q * (PAD // 4)
                end = out_ref[row : row + PAD // 4, :TILE] if side == 0 else out_ref[row : row + PAD // 4, SPAN - TILE : SPAN]
                turn = (PAD * q + PAD * side) % TILE
                moved = end if turn == 0 else pltpu.roll(end, turn, 1)
                packed = jnp.where((small >= PAD * q) & (small < PAD * (q + 1)), moved, packed)
            corner_send[2 * way + side] = packed

    def send_edges(part):
        for way in range(2):
            cols = slice(SPAN - TILE, SPAN) if way == 0 else slice(0, TILE)
            packed = jnp.zeros((PAD, TILE), F32)
            for q in range(4):
                row = TOP + part * TILE + q * PAD
                end = out_ref[row : row + PAD, cols]
                turn = (PAD * q + (PAD if way == 0 else 0)) % TILE
                moved = end if turn == 0 else pltpu.roll(end, turn, 1)
                packed = jnp.where((lane >= PAD * q) & (lane < PAD * (q + 1)), moved, packed)
            edge_send[way, part] = packed.astype(BF16)
            edge_copy(way, part).start()

    for part in range(TR):
        for half in range(2):
            for way in range(2):
                late_copy(half, way, part).wait()
            for place in range(part * TC, (part + 1) * TC):
                row = TOP + PLACES[place] // TC * TILE + half * SLAB
                col = PLACES[place] % TC * TILE
                value = total[half, place] + (recv[half, 0, place].astype(F32) + recv[half, 1, place].astype(F32))
                out_ref[row : row + SLAB, col : col + TILE] = value[0] / (jnp.maximum(value[1], 0.0) + 1.0)
        if part < 2:
            pack_corners(part)
            for copy in rim_copies(part):
                copy.start()
            send_edges(part * (TR - 1))
        if part == 2:
            send_edges(1)
            send_edges(2)

    blank = jnp.zeros((8, WIDE), F32)
    out_ref[0:8, :] = blank
    out_ref[TALL - 8 : TALL, :] = blank

    def unpack(part, carry):
        for way in range(2):
            edge_copy(way, part).wait()
        from_left = edge_recv[0, part].astype(F32) * has_left
        from_right = edge_recv[1, part].astype(F32) * has_right
        for q in range(4):
            turn = (TILE - PAD * q) % TILE
            near = from_right if turn == 0 else pltpu.roll(from_right, turn, 1)
            turn = (TILE - PAD - PAD * q) % TILE
            far = from_left if turn == 0 else pltpu.roll(from_left, turn, 1)
            rows = pl.ds(pl.multiple_of(TOP + part * TILE + q * PAD, 8), PAD)
            out_ref[rows, SPAN:] = jnp.where(lane < PAD, near, jnp.where(lane >= TILE - PAD, far, 0.0))
        return carry

    lax.fori_loop(0, TR, unpack, 0)
    for way in range(2):
        for copy in rim_copies(way):
            copy.wait()
    for way in range(2):
        start = TOP + SPAN if way == 0 else 8
        factor = has_below if way == 0 else has_above
        out_ref[start : start + PAD, :SPAN] = rim_recv[way] * factor
        near_data = corner_recv[2 * way] * (has_right * factor)
        far_data = corner_recv[2 * way + 1] * (has_left * factor)
        for q in range(4):
            turn = (TILE - PAD * q) % TILE
            near = near_data if turn == 0 else pltpu.roll(near_data, turn, 1)
            turn = (TILE - PAD - PAD * q) % TILE
            far = far_data if turn == 0 else pltpu.roll(far_data, turn, 1)
            row = start + q * (PAD // 4)
            out_ref[row : row + PAD // 4, SPAN:] = jnp.where(
                small < PAD, near, jnp.where(small >= TILE - PAD, far, 0.0)
            )


def coaddition_call(dest, offset, anchor, frac, scale, weight, image, mask, psf, consts):
    scalars = (dest, offset, anchor, frac, scale, weight)
    fixed = (jnp.asarray(wanted_labels()),) + tuple(consts)
    dma = pltpu.SemaphoreType.DMA
    slab = (2, SLAB, TILE)
    parts = CELLS // GROUP
    return pl.pallas_call(
        coaddition_kernel,
        in_specs=[pl.BlockSpec(memory_space=pltpu.SMEM)] * len(scalars)
        + [pl.BlockSpec(memory_space=pl.ANY)] * (3 + len(fixed)),
        out_specs=pl.BlockSpec(memory_space=pltpu.VMEM),
        out_shape=pltpu.VMEM((TALL, WIDE), F32),
        scratch_shapes=[pltpu.VMEM(a.shape, a.dtype) for a in fixed]
        + [
            pltpu.VMEM((2, WIN, 128), F32),
            pltpu.VMEM((768, 768), BF16),
            pltpu.VMEM((768, 768), jnp.int32),
            pltpu.VMEM(psf.shape, BF16),
            pltpu.VMEM((48 * 2 * CELLS, 128), F32),
            pltpu.VMEM((2 * CELLS, 48, 128), BF16),
            pltpu.VMEM((CELLS, 128), jnp.int32),
            pltpu.VMEM((8, 128), jnp.int32),
            pltpu.SMEM((8, 128), jnp.int32),
            pltpu.VMEM((2, 2, 6, 48, 16, 128), BF16),
            pltpu.VMEM((2, 2 * CELLS) + slab, BF16),
            pltpu.VMEM((2, CELLS) + slab, BF16),
            pltpu.VMEM((2, CELLS) + slab, BF16),
            pltpu.VMEM((2, 2, CELLS, 128), jnp.int32),
            pltpu.VMEM((8, 128), jnp.int32),
            pltpu.SMEM((8, 128), jnp.int32),
            pltpu.VMEM((2, 2, CELLS) + slab, BF16),
            pltpu.VMEM((2, 2, CELLS) + slab, BF16),
            pltpu.VMEM((2, CELLS) + slab, F32),
            pltpu.VMEM((2, TR, PAD, TILE), BF16),
            pltpu.VMEM((2, TR, PAD, TILE), BF16),
            pltpu.VMEM((2, PAD, SPAN), F32),
            pltpu.VMEM((4, PAD // 4, TILE), F32),
            pltpu.VMEM((4, PAD // 4, TILE), F32),
            dma((2, 2, parts)), dma((2, 2, parts)), dma((2, 2)), dma((2, 2)), dma((2, 2, TR)), dma((2, 2, TR)),
            dma((2, TR)), dma((2, TR)), dma((2, 3)), dma((2, 3)), dma(()), dma((2, LOADS)), dma(()), dma((len(fixed),)),
        ],
        compiler_params=pltpu.CompilerParams(
            vmem_limit_bytes=56 * 2**20, collective_id=0, has_side_effects=True
        ),
    )(*scalars, image, mask, psf, *fixed)


LEVEL_ROWS = ((8, 584), (16, 576), (24, 568), (40, 552))
BLOCK = 256
WAVE = 192


def starlet_kernel(edge_ref, first_ref, details_ref, smooth_ref, ping, pong, band, done, sem):
    top, bottom, left, right = (edge_ref[i] for i in range(4))
    tiles = WIDE // 128
    zero = jnp.zeros((8, WIDE), F32)
    for ref in (ping, pong):
        ref[0:8, :] = zero
        ref[TALL - 8 : TALL, :] = zero
    offset = lax.broadcasted_iota(jnp.int32, (512, 256), 0) - lax.broadcasted_iota(jnp.int32, (512, 256), 1) - 128
    offset = jnp.abs(offset)
    for k in range(SCALES):
        s = 2**k
        tap = jnp.where(offset == 0, 6.0, jnp.where(offset == s, 4.0, jnp.where(offset == 2 * s, 1.0, 0.0)))
        band[k] = (tap * (1.0 / 256.0)).astype(BF16)

    source = first_ref
    copies = []
    for k in range(SCALES):
        s = 2**k
        target = (ping, pong)[k % 2]
        begin, end = LEVEL_ROWS[k]

        def down(view, count, at=16, s=s):
            def near(by):
                return view[at + by : at + by + count, :]

            center = near(0)
            return center, (near(-2 * s) + near(2 * s)) + 4.0 * (near(-s) + near(s)) + 6.0 * center

        def across(rows, s=s):
            count = rows.shape[0]
            parts = [rows[:, 128 * j : 128 * (j + 1)] for j in range(tiles)]
            lane = lax.broadcasted_iota(jnp.int32, (count, 128), 1)

            def after(by):
                turned = [pltpu.roll(part, by, 1) for part in parts]
                return [jnp.where(lane < by, turned[j - 1], turned[j]) for j in range(tiles)]

            def before(by):
                turned = [pltpu.roll(part, 128 - by, 1) for part in parts]
                return [jnp.where(lane >= 128 - by, turned[(j + 1) % tiles], turned[j]) for j in range(tiles)]

            a, b, c, d = after(2 * s), before(2 * s), after(s), before(s)
            return [((a[j] + b[j]) + 4.0 * (c[j] + d[j]) + 6.0 * parts[j]) * (1.0 / 256.0) for j in range(tiles if s < 8 else tiles - 1)]

        def across_product(rows, k=k):
            high = rows.astype(BF16)
            low = (rows - high.astype(F32)).astype(BF16)
            full = []
            for first, count in ((0, 2), (2, 2), (4, 1))[: 3 if k < SCALES - 1 else 2]:
                total = None
                for part in (high, low):
                    pieces = [part[:, 128 * (j % tiles) : 128 * (j % tiles) + 128] for j in range(first - 1, first + count + 1)]
                    weights = band[k] if count == 2 else band[k, :384, :128]
                    term = lax.dot_general(
                        jnp.concatenate(pieces, axis=1), weights, (((1,), (0,)), ((), ())), preferred_element_type=F32
                    )
                    total = term if total is None else total + term
                full += [total[:, 128 * j : 128 * j + 128] for j in range(count)]
            return full

        def store(row, full, factor, target=target):
            count = full[0].shape[0]
            lane = lax.broadcasted_iota(jnp.int32, (count, 128), 1)
            side = jnp.where(lane < 64, right, left)
            for j in range(tiles):
                value = full[j] * side if j == tiles - 1 else full[j]
                value = value if factor is None else value * factor
                target[pl.ds(row, count), 128 * j : 128 * (j + 1)] = value

        if k < SCALES - 1:
            for row, last, factor in ((begin, TOP, top), (TOP + SPAN, end, bottom)):
                low, high = max(row - 16, 0), min(last + 16, TALL)
                count = last - row
                rows = source[low:high, :]
                if low > row - 16:
                    rows = jnp.concatenate([jnp.zeros((low - row + 16, WIDE), F32), rows], axis=0)
                if high < last + 16:
                    rows = jnp.concatenate([rows, jnp.zeros((last + 16 - high, WIDE), F32)], axis=0)
                store(row, across(down(rows, count)[1]), factor)

        def one(block, carry, k=k, source=source, down=down, across=across, store=store, across_product=across_product):
            row = pl.multiple_of(TOP + block * BLOCK, 8)
            here = pl.multiple_of(block * BLOCK, 8)
            view = source.at[pl.ds(pl.multiple_of(row - 16, 8), BLOCK + 32), :]
            spans = [(0, BLOCK - WAVE, across), (BLOCK - WAVE, WAVE, across_product)]
            for start, count, method in spans:
                center, rows = down(view, count, 16 + start)
                full = method(rows)
                if k < SCALES - 1:
                    store(pl.multiple_of(row + start, 8), full, None)
                at = pl.ds(pl.multiple_of(here + start, 8), count)
                for j in range(SPAN // 128):
                    cols = slice(128 * j, 128 * (j + 1))
                    done[k, at, cols] = center[:, cols] - full[j]
                    if k == SCALES - 1:
                        done[SCALES, at, cols] = full[j]
            return carry

        half = SPAN // BLOCK // 2
        for number in range(2):
            lax.fori_loop(number * half, (number + 1) * half, one, 0)
            rows = pl.ds(number * SPAN // 2, SPAN // 2)
            copies.append(pltpu.make_async_copy(done.at[k, rows], details_ref.at[k, rows], sem.at[2 * k + number]))
            if k == SCALES - 1:
                copies.append(pltpu.make_async_copy(done.at[SCALES, rows], smooth_ref.at[rows], sem.at[2 * SCALES + number]))
                copies[-1].start()
                copies[-2].start()
            else:
                copies[-1].start()
        source = target
    for copy in copies:
        copy.wait()


def starlet_call(edges, first):
    return pl.pallas_call(
        starlet_kernel,
        in_specs=[pl.BlockSpec(memory_space=pltpu.SMEM), pl.BlockSpec(memory_space=pltpu.VMEM)],
        out_specs=[pl.BlockSpec(memory_space=pltpu.HBM)] * 2,
        out_shape=[
            jax.ShapeDtypeStruct((SCALES, SPAN, SPAN), F32),
            jax.ShapeDtypeStruct((SPAN, SPAN), F32),
        ],
        scratch_shapes=[
            pltpu.VMEM((TALL, WIDE), F32),
            pltpu.VMEM((TALL, WIDE), F32),
            pltpu.VMEM((SCALES, 512, 256), BF16),
            pltpu.VMEM((SCALES + 1, SPAN, SPAN), F32),
            pltpu.SemaphoreType.DMA((2 * SCALES + 2,)),
        ],
        compiler_params=pltpu.CompilerParams(vmem_limit_bytes=40 * 2**20),
    )(edges, first)


def shards(image, mask, weight, anchor, frac, scale, kernels, dest, offset):
    first = coaddition_call(
        dest, offset, anchor[0].T, frac[0].T, scale[0].T, weight, image, mask, kernels[0].transpose(1, 0, 2), constants()
    )
    band, patch = lax.axis_index("band"), lax.axis_index("patch")
    edges = jnp.stack(
        [band > 0, band < lax.axis_size("band") - 1, patch > 0, patch < lax.axis_size("patch") - 1]
    ).astype(F32)
    return tuple(starlet_call(edges, first))


def solution(mesh):
    owner = ("patch", "band")
    in_specs = (
        P(owner, None, None),
        P(owner, None, None),
        P(owner),
        P(owner, None, None),
        P(owner, None, None),
        P(owner, None, None),
        P(owner, None, None, None),
        P(owner, None),
        P(owner, None),
    )
    out_specs = (P(None, "band", "patch"), P("band", "patch"))
    return jax.shard_map(shards, mesh=mesh, in_specs=in_specs, out_specs=out_specs, check_vma=False)
```

```python
import math
import numpy as np
import ml_dtypes
import jax
import jax.numpy as jnp
from jax import lax
from jax.experimental import pallas as pl
from jax.experimental.pallas import tpu as pltpu
from jax.sharding import PartitionSpec as P

TILE, KS, SCALES, TR, TC, MARGIN, WARP_N, SRC_N = 128, 41, 4, 4, 4, 20, 168, 184
ROWS = 176
HALF = 88
WIN = 256
F32, BF16 = jnp.float32, jnp.bfloat16


def split_bf16(values):
    high = values.astype(ml_dtypes.bfloat16)
    low = (values - high.astype(np.float64)).astype(ml_dtypes.bfloat16)
    return high, low


def spectra():
    bins = np.arange(WARP_N // 2 + 1)

    def forward(points, sign):
        angle = 2.0 * np.pi / WARP_N * np.outer(bins, points)
        return np.cos(angle), sign * np.sin(angle)

    order = (np.arange(WARP_N) + MARGIN) % WARP_N
    real, imag = forward(order, -1.0)
    rows = np.zeros((ROWS, WIN))
    rows[: len(bins), :WARP_N] = real
    rows[HALF : HALF + len(bins), :WARP_N] = imag
    cols = np.zeros((WIN, WIN))
    cols[:WARP_N, : len(bins)] = real.T
    cols[:WARP_N, 128 : 128 + len(bins)] = imag.T
    real, imag = forward(np.arange(KS), 1.0)
    kcols = np.zeros((64, WIN))
    kcols[:KS, : len(bins)] = real.T
    kcols[:KS, 128 : 128 + len(bins)] = imag.T
    krows = np.zeros((ROWS, 48))
    krows[: len(bins), :KS] = real
    krows[HALF : HALF + len(bins), :KS] = imag
    count = np.full(len(bins), 2.0)
    count[0] = count[-1] = 1.0
    angle = 2.0 * np.pi / WARP_N * np.outer(np.arange(TILE), bins)
    back_real = np.cos(angle) * count / WARP_N
    back_imag = -np.sin(angle) * count / WARP_N
    icols = np.zeros((WIN, TILE))
    icols[: len(bins)] = back_real.T
    icols[128 : 128 + len(bins)] = back_imag.T
    irows = np.zeros((TILE, ROWS))
    irows[:, : len(bins)] = 0.5 * back_real
    irows[:, HALF : HALF + len(bins)] = 0.5 * back_imag
    kcols_high, kcols_low = split_bf16(kcols)
    krows_high, krows_low = split_bf16(krows)
    icols_high, icols_low = split_bf16(icols)
    irows_high, irows_low = split_bf16(irows)
    rows_pad = rows[:, :ROWS]
    return (
        cols.astype(ml_dtypes.bfloat16),
        rows_pad.astype(ml_dtypes.bfloat16),
        np.concatenate([kcols_high, kcols_low]),
        np.concatenate([krows_high, krows_high, krows_low], axis=1),
        np.concatenate([icols_high, icols_low], axis=1),
        np.concatenate([irows_high, irows_low]),
    )


def phase_constants():
    j = np.arange(WIN)
    sign = 1.0 - 2.0 * (j % 2)
    cosine = (sign * np.cos(np.pi * j / 5.0)).astype(np.float32)
    sine = (sign * np.sin(np.pi * j / 5.0)).astype(np.float32)
    along = np.zeros((8, WIN), np.float32)
    along[0], along[1] = cosine, sine
    return along


def poly(coefficients, x):
    total = jnp.full_like(x, coefficients[-1])
    for value in coefficients[-2::-1]:
        total = total * x + value
    return total


SIN_PI = (3.14159265, -5.16771276, 2.55016332, -0.5992522, 0.0820504, -0.00702839)
SIN_TURN = (6.28318531, -41.34170222, 81.60524742, -76.70580022, 42.05775402, -15.08656526, 3.78131888, -0.62077872)
COS_TURN = (1.0, -19.73920874, 64.93938908, -85.45665831, 60.24213134, -26.40466819, 7.80013144, -1.45311232)


def lanczos(d, cos_row, sin_row, cos_col, sin_col):
    d2 = d * d
    u = cos_row * sin_col - sin_row * cos_col
    g = u / d2
    g = jnp.where(d2 < 1e-5, 1.0, g)
    return jnp.where(d2 < 25.0, g, 0.0).astype(BF16)


def dot(a, b):
    return lax.dot_general(a, b, (((1,), (0,)), ((), ())), preferred_element_type=F32)


def constants():
    return [jnp.asarray(a) for a in (phase_constants(),) + spectra()]


CELLS = TR * TC
GROUP = 4
LOADS = 2
SLAB = TILE // 2
SPAN = TR * TILE
PAD = 32
WIDE = SPAN + 128
TOP = 8 + PAD
TALL = SPAN + 2 * TOP
MESH = pl.DeviceIdType.MESH


def within(value, top):
    return jnp.minimum(jnp.maximum(value, 0), top)


def whole(a):
    return pl.BlockSpec(a.shape, lambda *_: (0,) * a.ndim)


PLACES = (0, 1, 2, 3, 12, 13, 14, 15, 4, 7, 8, 11, 5, 6, 9, 10)


def wanted_labels():
    lanes = np.arange(128)
    cell = np.asarray(PLACES)[lanes % CELLS]
    rows = np.full((8, 128), -1, np.int32)
    for source, step in enumerate((1, 2, 0)):
        rows[source] = (3 * (lanes // CELLS) + step) * CELLS + cell + 1
        rows[3 + source] = (3 * step + lanes // CELLS) * CELLS + cell + 1
    rows = np.where(lanes < 3 * CELLS, rows, -1).astype(np.int32)
    rows[6] = np.where(lanes < CELLS, lanes, np.where(lanes < 2 * CELLS, 64 + cell, -1))
    return rows


def coaddition_kernel(
    dest_ref, offset_ref, anchor_ref, frac_ref, scale_ref, weight_ref,
    image_hbm, mask_hbm, psf_hbm, wanted_hbm,
    along_hbm, cols_hbm, rows_hbm, kcols_hbm, krows_hbm, icols_hbm, irows_hbm,
    out_ref,
    wanted_ref, along_ref, cols_ref, rows_ref, kcols_ref, krows_ref, icols_ref, irows_ref,
    down_ref, image, mask, psf, taps_wide, kern_ref, label_ref, order, order_smem, planes, tiles, upper_in, lower_in, label_in, table, table_smem, send, recv, total, edge_send, edge_recv, rim_recv, corner_send, corner_recv,
    early_send_sem, early_recv_sem, label_send_sem, label_recv_sem, late_send_sem, late_recv_sem,
    edge_send_sem, edge_recv_sem, rim_send_sem, rim_recv_sem, local_sem, load_sem, psf_sem, constant_sem,
):
    psf_copy = pltpu.make_async_copy(psf_hbm, psf, psf_sem)
    constant_copies = [
        pltpu.make_async_copy(source, target, constant_sem.at[number])
        for number, (source, target) in enumerate(
            (
                (wanted_hbm, wanted_ref),
                (along_hbm, along_ref),
                (cols_hbm, cols_ref),
                (rows_hbm, rows_ref),
                (kcols_hbm, kcols_ref),
                (krows_hbm, krows_ref),
                (icols_hbm, icols_ref),
                (irows_hbm, irows_ref),
            )
        )
    ]
    constant_copies[0].start()
    constant_copies[1].start()
    psf_copy.start()
    loads = []
    for number in range(LOADS):
        rows = pl.ds(number * (768 // LOADS), 768 // LOADS)
        for kind, (source, target) in enumerate(((image_hbm, image), (mask_hbm, mask))):
            loads.append(pltpu.make_async_copy(source.at[0, rows], target.at[rows], load_sem.at[kind, number]))
    for load in loads:
        load.start()
    for copy in constant_copies[2:]:
        copy.start()

    patch, band = lax.axis_index("patch"), lax.axis_index("band")
    n_patch, n_band = lax.axis_size("patch"), lax.axis_size("band")
    left_patch, right_patch = lax.rem(patch + n_patch - 1, n_patch), lax.rem(patch + 1, n_patch)
    above_band, below_band = lax.rem(band + n_band - 1, n_band), lax.rem(band + 1, n_band)
    left, right = {"patch": left_patch, "band": band}, {"patch": right_patch, "band": band}
    above, below = {"patch": patch, "band": above_band}, {"patch": patch, "band": below_band}
    corners = [{"patch": p, "band": b} for b in (above_band, below_band) for p in (left_patch, right_patch)]
    has_left = jnp.where(patch > 0, 1.0, 0.0)
    has_right = jnp.where(patch < n_patch - 1, 1.0, 0.0)
    has_above = jnp.where(band > 0, 1.0, 0.0)
    has_below = jnp.where(band < n_band - 1, 1.0, 0.0)

    barrier = pltpu.get_barrier_semaphore()
    around = [left, right, above, below] + corners
    for device in around:
        pl.semaphore_signal(barrier, inc=1, device_id=device, device_id_type=MESH)

    def remote(src, dst, send_sem, recv_sem, device):
        return pltpu.make_async_remote_copy(
            src_ref=src, dst_ref=dst, send_sem=send_sem, recv_sem=recv_sem, device_id=device, device_id_type=MESH
        )

    beside = (upper_in, lower_in)

    early_to = ((right, left), (below, above))
    late_to = ((above, below), (left, right))

    def label_copy(half, way):
        return remote(
            label_ref,
            label_in.at[half, way],
            label_send_sem.at[half, way],
            label_recv_sem.at[half, way],
            early_to[half][way],
        )

    def early_copy(half, way, part):
        piece = pl.ds(part * GROUP, GROUP)
        return remote(
            tiles.at[half, piece],
            beside[half].at[way, piece],
            early_send_sem.at[half, way, part],
            early_recv_sem.at[half, way, part],
            early_to[half][way],
        )

    def late_copy(half, way, part):
        piece = pl.ds(part * TC, TC)
        return remote(
            send.at[half, way, piece],
            recv.at[half, way, piece],
            late_send_sem.at[half, way, part],
            late_recv_sem.at[half, way, part],
            late_to[half][way],
        )

    first_rows, last_rows = pl.ds(TOP, PAD), pl.ds(TOP + SPAN - PAD, PAD)

    def edge_copy(way, part):
        return remote(
            edge_send.at[way, part],
            edge_recv.at[way, part],
            edge_send_sem.at[way, part],
            edge_recv_sem.at[way, part],
            early_to[0][way],
        )

    def rim_copies(way):
        rows = (first_rows, last_rows)[way]
        triples = [(out_ref.at[rows, pl.ds(0, SPAN)], rim_recv.at[way], late_to[0][way])]
        for number in (2 * way, 2 * way + 1):
            triples.append((corner_send.at[number], corner_recv.at[number], corners[number]))
        return [
            remote(source, target, rim_send_sem.at[way, number], rim_recv_sem.at[way, number], device)
            for number, (source, target, device) in enumerate(triples)
        ]

    for copy in constant_copies[:2]:
        copy.wait()
    columns = jnp.transpose(along_ref[...])
    for number in range(2):
        down_ref[number] = jnp.broadcast_to(columns[:, number : number + 1], (WIN, 128))
    filled = jnp.int32(0)
    key_of = wanted_ref[6:7, :]
    sub = lax.broadcasted_iota(jnp.int32, (CELLS, 128), 0)
    sequence = jnp.zeros((1, 128), jnp.int32)
    labels = jnp.zeros((CELLS, 128), jnp.int32)
    for i in range(2 * CELLS):
        code, cell = dest_ref[0, i], offset_ref[0, i]
        away = code != 4
        key = jnp.where(away, filled, 64 + cell)
        sequence = jnp.where(key_of == key, i, sequence)
        labels = jnp.where(sub == key, code * CELLS + cell + 1, labels)
        filled = filled + away.astype(jnp.int32)
    order[...] = jnp.broadcast_to(sequence, (8, 128))
    label_ref[...] = labels
    order_copy = pltpu.make_async_copy(order, order_smem, local_sem)
    order_copy.start()

    psf_copy.wait()
    gap = jnp.zeros((2 * CELLS, 64 - KS), F32)
    for r in range(KS):
        tap = psf[r].astype(F32)
        taps_wide[2 * CELLS * r : 2 * CELLS * (r + 1), :] = jnp.concatenate([tap, gap, tap, gap], axis=1)
    taps_wide[2 * CELLS * KS :, :] = jnp.zeros((2 * CELLS * (48 - KS), 128), F32)
    for t in range(2 * CELLS):
        kern_ref[t] = taps_wide[pl.ds(t, 48, stride=2 * CELLS), :].astype(BF16)

    def prepare(block, carry):
        rows = pl.ds(pl.multiple_of(block * 64, 64), 64)
        usable = jnp.where((mask[rows, :] & 7) != 7, 1.0, 0.0).astype(BF16)
        masked = image[rows, :] * usable
        for plane, value in enumerate((masked, usable)):
            moved = jnp.concatenate([value[:, 64:], value[:, :64]], axis=1)
            for way, data in enumerate((value, moved)):
                for j in range(6):
                    for i in range(4):
                        planes[way, plane, j, block * 4 + i] = data[16 * i : 16 * i + 16, 128 * j : 128 * j + 128]
        return carry

    steps = 768 // 64 // LOADS
    for number in range(LOADS):
        for load in loads[2 * number : 2 * number + 2]:
            load.wait()
        lax.fori_loop(number * steps, (number + 1) * steps, prepare, 0)
    order_copy.wait()
    for copy in constant_copies[2:]:
        copy.wait()

    lane = lax.broadcasted_iota(jnp.int32, (ROWS, WIN), 1)
    sub = lax.broadcasted_iota(jnp.int32, (WIN, WIN), 0)
    short = lax.broadcasted_iota(jnp.int32, (8, WIN), 1)
    quantity = lax.broadcasted_iota(jnp.int32, (8, WIN), 0)
    index = (short + jnp.where(short < WARP_N - MARGIN, MARGIN, MARGIN - WARP_N)).astype(F32)

    def warp_rows(fraction, stretch, shift):
        position = (5.0 + fraction) + index * (1.0 + stretch)
        nearest = jnp.floor(position + 0.5)
        odd = nearest - 2.0 * jnp.floor(nearest * 0.5)
        part = position - nearest
        sine = (1.0 - 2.0 * odd) * part * poly(SIN_PI, part * part)
        sign = (1 - 2 * (shift & 1)).astype(F32)
        amplitude = ((-5.0 / math.pi**2) * sign) * sine
        turn = position - 10.0 * jnp.floor(position * 0.1) + lax.rem(shift, 10).astype(F32)
        turn = turn * 0.1
        turn = turn - jnp.floor(turn + 0.5)
        square = turn * turn
        cosine, sine = poly(COS_TURN, square), turn * poly(SIN_TURN, square)
        position = jnp.where(short < WARP_N, position, 1e4)
        return jnp.where(quantity == 0, position, jnp.where(quantity == 1, amplitude * cosine, amplitude * sine))

    weight = weight_ref[0]
    each = range(GROUP)

    def store_tile(slot, plane, value):
        for half in range(2):
            tiles[half, slot, plane] = value[half * SLAB : (half + 1) * SLAB].astype(BF16)

    def gather(half, position):
        value = None
        for source in range(3):
            slot = table_smem[3 * half + source, position]
            present = jnp.where(slot >= 0, 1.0, 0.0)
            at = within(slot, CELLS - 1)
            data = tiles[half, at] if source == 0 else beside[half][source - 1, at]
            term = data.astype(F32) * present
            value = term if value is None else value + term
        return value

    def find_slots():
        for half in range(2):
            for way in range(2):
                label_copy(half, way).wait()
            for source in range(3):
                lookup = label_ref[...] if source == 0 else label_in[half, source - 1]
                number = 3 * half + source
                found = jnp.zeros((1, 128), jnp.int32)
                for slot in range(CELLS):
                    same = lookup[slot : slot + 1] == wanted_ref[number : number + 1, :]
                    found = found + jnp.where(same, slot + 1, 0)
                table[number : number + 1, :] = found - 1
        to_smem = pltpu.make_async_copy(table, table_smem, local_sem)
        to_smem.start()
        to_smem.wait()

    def pass_on(half):
        for part in range(CELLS // GROUP):
            for way in range(2):
                early_copy(half, way, part).wait()

        def outgoing(part, carry):
            for way in range(2):
                for c in range(TC):
                    cell = part * TC + c
                    send[half, way, cell] = gather(half, 2 * CELLS * way + cell).astype(BF16)
                late_copy(half, way, part).start()
            return carry

        lax.fori_loop(0, TR, outgoing, 0)

    def work(step, carry):
        chosen = [within(order_smem[0, step * GROUP + g], 2 * CELLS - 1) for g in each]
        half_img, half_cov, lt = [], [], []
        for g in each:
            t = chosen[g]
            first_row, first_col = anchor_ref[0, t], anchor_ref[1, t]
            row16 = within(first_row // 16, (768 - WIN) // 16)
            col64 = within(first_col // 64, (768 - WIN) // 64)
            off_r = first_row - row16 * 16
            off_c = first_col - col64 * 64
            par = within(col64 % 2, 1)
            pair = within(col64 // 2, 4)
            s_img, s_cov = (
                jnp.concatenate(
                    [
                        jnp.concatenate([planes[par, plane, pair + j, row16 + i] for i in range(16)], axis=0)
                        for j in range(2)
                    ],
                    axis=1,
                )
                for plane in range(2)
            )
            q0 = jnp.transpose(warp_rows(frac_ref[0, t], scale_ref[0, t], off_r))[:ROWS]
            d0 = (lane - off_r).astype(F32) - q0[:, 0:1]
            l0 = lanczos(d0, q0[:, 1:2], q0[:, 2:3], along_ref[0:1, :], along_ref[1:2, :])
            q1 = warp_rows(frac_ref[1, t], scale_ref[1, t], off_c)
            d1 = (sub - off_c).astype(F32) - q1[0:1, :]
            cosd = jnp.concatenate([down_ref[0], down_ref[0]], axis=1)
            sind = jnp.concatenate([down_ref[1], down_ref[1]], axis=1)
            lt.append(lanczos(d1, q1[1:2, :], q1[2:3, :], cosd, sind))
            half_img.append(dot(l0, s_img).astype(BF16))
            half_cov.append(dot(l0[:TILE], s_cov).astype(BF16))
        warped = [dot(half_img[g], lt[g]).astype(BF16) for g in each]
        for g in each:
            coverage = dot(half_cov[g], lt[g][:, :TILE])
            store_tile(step * GROUP + g, 1, weight * coverage)
        x1 = dot(jnp.concatenate(warped, axis=0), cols_ref[...]).astype(BF16)
        x2 = [dot(rows_ref[...], x1[g * ROWS : (g + 1) * ROWS]) for g in each]
        k1 = dot(jnp.concatenate([kern_ref[chosen[g]] for g in each], axis=0), kcols_ref[...])
        k1h = k1.astype(BF16)
        k1l = (k1 - k1h.astype(F32)).astype(BF16)
        z = []
        for g in each:
            h, l = k1h[g * 48 : g * 48 + 48], k1l[g * 48 : g * 48 + 48]
            k2 = dot(krows_ref[...], jnp.concatenate([h, l, h], axis=0))
            x = x2[g]
            xrr, xri, xir, xii = x[:HALF, :128], x[:HALF, 128:], x[HALF:, :128], x[HALF:, 128:]
            krr, kri, kir, kii = k2[:HALF, :128], k2[:HALF, 128:], k2[HALF:, :128], k2[HALF:, 128:]
            xpr, xpi, xmr, xmi = xrr - xii, xir + xri, xrr + xii, xir - xri
            kpr, kpi, kmr, kmi = krr - kii, kir + kri, krr + kii, kir - kri
            ppr, ppi = xpr * kpr - xpi * kpi, xpr * kpi + xpi * kpr
            pmr, pmi = xmr * kmr - xmi * kmi, xmr * kmi + xmi * kmr
            top = jnp.concatenate([ppr + pmr, ppi - pmi], axis=1)
            bottom = jnp.concatenate([ppi + pmi, pmr - ppr], axis=1)
            z.append(jnp.concatenate([top, bottom], axis=0).astype(BF16))
        y = dot(jnp.concatenate(z, axis=0), icols_ref[...])
        y = y[:, :TILE] + y[:, TILE:]
        yh = y.astype(BF16)
        yl = (y - yh.astype(F32)).astype(BF16)
        ycat = jnp.concatenate([yh, yl], axis=1)
        for g in each:
            o = dot(irows_ref[...], ycat[g * ROWS : (g + 1) * ROWS])
            matched = o[:TILE, :TILE] + (o[:TILE, TILE:] + o[TILE:, :TILE])
            store_tile(step * GROUP + g, 0, weight * matched)

        @pl.when(step == 0)
        def _():
            pl.semaphore_wait(barrier, len(around))

        @pl.when(step < CELLS // GROUP)
        def _():
            for half in range(2):
                for way in range(2):
                    early_copy(half, way, step).start()

        @pl.when(step == 0)
        def _():
            for half in range(2):
                for way in range(2):
                    label_copy(half, way).start()

        @pl.when(step == 4)
        def _():
            find_slots()
            pass_on(1)

        @pl.when(step == 6)
        def _():
            pass_on(0)

        return carry

    lax.fori_loop(0, 2 * CELLS // GROUP, work, 0)

    def staying(cell, carry):
        for half in range(2):
            total[half, cell] = gather(half, CELLS + cell) + tiles[half, CELLS + cell].astype(F32)
        return carry

    lax.fori_loop(0, CELLS, staying, 0)

    lane = lax.broadcasted_iota(jnp.int32, (PAD, TILE), 1)

    small = lax.broadcasted_iota(jnp.int32, (PAD // 4, TILE), 1)

    def pack_corners(way):
        for side in range(2):
            packed = jnp.zeros((PAD // 4, TILE), F32)
            for q in range(4):
                row = (TOP if way == 0 else TOP + SPAN - PAD) + q * (PAD // 4)
                end = out_ref[row : row + PAD // 4, :TILE] if side == 0 else out_ref[row : row + PAD // 4, SPAN - TILE : SPAN]
                turn = (PAD * q + PAD * side) % TILE
                moved = end if turn == 0 else pltpu.roll(end, turn, 1)
                packed = jnp.where((small >= PAD * q) & (small < PAD * (q + 1)), moved, packed)
            corner_send[2 * way + side] = packed

    def send_edges(part):
        for way in range(2):
            cols = slice(SPAN - TILE, SPAN) if way == 0 else slice(0, TILE)
            packed = jnp.zeros((PAD, TILE), F32)
            for q in range(4):
                row = TOP + part * TILE + q * PAD
                end = out_ref[row : row + PAD, cols]
                turn = (PAD * q + (PAD if way == 0 else 0)) % TILE
                moved = end if turn == 0 else pltpu.roll(end, turn, 1)
                packed = jnp.where((lane >= PAD * q) & (lane < PAD * (q + 1)), moved, packed)
            edge_send[way, part] = packed.astype(BF16)
            edge_copy(way, part).start()

    for part in range(TR):
        for half in range(2):
            for way in range(2):
                late_copy(half, way, part).wait()
            for place in range(part * TC, (part + 1) * TC):
                row = TOP + PLACES[place] // TC * TILE + half * SLAB
                col = PLACES[place] % TC * TILE
                value = total[half, place] + (recv[half, 0, place].astype(F32) + recv[half, 1, place].astype(F32))
                out_ref[row : row + SLAB, col : col + TILE] = value[0] / (jnp.maximum(value[1], 0.0) + 1.0)
        if part < 2:
            pack_corners(part)
            for copy in rim_copies(part):
                copy.start()
            send_edges(part * (TR - 1))
        if part == 2:
            send_edges(1)
            send_edges(2)

    blank = jnp.zeros((8, WIDE), F32)
    out_ref[0:8, :] = blank
    out_ref[TALL - 8 : TALL, :] = blank

    def unpack(part, carry):
        for way in range(2):
            edge_copy(way, part).wait()
        from_left = edge_recv[0, part].astype(F32) * has_left
        from_right = edge_recv[1, part].astype(F32) * has_right
        for q in range(4):
            turn = (TILE - PAD * q) % TILE
            near = from_right if turn == 0 else pltpu.roll(from_right, turn, 1)
            turn = (TILE - PAD - PAD * q) % TILE
            far = from_left if turn == 0 else pltpu.roll(from_left, turn, 1)
            rows = pl.ds(pl.multiple_of(TOP + part * TILE + q * PAD, 8), PAD)
            out_ref[rows, SPAN:] = jnp.where(lane < PAD, near, jnp.where(lane >= TILE - PAD, far, 0.0))
        return carry

    lax.fori_loop(0, TR, unpack, 0)
    for way in range(2):
        for copy in rim_copies(way):
            copy.wait()
    for way in range(2):
        start = TOP + SPAN if way == 0 else 8
        factor = has_below if way == 0 else has_above
        out_ref[start : start + PAD, :SPAN] = rim_recv[way] * factor
        near_data = corner_recv[2 * way] * (has_right * factor)
        far_data = corner_recv[2 * way + 1] * (has_left * factor)
        for q in range(4):
            turn = (TILE - PAD * q) % TILE
            near = near_data if turn == 0 else pltpu.roll(near_data, turn, 1)
            turn = (TILE - PAD - PAD * q) % TILE
            far = far_data if turn == 0 else pltpu.roll(far_data, turn, 1)
            row = start + q * (PAD // 4)
            out_ref[row : row + PAD // 4, SPAN:] = jnp.where(
                small < PAD, near, jnp.where(small >= TILE - PAD, far, 0.0)
            )


def coaddition_call(dest, offset, anchor, frac, scale, weight, image, mask, psf, consts):
    scalars = (dest, offset, anchor, frac, scale, weight)
    fixed = (jnp.asarray(wanted_labels()),) + tuple(consts)
    dma = pltpu.SemaphoreType.DMA
    slab = (2, SLAB, TILE)
    parts = CELLS // GROUP
    return pl.pallas_call(
        coaddition_kernel,
        in_specs=[pl.BlockSpec(memory_space=pltpu.SMEM)] * len(scalars)
        + [pl.BlockSpec(memory_space=pl.ANY)] * (3 + len(fixed)),
        out_specs=pl.BlockSpec(memory_space=pltpu.VMEM),
        out_shape=pltpu.VMEM((TALL, WIDE), F32),
        scratch_shapes=[pltpu.VMEM(a.shape, a.dtype) for a in fixed]
        + [
            pltpu.VMEM((2, WIN, 128), F32),
            pltpu.VMEM((768, 768), BF16),
            pltpu.VMEM((768, 768), jnp.int32),
            pltpu.VMEM(psf.shape, BF16),
            pltpu.VMEM((48 * 2 * CELLS, 128), F32),
            pltpu.VMEM((2 * CELLS, 48, 128), BF16),
            pltpu.VMEM((CELLS, 128), jnp.int32),
            pltpu.VMEM((8, 128), jnp.int32),
            pltpu.SMEM((8, 128), jnp.int32),
            pltpu.VMEM((2, 2, 6, 48, 16, 128), BF16),
            pltpu.VMEM((2, 2 * CELLS) + slab, BF16),
            pltpu.VMEM((2, CELLS) + slab, BF16),
            pltpu.VMEM((2, CELLS) + slab, BF16),
            pltpu.VMEM((2, 2, CELLS, 128), jnp.int32),
            pltpu.VMEM((8, 128), jnp.int32),
            pltpu.SMEM((8, 128), jnp.int32),
            pltpu.VMEM((2, 2, CELLS) + slab, BF16),
            pltpu.VMEM((2, 2, CELLS) + slab, BF16),
            pltpu.VMEM((2, CELLS) + slab, F32),
            pltpu.VMEM((2, TR, PAD, TILE), BF16),
            pltpu.VMEM((2, TR, PAD, TILE), BF16),
            pltpu.VMEM((2, PAD, SPAN), F32),
            pltpu.VMEM((4, PAD // 4, TILE), F32),
            pltpu.VMEM((4, PAD // 4, TILE), F32),
            dma((2, 2, parts)), dma((2, 2, parts)), dma((2, 2)), dma((2, 2)), dma((2, 2, TR)), dma((2, 2, TR)),
            dma((2, TR)), dma((2, TR)), dma((2, 3)), dma((2, 3)), dma(()), dma((2, LOADS)), dma(()), dma((len(fixed),)),
        ],
        compiler_params=pltpu.CompilerParams(
            vmem_limit_bytes=56 * 2**20, collective_id=0, has_side_effects=True
        ),
    )(*scalars, image, mask, psf, *fixed)


LEVEL_ROWS = ((8, 584), (16, 576), (24, 568), (40, 552))
BLOCK = 256
WAVE = 192


def starlet_kernel(edge_ref, first_ref, details_ref, smooth_ref, ping, pong, band, done, sem):
    top, bottom, left, right = (edge_ref[i] for i in range(4))
    tiles = WIDE // 128
    zero = jnp.zeros((8, WIDE), F32)
    for ref in (ping, pong):
        ref[0:8, :] = zero
        ref[TALL - 8 : TALL, :] = zero
    offset = lax.broadcasted_iota(jnp.int32, (512, 256), 0) - lax.broadcasted_iota(jnp.int32, (512, 256), 1) - 128
    offset = jnp.abs(offset)
    for k in range(SCALES):
        s = 2**k
        tap = jnp.where(offset == 0, 6.0, jnp.where(offset == s, 4.0, jnp.where(offset == 2 * s, 1.0, 0.0)))
        band[k] = (tap * (1.0 / 256.0)).astype(BF16)

    source = first_ref
    copies = []
    for k in range(SCALES):
        s = 2**k
        target = (ping, pong)[k % 2]
        begin, end = LEVEL_ROWS[k]

        def down(view, count, at=16, s=s):
            def near(by):
                return view[at + by : at + by + count, :]

            center = near(0)
            return center, (near(-2 * s) + near(2 * s)) + 4.0 * (near(-s) + near(s)) + 6.0 * center

        def across(rows, s=s):
            count = rows.shape[0]
            parts = [rows[:, 128 * j : 128 * (j + 1)] for j in range(tiles)]
            lane = lax.broadcasted_iota(jnp.int32, (count, 128), 1)

            def after(by):
                turned = [pltpu.roll(part, by, 1) for part in parts]
                return [jnp.where(lane < by, turned[j - 1], turned[j]) for j in range(tiles)]

            def before(by):
                turned = [pltpu.roll(part, 128 - by, 1) for part in parts]
                return [jnp.where(lane >= 128 - by, turned[(j + 1) % tiles], turned[j]) for j in range(tiles)]

            a, b, c, d = after(2 * s), before(2 * s), after(s), before(s)
            return [((a[j] + b[j]) + 4.0 * (c[j] + d[j]) + 6.0 * parts[j]) * (1.0 / 256.0) for j in range(tiles if s < 8 else tiles - 1)]

        def across_product(rows, k=k):
            high = rows.astype(BF16)
            low = (rows - high.astype(F32)).astype(BF16)
            full = []
            for first, count in ((0, 2), (2, 2), (4, 1))[: 3 if k < SCALES - 1 else 2]:
                total = None
                for part in (high, low):
                    pieces = [part[:, 128 * (j % tiles) : 128 * (j % tiles) + 128] for j in range(first - 1, first + count + 1)]
                    weights = band[k] if count == 2 else band[k, :384, :128]
                    term = lax.dot_general(
                        jnp.concatenate(pieces, axis=1), weights, (((1,), (0,)), ((), ())), preferred_element_type=F32
                    )
                    total = term if total is None else total + term
                full += [total[:, 128 * j : 128 * j + 128] for j in range(count)]
            return full

        def store(row, full, factor, target=target):
            count = full[0].shape[0]
            lane = lax.broadcasted_iota(jnp.int32, (count, 128), 1)
            side = jnp.where(lane < 64, right, left)
            for j in range(tiles):
                value = full[j] * side if j == tiles - 1 else full[j]
                value = value if factor is None else value * factor
                target[pl.ds(row, count), 128 * j : 128 * (j + 1)] = value

        if k < SCALES - 1:
            for row, last, factor in ((begin, TOP, top), (TOP + SPAN, end, bottom)):
                low, high = max(row - 16, 0), min(last + 16, TALL)
                count = last - row
                rows = source[low:high, :]
                if low > row - 16:
                    rows = jnp.concatenate([jnp.zeros((low - row + 16, WIDE), F32), rows], axis=0)
                if high < last + 16:
                    rows = jnp.concatenate([rows, jnp.zeros((last + 16 - high, WIDE), F32)], axis=0)
                store(row, across(down(rows, count)[1]), factor)

        def one(block, carry, k=k, source=source, down=down, across=across, store=store, across_product=across_product):
            row = pl.multiple_of(TOP + block * BLOCK, 8)
            here = pl.multiple_of(block * BLOCK, 8)
            view = source.at[pl.ds(pl.multiple_of(row - 16, 8), BLOCK + 32), :]
            spans = [(0, BLOCK - WAVE, across), (BLOCK - WAVE, WAVE, across_product)]
            for start, count, method in spans:
                center, rows = down(view, count, 16 + start)
                full = method(rows)
                if k < SCALES - 1:
                    store(pl.multiple_of(row + start, 8), full, None)
                at = pl.ds(pl.multiple_of(here + start, 8), count)
                for j in range(SPAN // 128):
                    cols = slice(128 * j, 128 * (j + 1))
                    done[k, at, cols] = center[:, cols] - full[j]
                    if k == SCALES - 1:
                        done[SCALES, at, cols] = full[j]
            return carry

        half = SPAN // BLOCK // 2
        for number in range(2):
            lax.fori_loop(number * half, (number + 1) * half, one, 0)
            rows = pl.ds(number * SPAN // 2, SPAN // 2)
            copies.append(pltpu.make_async_copy(done.at[k, rows], details_ref.at[k, rows], sem.at[2 * k + number]))
            if k == SCALES - 1:
                copies.append(pltpu.make_async_copy(done.at[SCALES, rows], smooth_ref.at[rows], sem.at[2 * SCALES + number]))
                copies[-1].start()
                copies[-2].start()
            else:
                copies[-1].start()
        source = target
    for copy in copies:
        copy.wait()


def starlet_call(edges, first):
    return pl.pallas_call(
        starlet_kernel,
        in_specs=[pl.BlockSpec(memory_space=pltpu.SMEM), pl.BlockSpec(memory_space=pltpu.VMEM)],
        out_specs=[pl.BlockSpec(memory_space=pltpu.HBM)] * 2,
        out_shape=[
            jax.ShapeDtypeStruct((SCALES, SPAN, SPAN), F32),
            jax.ShapeDtypeStruct((SPAN, SPAN), F32),
        ],
        scratch_shapes=[
            pltpu.VMEM((TALL, WIDE), F32),
            pltpu.VMEM((TALL, WIDE), F32),
            pltpu.VMEM((SCALES, 512, 256), BF16),
            pltpu.VMEM((SCALES + 1, SPAN, SPAN), F32),
            pltpu.SemaphoreType.DMA((2 * SCALES + 2,)),
        ],
        compiler_params=pltpu.CompilerParams(vmem_limit_bytes=40 * 2**20),
    )(edges, first)


def shards(image, mask, weight, anchor, frac, scale, kernels, dest, offset):
    first = coaddition_call(
        dest, offset, anchor[0].T, frac[0].T, scale[0].T, weight, image, mask, kernels[0].transpose(1, 0, 2), constants()
    )
    band, patch = lax.axis_index("band"), lax.axis_index("patch")
    edges = jnp.stack(
        [band > 0, band < lax.axis_size("band") - 1, patch > 0, patch < lax.axis_size("patch") - 1]
    ).astype(F32)
    return tuple(starlet_call(edges, first))


def solution(mesh):
    owner = ("patch", "band")
    in_specs = (
        P(owner, None, None),
        P(owner, None, None),
        P(owner),
        P(owner, None, None),
        P(owner, None, None),
        P(owner, None, None),
        P(owner, None, None, None),
        P(owner, None),
        P(owner, None),
    )
    out_specs = (P(None, "band", "patch"), P("band", "patch"))
    return jax.shard_map(shards, mesh=mesh, in_specs=in_specs, out_specs=out_specs, check_vma=False)
```
